32 devices in a mesh: req: 4 (over x, core), pg: 8 (over z, y).
Axes of the slice: x: 2, y: 2, z: 4, core: 2. Of those that a mesh axis runs over, the one named last changes fastest.
Arguments:
- tokens: bfloat16 [2048, 1024], P(('req', 'pg')), may hold values from -15 to 15
- variate_ids: int32 [2048], P('req'), may hold values from 0 to 3
- cache_pages: int32 [8], P('req'), may hold values from 1 to 24, 96 in all
- page_table: int32 [8, 24], P('req'), may hold values from 0 to 47, as said below
- kv_cache: bfloat16 [192, 128, 2048], P(('req', 'pg')), may hold values from -104 to 104
- cache_variates: int32 [192, 128], P(('req', 'pg')), may hold values from 0 to 3
- attn_gain: float32 [1024], replicated, may hold values from 0.25 to 1.75
- w_query: bfloat16 [1024, 1024], P('req', 'pg'), may hold values from -0.1875 to 0.1875
- w_keyval: bfloat16 [1024, 2048], P('req', 'pg'), may hold values from -0.1875 to 0.1875
- w_out: bfloat16 [1024, 1024], P('req', 'pg'), may hold values from -0.1875 to 0.1875
- variate_bias: float32 [2, 16], replicated, may hold values from -3 to 3
- head_gain: float32 [1024], replicated, may hold values from 0.25 to 1.75
- w_head: bfloat16 [1024, 256], P('req', 'pg'), may hold values from -0.1875 to 0.1875
Outputs:
- hidden_out: bfloat16 [2048, 1024], P(('req', 'pg'))
- appended_kv: bfloat16 [2048, 2048], P(('req', 'pg'))
- mix_logits: bfloat16 [2048, 256], P(('req', 'pg'))
- request_norm: float32 [8], P('req')
- request_peak: float32 [8], P('req')
The draws below stay inside these ranges and needn't reach their ends.
Inputs may be any that keep to these rules, and one draw needn't show every extreme that they name: Row r of page_table lists 24 entries; entry e places logical page n of request r in slot e mod 6 of the device with pg index e // 6 among the devices of r's req index. The rows of the 2 requests of one req index together hold every value once.
All inputs are finite; a program needn't handle non-finite values. No bound on the sum of `cache_pages` on one device may be relied on, other than what follows from the above.
Results may differ from the reference program's by a relative error of at most 0.017.
Values may be sent and summed in bfloat16 or wider, within the bound.
A program may use at most 128 MiB of HBM per device.

```python
import math
import jax
import jax.numpy as jnp
import numpy as np
from jax import lax

D = 1024
H = 16
DH = 64
MIXW = 256
NVAR = 4
PAGE = 128
REQ_DEV = 2
TOK_DEV = 64
SLOTS = 6
REQUESTS = 8
FRESH = 256
MAXPAGES = 24
TOKENS = 2048
CACHE_SLOTS = 192
N_PG = 8


def draw_tokens(key, part):
    row_index = jnp.arange(TOKENS, dtype=jnp.int32) % FRESH
    ramp_rows = row_index.astype(jnp.float32) / FRESH
    base_draw = jnp.clip(jax.random.normal(key, (TOKENS, D), jnp.float32), -5.0, 5.0)
    row_scale = jnp.exp(jnp.log(3.0) * ramp_rows)
    return (base_draw * row_scale[:, None]).astype(jnp.bfloat16)


def draw_page_table(key, part):
    group_count = REQUESTS // REQ_DEV
    group_keys = jax.random.split(key, group_count)
    orders = jax.vmap(lambda group_key: jax.random.permutation(group_key, REQ_DEV * MAXPAGES))(group_keys)
    return orders.reshape(REQUESTS, MAXPAGES).astype(jnp.int32)


def draw_kv_cache(key, part):
    full_shape = (CACHE_SLOTS, PAGE, 2 * D)
    return jnp.clip(jax.random.normal(key, full_shape, jnp.float32), -6.0, 6.0).astype(jnp.bfloat16)


def touch_ends(drawn, key, low, largest):
    spot = [jax.random.randint(jax.random.fold_in(key, axis), (), 0, length) for axis, length in enumerate(drawn.shape)]
    widest = drawn.shape.index(max(drawn.shape))
    neighbour = spot[:widest] + [(spot[widest] + 1) % drawn.shape[widest]] + spot[widest + 1:]
    return drawn.at[tuple(spot)].set(low).at[tuple(neighbour)].set(largest)


def shard_levels(key, extent, shards, least, largest):
    level = 1.0
    for position, parts in shards:
        draws = jax.random.uniform(jax.random.fold_in(jax.random.fold_in(key, 6), position), (parts,), jnp.float32, least / len(shards), largest / len(shards))
        level = level * jnp.repeat(jnp.exp(draws), extent[position] // parts).reshape((-1,) + (1,) * (len(extent) - 1 - position))
    return level


def profile(number_of, total, bound, skew):
    portions = [(1 << 20) // math.isqrt(standing ** skew) + 1 for standing in range(2, number_of + 1)]
    surplus, given = total - bound - (number_of - 1), [1] * (number_of - 1)
    while surplus > 0:
        movable = [i for i in range(number_of - 1) if given[i] < bound]
        mass, left = sum([portions[i] for i in movable]), surplus
        for i in movable:
            extra = min(bound - given[i], max(1, left * portions[i] // mass), surplus)
            given[i] = given[i] + extra
            surplus = surplus - extra
    return np.array([bound] + given)


def ragged_sizes(key, count, total, limit, lean):
    if count == 2:
        one = jax.random.randint(key, (), max(1, total - limit), min(limit, total - 1) + 1)
        return jnp.stack([one, total - one])
    tallies = jnp.asarray(profile(count, total, limit, lean), jnp.int32)
    twos = (count - 1) // 2
    giver, sink = tallies[1:1 + 2 * twos:2], tallies[2:2 + 2 * twos:2]
    margin = jnp.minimum(giver - 1, limit - sink)
    moved = jax.random.randint(jax.random.fold_in(key, 1), (twos,), 0, 1 << 20) % (margin + 1)
    tallies = tallies.at[1:1 + 2 * twos:2].set(giver - moved).at[2:2 + 2 * twos:2].set(sink + moved)
    return tallies[jax.random.permutation(jax.random.fold_in(key, 2), count)]


def scatter_about(key, extent, scale, limit, shards=(), kind=jnp.bfloat16):
    values = jax.random.normal(key, extent, jnp.float32) * scale
    if len(shards) > 0:
        values = shard_levels(key, extent, shards, -0.22, 0.18) * values
    return jnp.clip(values, min=-limit, max=limit).astype(kind)


def setup_inputs(seed: int = 0) -> dict:
    key_list = jax.random.split(jax.random.key(seed), 14)
    return {
        "tokens": draw_tokens(jax.random.fold_in(key_list[13], 71), 0),
        "variate_ids": touch_ends(jax.random.randint(key_list[1], (TOKENS,), 0, NVAR), jax.random.fold_in(key_list[1], 1), 0, NVAR - 1).astype(jnp.int32),
        "cache_pages": ragged_sizes(key_list[2], REQUESTS, REQUESTS * MAXPAGES // 2, MAXPAGES, 2).astype(jnp.int32),
        "page_table": draw_page_table(jax.random.fold_in(key_list[13], 71), 0),
        "kv_cache": draw_kv_cache(jax.random.fold_in(key_list[13], 71), 0),
        "cache_variates": touch_ends(jax.random.randint(key_list[5], (CACHE_SLOTS, PAGE), 0, NVAR), jax.random.fold_in(key_list[5], 1), 0, NVAR - 1).astype(jnp.int32),
        "attn_gain": jnp.clip(1.0 + 0.15 * jax.random.normal(key_list[6], (D,), jnp.float32), 0.25, 1.75),
        "w_query": scatter_about(key_list[7], (D, D), D ** -0.5, 0.1875, ((0, 4), (1, 8))),
        "w_keyval": scatter_about(key_list[8], (D, 2 * D), D ** -0.5, 0.1875, ((0, 4), (1, 8))),
        "w_out": scatter_about(key_list[9], (D, D), D ** -0.5, 0.1875, ((0, 4), (1, 8))),
        "variate_bias": scatter_about(key_list[10], (2, H), 1.0, 3.0, (), jnp.float32),
        "head_gain": jnp.clip(1.0 + 0.15 * jax.random.normal(key_list[11], (D,), jnp.float32), 0.25, 1.75),
        "w_head": scatter_about(key_list[12], (D, MIXW), D ** -0.5, 0.1875, ((0, 4), (1, 8))),
    }


EPSILON = 1e-05
NEGATIVE = -1e+30

def rms_norm(values, gain):
    wide = values.astype(jnp.float32)
    power = lax.optimization_barrier(jnp.mean(wide * wide, axis=-1, keepdims=True))
    return (wide * lax.rsqrt(power + EPSILON) * gain.astype(jnp.float32)).astype(jnp.bfloat16)

def rope_angles(positions, half_width):
    steps = jnp.arange(half_width, dtype=jnp.float32) / half_width
    freqs = jnp.exp(-math.log(10000.0) * steps)
    angle = positions.astype(jnp.float32)[:, None] * freqs[None, :]
    return (jnp.cos(angle), jnp.sin(angle))

def rotate(values, cosine, sine_part, head_count):
    count = values.shape[0]
    halves = values.astype(jnp.float32).reshape(count, head_count, 2, -1)
    front_half = halves[:, :, 0, :]
    second = halves[:, :, 1, :]
    cosine_wide = cosine[:, None, :]
    sine_wide = sine_part[:, None, :]
    turned = jnp.stack([front_half * cosine_wide - second * sine_wide, second * cosine_wide + front_half * sine_wide], axis=2)
    return turned.reshape(count, -1).astype(jnp.bfloat16)

def lookup_small(table_rows, lookup_index, count):
    matches = lookup_index[:, None] == jnp.arange(count, dtype=jnp.int32)[None, :]
    return lax.optimization_barrier(jnp.sum(jnp.where(matches, table_rows[None, :], 0), axis=1)).astype(jnp.int32)

def slot_owners(table_rows, pages_held, slot_base, count):
    request_count, page_count = table_rows.shape
    slot_ids = slot_base + jnp.arange(count, dtype=jnp.int32)
    matches = table_rows[:, :, None] == slot_ids[None, None, :]
    live_pages = jnp.arange(page_count, dtype=jnp.int32)[None, :, None] < pages_held[:, None, None]
    live_hits = matches & live_pages
    used = jnp.any(live_hits, axis=(0, 1))
    request_ids = lax.optimization_barrier(jnp.sum(jnp.where(live_hits, jnp.arange(request_count, dtype=jnp.int32)[:, None, None], 0), axis=(0, 1))).astype(jnp.int32)
    return (used, request_ids)

def block_stats(query_rows, key_rows, value_rows, allowed, same_var, variate_bias, head_count):
    count = query_rows.shape[0]
    width = key_rows.shape[0]
    query_heads = query_rows.astype(jnp.float32).reshape(count, head_count, -1)
    key_heads = key_rows.astype(jnp.float32).reshape(width, head_count, -1)
    value_heads = value_rows.astype(jnp.float32).reshape(width, head_count, -1)
    scaling = 1.0 / math.sqrt(query_heads.shape[2])
    scores = jnp.einsum('qhd,khd->qhk', query_heads, key_heads) * scaling
    variate_term = jnp.where(same_var[:, None, :], variate_bias[0][None, :, None], variate_bias[1][None, :, None])
    masked = jnp.where(allowed[:, None, :], scores + variate_term, NEGATIVE)
    block_peak = lax.optimization_barrier(jnp.max(masked, axis=2))
    block_exps = jnp.where(allowed[:, None, :], jnp.exp(masked - block_peak[:, :, None]), 0.0)
    block_total = lax.optimization_barrier(jnp.sum(block_exps, axis=2))
    block_weights = block_exps.astype(jnp.bfloat16).astype(jnp.float32)
    summed = jnp.einsum('qhk,khd->qhd', block_weights, value_heads)
    return (block_peak, block_total, summed)

def merge_state(carry_state, block_part):
    old_peak, old_total, old_summed = carry_state
    new_peak, new_total, new_summed = block_part
    running_peak = jnp.maximum(old_peak, new_peak)
    keep_factor = jnp.exp(old_peak - running_peak)
    take_factor = jnp.exp(new_peak - running_peak)
    return (running_peak, old_total * keep_factor + new_total * take_factor, old_summed * keep_factor[..., None] + new_summed * take_factor[..., None])

def keep_same(carry_state):
    return carry_state

def group_attention(queries, new_pairs, group_ids, pages_held, table_rows, cache_group, cache_ids, variate_bias):
    used, slot_request = slot_owners(table_rows, pages_held, 0, N_PG * SLOTS)

    def one_request(request):
        query_rows = lax.dynamic_slice_in_dim(queries, request * FRESH, FRESH, 0)
        query_ids = lax.dynamic_slice_in_dim(group_ids, request * FRESH, FRESH, 0)
        start_state = (jnp.full((FRESH, H), NEGATIVE, jnp.float32), jnp.zeros((FRESH, H), jnp.float32), jnp.zeros((FRESH, H, DH), jnp.float32))

        def visit(carry_state, entry):

            def work(inner_state):
                page = lax.dynamic_index_in_dim(cache_group, entry, 0, keepdims=False)
                page_ids = lax.dynamic_index_in_dim(cache_ids, entry, 0, keepdims=False)
                allowed = jnp.ones((FRESH, PAGE), dtype=jnp.bool_)
                same_var = query_ids[:, None] == page_ids[None, :]
                return merge_state(inner_state, block_stats(query_rows, page[:, :D], page[:, D:], allowed, same_var, variate_bias, H))
            take = used[entry] & (slot_request[entry] == request)
            return (lax.cond(take, work, keep_same, carry_state), None)
        state, _ = lax.scan(visit, start_state, jnp.arange(N_PG * SLOTS, dtype=jnp.int32))

        def fresh_step(inner_state, block):
            begin_row = block * TOK_DEV

            def fresh_block(block_state):
                block_rows = lax.dynamic_slice_in_dim(new_pairs, begin_row, TOK_DEV, 0)
                block_ids = lax.dynamic_slice_in_dim(group_ids, begin_row, TOK_DEV, 0)
                offset = begin_row % FRESH
                allowed = (offset + jnp.arange(TOK_DEV, dtype=jnp.int32))[None, :] <= jnp.arange(FRESH, dtype=jnp.int32)[:, None]
                same_var = query_ids[:, None] == block_ids[None, :]
                return merge_state(block_state, block_stats(query_rows, block_rows[:, :D], block_rows[:, D:], allowed, same_var, variate_bias, H))
            return (lax.cond(begin_row // FRESH == request, fresh_block, keep_same, inner_state), None)
        state, _ = lax.scan(fresh_step, state, jnp.arange(N_PG, dtype=jnp.int32))
        return (state[2] / state[1][..., None]).reshape(FRESH, D).astype(jnp.bfloat16)
    return lax.map(one_request, jnp.arange(REQ_DEV, dtype=jnp.int32))

def reference(tokens, variate_ids, cache_pages, page_table, kv_cache, cache_variates, attn_gain, w_query, w_keyval, w_out, variate_bias, head_gain, w_head):
    normed = rms_norm(tokens, attn_gain)
    query_raw = jnp.dot(normed, w_query, preferred_element_type=jnp.float32).astype(jnp.bfloat16)
    keyval_raw = jnp.dot(normed, w_keyval, preferred_element_type=jnp.float32).astype(jnp.bfloat16)
    row_index = jnp.arange(TOKENS, dtype=jnp.int32)
    positions = lookup_small(cache_pages, row_index // FRESH, REQUESTS) * PAGE + row_index % FRESH
    cosine, sine_part = rope_angles(positions, DH // 2)
    queries = rotate(query_raw, cosine, sine_part, H)
    new_keys = rotate(keyval_raw[:, :D], cosine, sine_part, H)
    appended = jnp.concatenate([new_keys, keyval_raw[:, D:]], axis=1)
    group_count = REQUESTS // REQ_DEV
    span = REQ_DEV * FRESH
    group_slots = N_PG * SLOTS

    def per_group(group_index):
        return group_attention(lax.dynamic_slice_in_dim(queries, group_index * span, span, 0), lax.dynamic_slice_in_dim(appended, group_index * span, span, 0), lax.dynamic_slice_in_dim(variate_ids, group_index * span, span, 0), lax.dynamic_slice_in_dim(cache_pages, group_index * REQ_DEV, REQ_DEV, 0), lax.dynamic_slice_in_dim(page_table, group_index * REQ_DEV, REQ_DEV, 0), lax.dynamic_slice_in_dim(kv_cache, group_index * group_slots, group_slots, 0), lax.dynamic_slice_in_dim(cache_variates, group_index * group_slots, group_slots, 0), variate_bias)
    attention = lax.map(per_group, jnp.arange(group_count, dtype=jnp.int32)).reshape(TOKENS, D)
    hidden = (tokens.astype(jnp.float32) + jnp.dot(attention, w_out, preferred_element_type=jnp.float32)).astype(jnp.bfloat16)
    head_in = rms_norm(hidden, head_gain)
    logits = jnp.dot(head_in, w_head, preferred_element_type=jnp.float32)
    wide = hidden.astype(jnp.float32)
    energy = lax.optimization_barrier(jnp.sum((wide * wide).reshape(REQUESTS, FRESH * D), axis=1))
    peaks = lax.optimization_barrier(jnp.max(logits.reshape(REQUESTS, FRESH * MIXW), axis=1))
    return (hidden, appended, logits.astype(jnp.bfloat16), jnp.sqrt(energy), peaks)
```

```python
import math

import jax
import jax.numpy as jnp
from jax import lax
from jax.experimental import pallas as pl
from jax.experimental.pallas import tpu as pltpu
from jax.sharding import PartitionSpec as P

PAGE = 128


EPSILON = 1e-05
NEGATIVE = -1e30


def joined_2(value, axis, join):
    pieces = jax.tree.map(lambda part: lax.all_gather(part, axis), value)
    head = jax.tree.map(lambda part: part[0], pieces)
    tail = jax.tree.map(lambda part: part[1:], pieces)
    total, _ = lax.scan(lambda total, slab: (join(total, slab), None), head, tail)
    return total


def rms_norm(values, gain):
    wide = values.astype(jnp.float32)
    power = jnp.mean(wide * wide, axis=-1, keepdims=True)
    return (wide * lax.rsqrt(power + EPSILON) * gain).astype(jnp.bfloat16)


def rope_angles(positions, half_width):
    steps = jnp.arange(half_width, dtype=jnp.float32) / half_width
    freqs = jnp.exp(-math.log(10000.0) * steps)
    angle = positions.astype(jnp.float32)[:, None] * freqs[None, :]
    return (jnp.cos(angle), jnp.sin(angle))


def rotate(values, cosine, sine_part, head_count):
    count = values.shape[0]
    halves = values.astype(jnp.float32).reshape(count, head_count, 2, -1)
    front_half = halves[:, :, 0, :]
    second = halves[:, :, 1, :]
    cosine_wide = cosine[:, None, :]
    sine_wide = sine_part[:, None, :]
    turned = jnp.stack(
        [
            front_half * cosine_wide - second * sine_wide,
            second * cosine_wide + front_half * sine_wide,
        ],
        axis=2,
    )
    return turned.reshape(count, -1).astype(jnp.bfloat16)


def lookup_small(table_rows, lookup_index, count):
    matches = lookup_index[:, None] == jnp.arange(count, dtype=jnp.int32)[None, :]
    return jnp.sum(jnp.where(matches, table_rows[None, :], 0), axis=1)


def combine_stats(left_side, right_side):
    return (left_side[0] + right_side[0], jnp.maximum(left_side[1], right_side[1]))


def attend_kernel(
    pages_ref, table_ref, bias_ref, q_ref, ids_ref, new_ref, cids_ref, kv_hbm,
    out_ref, kv_buf, vt_buf, acc_ref, peak_ref, sum_ref, same_ref, sems,
):
    request_count, _, span = ids_ref.shape
    slot_count, page_rows, _ = kv_hbm.shape
    features = q_ref.shape[1]
    pairs = features // 128
    own_rows = new_ref.shape[0]
    entries = table_ref.shape[1]
    me = lax.axis_index("pg")

    def fetch(slot):
        return pltpu.make_async_copy(kv_hbm.at[slot], kv_buf.at[slot], sems.at[slot])

    for slot in range(slot_count):
        fetch(slot).start()

    acc_ref[...] = jnp.zeros_like(acc_ref)
    sum_ref[...] = jnp.zeros_like(sum_ref)
    peak_ref[...] = jnp.full_like(peak_ref, NEGATIVE)

    def absorb(request, k_of, v_of, key_ids, count, offset):
        lane = lax.broadcasted_iota(jnp.int32, (count, 128), 1)
        left = jnp.where(lane < 64, 1.0, 0.0).astype(jnp.bfloat16)
        right = jnp.where(lane < 64, 0.0, 1.0).astype(jnp.bfloat16)
        row = lax.broadcasted_iota(jnp.int32, (128, count), 0)
        ones_row = lax.broadcasted_iota(jnp.int32, (16, 2 * count), 0)
        ones_col = lax.broadcasted_iota(jnp.int32, (16, 2 * count), 1)
        ones = jnp.where((ones_row < 8) == (ones_col < count), 1.0, 0.0).astype(jnp.bfloat16)
        for pair in range(pairs):
            value = v_of(pair).astype(jnp.float32).T
            vt_buf[pair, :128, 0:count] = jnp.where(row < 64, value, 0.0).astype(jnp.bfloat16)
            vt_buf[pair, :128, count : 2 * count] = jnp.where(row >= 64, value, 0.0).astype(
                jnp.bfloat16
            )
            vt_buf[pair, 128:, 0 : 2 * count] = ones

        def tile(index, _):
            start = pl.multiple_of(index * 256, 256)
            query_ids = ids_ref[request, :, pl.ds(start, 256)]
            same = jnp.broadcast_to(query_ids, (count, 256)) == jnp.concatenate(
                [key_ids, key_ids], axis=1
            )
            same_ref[:count] = jnp.where(same, 1.0, 0.0)
            if offset is not None:
                allowed = (
                    lax.broadcasted_iota(jnp.int32, (count, 256), 0) + offset
                    <= lax.broadcasted_iota(jnp.int32, (count, 256), 1) + start
                )
            for pair in range(pairs):
                keys = k_of(pair)
                both = jnp.concatenate([keys * left, keys * right], axis=0)
                query = q_ref[pl.ds(request * span + start, 256), 128 * pair : 128 * pair + 128]
                scores = lax.dot_general(
                    both, query, (((1,), (1,)), ((), ())), preferred_element_type=jnp.float32
                )
                weights, fades = [], []
                for side in range(2):
                    head = 2 * pair + side
                    part = scores[side * count : (side + 1) * count] * 0.125
                    part = part + jnp.where(
                        same_ref[:count] > 0.5, bias_ref[0, head], bias_ref[1, head]
                    )
                    if offset is not None:
                        part = jnp.where(allowed, part, NEGATIVE)
                    old = peak_ref[request, head : head + 1, pl.ds(start, 256)]
                    new = jnp.maximum(old, jnp.max(part, axis=0, keepdims=True))
                    peak_ref[request, head : head + 1, pl.ds(start, 256)] = new
                    weight = jnp.exp(part - new)
                    if offset is not None:
                        weight = jnp.where(allowed, weight, 0.0)
                    weights.append(weight.astype(jnp.bfloat16))
                    fades.append(jnp.exp(old - new))
                summed = jnp.dot(
                    vt_buf[pair, :, 0 : 2 * count],
                    jnp.concatenate(weights, axis=0),
                    preferred_element_type=jnp.float32,
                )
                for side in range(2):
                    head = 2 * pair + side
                    rows = slice(128 * pair + 64 * side, 128 * pair + 64 * side + 64)
                    acc_ref[request, rows, pl.ds(start, 256)] = (
                        acc_ref[request, rows, pl.ds(start, 256)] * fades[side]
                        + summed[64 * side : 64 * side + 64]
                    )
                    sum_ref[request, head : head + 1, pl.ds(start, 256)] = (
                        sum_ref[request, head : head + 1, pl.ds(start, 256)] * fades[side]
                        + summed[128 + 8 * side : 129 + 8 * side]
                    )
            return 0

        lax.fori_loop(0, span // 256, tile, 0)

    first_row = me * own_rows
    request_own = first_row // span
    offset = first_row % span
    chunk = pl.multiple_of((offset // 128) * 128, 128)
    wide_ids = ids_ref[request_own, :, pl.ds(chunk, 128)]
    column = jnp.broadcast_to(wide_ids, (128, 128)).T
    lower = offset - chunk
    own_ids = jnp.where(lower == 0, column[:own_rows], column[128 - own_rows :])
    absorb(
        request_own,
        lambda pair: new_ref[:, 128 * pair : 128 * pair + 128],
        lambda pair: new_ref[:, features + 128 * pair : features + 128 * pair + 128],
        own_ids,
        own_rows,
        offset,
    )

    def visit(slot, _):
        entry = me * slot_count + slot

        def look(flat, owner):
            request = flat // entries
            page = flat % entries
            hit = (table_ref[request, page] == entry) & (page < pages_ref[request])
            return jnp.where(hit, request, owner)

        owner = lax.fori_loop(0, request_count * entries, look, jnp.int32(-1))
        fetch(slot).wait()

        @pl.when(owner >= 0)
        def _():
            column = jnp.broadcast_to(cids_ref[pl.ds(slot, 1), :], (page_rows, 128)).T
            absorb(
                owner,
                lambda pair: kv_buf[slot, :, 128 * pair : 128 * pair + 128],
                lambda pair: kv_buf[slot, :, features + 128 * pair : features + 128 * pair + 128],
                column,
                page_rows,
                None,
            )

        return 0

    lax.fori_loop(0, slot_count, visit, 0)

    def close(flat, _):
        request = flat // (span // 256)
        start = pl.multiple_of((flat % (span // 256)) * 256, 256)
        place = pl.ds(pl.multiple_of(flat * 256, 256), 256)
        total = sum_ref[request, :, pl.ds(start, 256)]
        live = total > 0
        safe = jnp.where(live, total, 1.0)
        level = jnp.where(live, peak_ref[request, :, pl.ds(start, 256)] + jnp.log(safe), NEGATIVE)
        inverse = jnp.where(live, 1.0 / safe, 0.0)
        for pair in range(pairs):
            block = jnp.concatenate(
                [
                    acc_ref[request, 128 * pair + 64 * side : 128 * pair + 64 * side + 64, pl.ds(start, 256)]
                    * inverse[2 * pair + side : 2 * pair + side + 1]
                    for side in range(2)
                ],
                axis=0,
            )
            out_ref[place, 128 * pair : 128 * pair + 128] = block.T.astype(jnp.bfloat16)
        high = level.astype(jnp.bfloat16).astype(jnp.float32)
        middle = (level - high).astype(jnp.bfloat16).astype(jnp.float32)
        low = level - high - middle
        heads = level.shape[0]
        filler = jnp.zeros((128 - 3 * heads, 256), jnp.float32)
        stacked = jnp.concatenate([high, middle, low, filler], axis=0)
        out_ref[place, features : features + 128] = stacked.T.astype(jnp.bfloat16)
        return 0

    lax.fori_loop(0, request_count * (span // 256), close, 0)


def attend(pages, table, bias, queries, ids, new_pairs, cache_ids, kv_cache):
    request_count = pages.shape[0]
    rows, features = queries.shape
    span = rows // request_count
    slot_count, page_rows, _ = kv_cache.shape
    heads = bias.shape[1]
    smem = pl.BlockSpec(memory_space=pltpu.SMEM)
    vmem = pl.BlockSpec(memory_space=pltpu.VMEM)
    return pl.pallas_call(
        attend_kernel,
        out_shape=jax.ShapeDtypeStruct((rows, features + 128), jnp.bfloat16),
        in_specs=[smem, smem, smem, vmem, vmem, vmem, vmem, pl.BlockSpec(memory_space=pl.ANY)],
        out_specs=vmem,
        scratch_shapes=[
            pltpu.VMEM(kv_cache.shape, jnp.bfloat16),
            pltpu.VMEM((features // 128, 144, 2 * page_rows), jnp.bfloat16),
            pltpu.VMEM((request_count, features, span), jnp.float32),
            pltpu.VMEM((request_count, heads, span), jnp.float32),
            pltpu.VMEM((request_count, heads, span), jnp.float32),
            pltpu.VMEM((page_rows, 256), jnp.float32),
            pltpu.SemaphoreType.DMA((slot_count,)),
        ],
        compiler_params=pltpu.CompilerParams(vmem_limit_bytes=56 * 1024 * 1024),
        cost_estimate=pl.CostEstimate(
            flops=4 * slot_count * page_rows * span * features * 4,
            bytes_accessed=kv_cache.size * 2 + rows * features * 4,
            transcendentals=slot_count * page_rows * span * heads,
        ),
    )(pages, table, bias, queries, ids.reshape(request_count, 1, span), new_pairs, cache_ids, kv_cache)


def per_device(
    tokens,
    variate_ids,
    cache_pages,
    page_table,
    kv_cache,
    cache_variates,
    attn_gain,
    w_query,
    w_keyval,
    w_out,
    variate_bias,
    head_gain,
    w_head,
):
    own_rows, features = tokens.shape
    request_count = cache_pages.shape[0]
    group_rows = variate_ids.shape[0]
    span_rows = group_rows // request_count
    head_count = variate_bias.shape[1]
    head_width = features // head_count
    holder_index = lax.axis_index("pg")
    first_row = holder_index * own_rows
    own_request = first_row // span_rows
    normed = rms_norm(tokens, attn_gain)
    query_full, keyval_full, out_full, head_full = (
        lax.all_gather(w_query, "req", axis=0, tiled=True),
        lax.all_gather(w_keyval, "req", axis=0, tiled=True),
        lax.all_gather(w_out, "req", axis=0, tiled=True),
        lax.all_gather(w_head, "req", axis=0, tiled=True),
    )
    own_index = first_row + jnp.arange(own_rows, dtype=jnp.int32)
    own_positions = (
        lookup_small(cache_pages, own_index // span_rows, request_count) * PAGE
        + own_index % span_rows
    )
    own_cos, own_sin = rope_angles(own_positions, head_width // 2)
    query_cols = query_full.shape[1]
    joined = jnp.concatenate([query_full, keyval_full], axis=1)
    projected = jnp.dot(
        normed, lax.all_gather(joined, "pg", axis=1, tiled=True), preferred_element_type=jnp.float32
    )
    projected = projected.reshape(own_rows, -1, joined.shape[1])
    query_raw = projected[:, :, :query_cols].reshape(own_rows, features).astype(jnp.bfloat16)
    keyval_raw = projected[:, :, query_cols:].reshape(own_rows, 2 * features).astype(jnp.bfloat16)
    own_queries = rotate(query_raw, own_cos, own_sin, head_count)
    new_keys = rotate(keyval_raw[:, :features], own_cos, own_sin, head_count)
    new_values = keyval_raw[:, features:]
    appended = jnp.concatenate([new_keys, new_values], axis=1)
    queries = lax.all_gather(own_queries, "pg", axis=0, tiled=True)
    partial_out = attend(
        cache_pages,
        page_table,
        variate_bias,
        queries,
        variate_ids,
        appended,
        cache_variates,
        kv_cache,
    )
    holders = group_rows // own_rows
    parts = lax.all_to_all(
        partial_out.reshape(holders, own_rows, features + 128), "pg", 0, 0, tiled=True
    )
    levels = parts[:, :, features : features + 3 * head_count].astype(jnp.float32)
    levels = levels.reshape(holders, own_rows, 3, head_count).sum(axis=2)
    shares = jax.nn.softmax(levels, axis=0)
    attention = (
        jnp.sum(
            parts[:, :, :features].astype(jnp.float32).reshape(holders, own_rows, head_count, -1)
            * shares[..., None],
            axis=0,
        )
        .reshape(own_rows, features)
        .astype(jnp.bfloat16)
    )
    out_part = jnp.dot(
        attention,
        lax.all_gather(out_full, "pg", axis=1, tiled=True),
        preferred_element_type=jnp.float32,
    )
    hidden = (tokens.astype(jnp.float32) + out_part).astype(jnp.bfloat16)
    head_in = rms_norm(hidden, head_gain)
    logits = jnp.dot(
        head_in,
        lax.all_gather(head_full, "pg", axis=1, tiled=True),
        preferred_element_type=jnp.float32,
    )
    wide = hidden.astype(jnp.float32)
    energy = jnp.sum(wide * wide)
    peak_logit = jnp.max(logits)
    own_slot = jnp.arange(request_count, dtype=jnp.int32) == own_request
    energies = jnp.where(own_slot, energy, 0.0)
    peak_terms = jnp.where(own_slot, peak_logit, NEGATIVE)
    total_energy, request_top = joined_2((energies, peak_terms), "pg", combine_stats)
    return (hidden, appended, logits.astype(jnp.bfloat16), jnp.sqrt(total_energy), request_top)


def solution(mesh):
    placed = (
        P(("req", "pg"), None),
        P("req"),
        P("req"),
        P("req", None),
        P(("req", "pg"), None, None),
        P(("req", "pg"), None),
        P(),
        P("req", "pg"),
        P("req", "pg"),
        P("req", "pg"),
        P(),
        P(),
        P("req", "pg"),
    )
    return jax.shard_map(
        per_device,
        mesh=mesh,
        in_specs=placed,
        out_specs=(
            P(("req", "pg"), None),
            P(("req", "pg"), None),
            P(("req", "pg"), None),
            P("req"),
            P("req"),
        ),
        check_vma=False,
    )
```

```python
import functools
import math

import jax
import jax.numpy as jnp
from jax import lax
from jax.experimental import pallas as pl
from jax.experimental.pallas import tpu as pltpu
from jax.sharding import PartitionSpec as P

PAGE = 128


EPSILON = 1e-05
NEGATIVE = -1e30


def rms_norm(values, gain):
    wide = values.astype(jnp.float32)
    power = jnp.mean(wide * wide, axis=-1, keepdims=True)
    return (wide * lax.rsqrt(power + EPSILON) * gain).astype(jnp.bfloat16)


def rope_angles(positions, half_width):
    steps = jnp.arange(half_width, dtype=jnp.float32) / half_width
    freqs = jnp.exp(-math.log(10000.0) * steps)
    angle = positions.astype(jnp.float32)[:, None] * freqs[None, :]
    return (jnp.cos(angle), jnp.sin(angle))


def rotate(values, cosine, sine_part, head_count):
    count = values.shape[0]
    halves = values.astype(jnp.float32).reshape(count, head_count, 2, -1)
    front_half = halves[:, :, 0, :]
    second = halves[:, :, 1, :]
    cosine_wide = cosine[:, None, :]
    sine_wide = sine_part[:, None, :]
    turned = jnp.stack(
        [
            front_half * cosine_wide - second * sine_wide,
            second * cosine_wide + front_half * sine_wide,
        ],
        axis=2,
    )
    return turned.reshape(count, -1).astype(jnp.bfloat16)


def lookup_small(table_rows, lookup_index, count):
    matches = lookup_index[:, None] == jnp.arange(count, dtype=jnp.int32)[None, :]
    return jnp.sum(jnp.where(matches, table_rows[None, :], 0), axis=1)


def attend_kernel(
    pages_ref, table_ref, bias_ref, q_ref, ids_ref, new_ref, cids_ref, kv_hbm,
    out_ref, kv_buf, vt_buf, acc_ref, peak_ref, sum_ref, same_ref, sems,
):
    request_count, _, span = ids_ref.shape
    slot_count, page_rows, _ = kv_hbm.shape
    pairs = q_ref.shape[0]
    features = 128 * pairs
    own_rows = new_ref.shape[0]
    entries = table_ref.shape[1]
    me = lax.axis_index("pg")

    def fetch(slot):
        return pltpu.make_async_copy(kv_hbm.at[slot], kv_buf.at[slot], sems.at[slot])

    for slot in range(slot_count):
        fetch(slot).start()

    acc_ref[...] = jnp.zeros_like(acc_ref)
    sum_ref[...] = jnp.zeros_like(sum_ref)
    peak_ref[...] = jnp.full_like(peak_ref, NEGATIVE)

    def absorb(request, k_of, v_of, key_ids, count, offset):
        lane = lax.broadcasted_iota(jnp.int32, (count, 128), 1)
        left = jnp.where(lane < 64, 1.0, 0.0).astype(jnp.bfloat16)
        right = jnp.where(lane < 64, 0.0, 1.0).astype(jnp.bfloat16)
        row = lax.broadcasted_iota(jnp.int32, (128, count), 0)
        ones_row = lax.broadcasted_iota(jnp.int32, (16, 2 * count), 0)
        ones_col = lax.broadcasted_iota(jnp.int32, (16, 2 * count), 1)
        ones = jnp.where((ones_row < 8) == (ones_col < count), 1.0, 0.0).astype(jnp.bfloat16)
        for pair in range(pairs):
            value = v_of(pair).astype(jnp.float32).T
            vt_buf[pair, :128, 0:count] = jnp.where(row < 64, value, 0.0).astype(jnp.bfloat16)
            vt_buf[pair, :128, count : 2 * count] = jnp.where(row >= 64, value, 0.0).astype(
                jnp.bfloat16
            )
            vt_buf[pair, 128:, 0 : 2 * count] = ones

        def tile(index, _):
            start = pl.multiple_of(index * 256, 256)
            query_ids = ids_ref[request, :, pl.ds(start, 256)]
            same = jnp.broadcast_to(query_ids, (count, 256)) == jnp.concatenate(
                [key_ids, key_ids], axis=1
            )
            same_ref[:count] = jnp.where(same, 1.0, 0.0)
            if offset is not None:
                allowed = (
                    lax.broadcasted_iota(jnp.int32, (count, 256), 0) + offset
                    <= lax.broadcasted_iota(jnp.int32, (count, 256), 1) + start
                )
            for pair in range(pairs):
                keys = k_of(pair)
                both = jnp.concatenate([keys * left, keys * right], axis=0)
                query = q_ref[pair, pl.ds(request * span + start, 256), :]
                scores = lax.dot_general(
                    both, query, (((1,), (1,)), ((), ())), preferred_element_type=jnp.float32
                )
                weights, fades = [], []
                for side in range(2):
                    head = 2 * pair + side
                    part = scores[side * count : (side + 1) * count] * 0.125
                    part = part + jnp.where(
                        same_ref[:count] > 0.5, bias_ref[0, head], bias_ref[1, head]
                    )
                    if offset is not None:
                        part = jnp.where(allowed, part, NEGATIVE)
                    old = peak_ref[request, head : head + 1, pl.ds(start, 256)]
                    new = jnp.maximum(old, jnp.max(part, axis=0, keepdims=True))
                    peak_ref[request, head : head + 1, pl.ds(start, 256)] = new
                    weight = jnp.exp(part - new)
                    if offset is not None:
                        weight = jnp.where(allowed, weight, 0.0)
                    weights.append(weight.astype(jnp.bfloat16))
                    fades.append(jnp.exp(old - new))
                summed = jnp.dot(
                    vt_buf[pair, :, 0 : 2 * count],
                    jnp.concatenate(weights, axis=0),
                    preferred_element_type=jnp.float32,
                )
                for side in range(2):
                    head = 2 * pair + side
                    rows = slice(128 * pair + 64 * side, 128 * pair + 64 * side + 64)
                    acc_ref[request, rows, pl.ds(start, 256)] = (
                        acc_ref[request, rows, pl.ds(start, 256)] * fades[side]
                        + summed[64 * side : 64 * side + 64]
                    )
                    sum_ref[request, head : head + 1, pl.ds(start, 256)] = (
                        sum_ref[request, head : head + 1, pl.ds(start, 256)] * fades[side]
                        + summed[128 + 8 * side : 129 + 8 * side]
                    )
            return 0

        lax.fori_loop(0, span // 256, tile, 0)

    first_row = me * own_rows
    request_own = first_row // span
    offset = first_row % span
    chunk = pl.multiple_of((offset // 128) * 128, 128)
    wide_ids = ids_ref[request_own, :, pl.ds(chunk, 128)]
    column = jnp.broadcast_to(wide_ids, (128, 128)).T
    lower = offset - chunk
    own_ids = jnp.where(lower == 0, column[:own_rows], column[128 - own_rows :])
    absorb(
        request_own,
        lambda pair: new_ref[:, 128 * pair : 128 * pair + 128],
        lambda pair: new_ref[:, features + 128 * pair : features + 128 * pair + 128],
        own_ids,
        own_rows,
        offset,
    )

    def visit(slot, _):
        entry = me * slot_count + slot

        def look(flat, owner):
            request = flat // entries
            page = flat % entries
            hit = (table_ref[request, page] == entry) & (page < pages_ref[request])
            return jnp.where(hit, request, owner)

        owner = lax.fori_loop(0, request_count * entries, look, jnp.int32(-1))
        fetch(slot).wait()

        @pl.when(owner >= 0)
        def _():
            column = jnp.broadcast_to(cids_ref[pl.ds(slot, 1), :], (page_rows, 128)).T
            absorb(
                owner,
                lambda pair: kv_buf[slot, :, 128 * pair : 128 * pair + 128],
                lambda pair: kv_buf[slot, :, features + 128 * pair : features + 128 * pair + 128],
                column,
                page_rows,
                None,
            )

        return 0

    lax.fori_loop(0, slot_count, visit, 0)

    def close(flat, _):
        request = flat // (span // 256)
        start = pl.multiple_of((flat % (span // 256)) * 256, 256)
        place = pl.ds(pl.multiple_of(flat * 256, 256), 256)
        total = sum_ref[request, :, pl.ds(start, 256)]
        live = total > 0
        safe = jnp.where(live, total, 1.0)
        level = jnp.where(live, peak_ref[request, :, pl.ds(start, 256)] + jnp.log(safe), NEGATIVE)
        inverse = jnp.where(live, 1.0 / safe, 0.0)
        for pair in range(pairs):
            block = jnp.concatenate(
                [
                    acc_ref[request, 128 * pair + 64 * side : 128 * pair + 64 * side + 64, pl.ds(start, 256)]
                    * inverse[2 * pair + side : 2 * pair + side + 1]
                    for side in range(2)
                ],
                axis=0,
            )
            out_ref[place, 128 * pair : 128 * pair + 128] = block.T.astype(jnp.bfloat16)
        high = level.astype(jnp.bfloat16).astype(jnp.float32)
        middle = (level - high).astype(jnp.bfloat16).astype(jnp.float32)
        low = level - high - middle
        heads = level.shape[0]
        filler = jnp.zeros((128 - 3 * heads, 256), jnp.float32)
        stacked = jnp.concatenate([high, middle, low, filler], axis=0)
        out_ref[place, features : features + 128] = stacked.T.astype(jnp.bfloat16)
        return 0

    lax.fori_loop(0, request_count * (span // 256), close, 0)


def attend(pages, table, bias, queries, ids, new_pairs, cache_ids, kv_cache):
    request_count = pages.shape[0]
    pairs, rows, _ = queries.shape
    features = 128 * pairs
    span = rows // request_count
    slot_count, page_rows, _ = kv_cache.shape
    heads = bias.shape[1]
    smem = pl.BlockSpec(memory_space=pltpu.SMEM)
    vmem = pl.BlockSpec(memory_space=pltpu.VMEM)
    return pl.pallas_call(
        attend_kernel,
        out_shape=jax.ShapeDtypeStruct((rows, features + 128), jnp.bfloat16),
        in_specs=[smem, smem, smem, vmem, vmem, vmem, vmem, pl.BlockSpec(memory_space=pl.ANY)],
        out_specs=vmem,
        scratch_shapes=[
            pltpu.VMEM(kv_cache.shape, jnp.bfloat16),
            pltpu.VMEM((features // 128, 144, 2 * page_rows), jnp.bfloat16),
            pltpu.VMEM((request_count, features, span), jnp.float32),
            pltpu.VMEM((request_count, heads, span), jnp.float32),
            pltpu.VMEM((request_count, heads, span), jnp.float32),
            pltpu.VMEM((page_rows, 256), jnp.float32),
            pltpu.SemaphoreType.DMA((slot_count,)),
        ],
        compiler_params=pltpu.CompilerParams(vmem_limit_bytes=56 * 1024 * 1024),
        cost_estimate=pl.CostEstimate(
            flops=4 * slot_count * page_rows * span * features * 4,
            bytes_accessed=kv_cache.size * 2 + rows * features * 4,
            transcendentals=slot_count * page_rows * span * heads,
        ),
    )(pages, table, bias, queries, ids.reshape(request_count, 1, span), new_pairs, cache_ids, kv_cache)


def remote(source, target, send_sem, recv_sem, where):
    return pltpu.make_async_remote_copy(
        src_ref=source,
        dst_ref=target,
        send_sem=send_sem,
        recv_sem=recv_sem,
        device_id=where,
        device_id_type=pl.DeviceIdType.MESH,
    )


def greet(places):
    barrier = pltpu.get_barrier_semaphore()
    for place in places:
        pl.semaphore_signal(barrier, inc=1, device_id=place, device_id_type=pl.DeviceIdType.MESH)
    return lambda: pl.semaphore_wait(barrier, len(places))


def project_kernel(
    pages_ref, freq_ref, tokens_ref, gain_ref, wq_ref, wkv_ref, wo_ref, wh_ref,
    q_out, app_out, wo_out, wh_out,
    tok, wqkv, kv_stage, wh_all, cos_ref, sin_ref,
    tok_far, tok_near, tok_recv,
    w_far, w_near, w_recv,
    wox_send, wox_recv, wo_far, wo_near, wo_recv, wo_core, wo_core_recv,
    whx_send, whx_recv, wh_far, wh_near, wh_recv, wh_core, wh_core_recv,
    q_far, q_near, q_recv, kv_send, kv_recv, local_sem,
):
    _, planes, own_rows, features = tok.shape
    holders = 2 * planes
    req_count, deep, joined = wqkv.shape
    req_pairs = req_count // 2
    request_count = pages_ref.shape[0]
    rows = holders * own_rows
    span = rows // request_count
    me = lax.axis_index("pg")
    mine = lax.axis_index("req")
    zz, yy = me // 2, me % 2
    xx, cc = mine // 2, mine % 2
    other = 1 - yy
    core_place = {"req": 2 * xx + 1 - cc}
    near_place = {"pg": 2 * zz + other}

    def plane(step):
        return (zz + step) % planes

    def far_place(step):
        return {"pg": 2 * plane(step) + yy}

    def req_far(step):
        return (xx + step) % req_pairs

    places = [{"pg": (me + step) % holders} for step in range(1, holders)]
    places += [{"req": 2 * req_far(step) + cc} for step in range(1, req_pairs)] + [core_place]
    arrived = greet(places)

    wide = tokens_ref[...].astype(jnp.float32)
    power = jnp.mean(wide * wide, axis=-1, keepdims=True)
    tok[yy, zz] = (wide * lax.rsqrt(power + EPSILON) * gain_ref[...]).astype(jnp.bfloat16)
    wqkv[mine, :, 0:128] = wq_ref[...]
    wqkv[mine, :, 128:joined] = wkv_ref[...]
    head_cols = wh_ref.shape[1]
    packs = 128 // head_cols
    slab = deep // packs
    wh_wide = wh_ref[...].astype(jnp.float32)
    wh_all[xx, cc, me] = jnp.concatenate(
        [wh_wide[slab * pack : slab * pack + slab] for pack in range(packs)], axis=1
    ).astype(jnp.bfloat16)

    def columns(holder):
        return pl.ds(pl.multiple_of(holder * 128, 128), 128)

    keep = pltpu.make_async_copy(wo_ref, wo_out.at[xx, cc, :, columns(me)], local_sem.at[0])
    keep.start()
    arrived()

    started = []

    def begin(copy):
        copy.start()
        started.append(copy)

    def tok_copy(side, depth, send_sem, place):
        return remote(
            tok.at[side, depth], tok.at[side, depth], send_sem, tok_recv.at[side, depth], place
        )

    for step in range(1, planes):
        begin(tok_copy(yy, zz, tok_far.at[step], far_place(step)))
    begin(tok_copy(yy, zz, tok_near.at[0], near_place))

    def w_copy(block, send_sem, place):
        return remote(wqkv.at[block], wqkv.at[block], send_sem, w_recv.at[block], place)

    for step in range(1, req_pairs):
        begin(w_copy(mine, w_far.at[step], {"req": 2 * req_far(step) + cc}))
    begin(w_copy(mine, w_near.at[0], core_place))
    for step in range(1, req_pairs):
        place = {"req": 2 * req_far(step) + cc}
        begin(
            remote(
                wo_ref, wo_out.at[xx, cc, :, columns(me)], wox_send.at[step], wox_recv.at[xx], place
            )
        )
        begin(
            remote(
                wh_all.at[xx, cc, me], wh_all.at[xx, cc, me], whx_send.at[step], whx_recv.at[xx], place
            )
        )

    row = lax.broadcasted_iota(jnp.int32, (1, rows), 1)
    held = jnp.zeros((1, rows), jnp.int32)
    for request in range(request_count):
        held = jnp.where(row // span == request, pages_ref[request], held)
    position = (held * PAGE + row % span).astype(jnp.float32)
    angle = freq_ref[...] * position
    cosine, sine = jnp.cos(angle), jnp.sin(angle)
    cos_ref[...] = jnp.concatenate([cosine] * 4, axis=0).T.reshape(cos_ref.shape)
    sin_ref[...] = jnp.concatenate([-sine, sine, -sine, sine], axis=0).T.reshape(sin_ref.shape)

    for step in range(1, req_pairs):
        block = 2 * req_far(step) + cc
        w_copy(block, w_far.at[step], core_place).wait_recv()
        begin(w_copy(block, w_near.at[step], core_place))
    for step in range(1, planes):
        tok_copy(yy, plane(step), tok_far.at[step], near_place).wait_recv()
        begin(tok_copy(yy, plane(step), tok_near.at[step], near_place))

    def wo_copy(holder, send_sem, place):
        part = wo_out.at[:, cc, :, columns(holder)]
        return remote(part, part, send_sem, wo_recv.at[holder], place)

    def wh_copy(holder, send_sem, place):
        part = wh_all.at[:, cc, holder]
        return remote(part, part, send_sem, wh_recv.at[holder], place)

    keep.wait()
    for step in range(1, req_pairs):
        depth = req_far(step)
        remote(
            wo_ref, wo_out.at[depth, cc, :, columns(me)], wox_send.at[step], wox_recv.at[depth],
            core_place,
        ).wait_recv()
        remote(
            wh_all.at[depth, cc, me], wh_all.at[depth, cc, me], whx_send.at[step], whx_recv.at[depth],
            core_place,
        ).wait_recv()

    for step in range(req_pairs):
        block = 2 * req_far(step) + 1 - cc
        w_copy(block, w_near.at[step], core_place).wait_recv()

    def q_copy(turn, holder_side, depth, send_sem, place):
        side = holder_side if turn == 0 else 1 - holder_side
        part = q_out.at[2 * depth + holder_side, :, side]
        return remote(part, part, send_sem, q_recv.at[turn, holder_side, depth], place)

    def kv_copy(source, side, depth, send_sem, place):
        start = pl.multiple_of(source * 256, 256)
        return remote(
            kv_stage.at[depth, side], app_out.at[:, pl.ds(start, 256)], send_sem,
            kv_recv.at[source], place,
        )

    lane = lax.broadcasted_iota(jnp.int32, (planes * own_rows, 128), 1)
    front = (lane % 64) < 32
    is_key = (jnp.zeros((planes * own_rows, 128), jnp.int32) + me) < planes

    def turned(value, cosine, sine):
        value = value.astype(jnp.bfloat16).astype(jnp.float32)
        swapped = jnp.where(front, pltpu.roll(value, 96, 1), pltpu.roll(value, 32, 1))
        return value * cosine + swapped * sine

    def half(turn):
        side = yy if turn == 0 else other
        block = tok[side].reshape(planes * own_rows, features)
        made = jnp.dot(
            block, wqkv[...].reshape(features, joined), preferred_element_type=jnp.float32
        )
        cosine = cos_ref[:, side].reshape(planes * own_rows, 128)
        sine = sin_ref[:, side].reshape(planes * own_rows, 128)
        q_out[me, :, side] = (
            turned(made[:, :128], cosine, sine)
            .astype(jnp.bfloat16)
            .reshape(planes, own_rows, 128)
        )
        for step in range(1, planes):
            begin(q_copy(turn, yy, zz, q_far.at[turn, step], far_place(step)))
        begin(q_copy(turn, yy, zz, q_near.at[turn, 0], near_place))
        key_cos = jnp.where(is_key, cosine, 1.0)
        key_sin = jnp.where(is_key, sine, 0.0)
        for part in range((joined - 128) // 128):
            piece = turned(made[:, 128 + 128 * part : 256 + 128 * part], key_cos, key_sin)
            kv_stage[:, side, :, 128 * part : 128 * part + 128] = piece.astype(
                jnp.bfloat16
            ).reshape(planes, own_rows, 128)
        for step in range(0 if turn == 1 else 1, planes):
            place = {"pg": 2 * plane(step) + side}
            begin(kv_copy(me, side, plane(step), kv_send.at[turn, step], place))

    half(0)
    own_keep = pltpu.make_async_copy(
        kv_stage.at[zz, yy],
        app_out.at[:, pl.ds(pl.multiple_of(me * 256, 256), 256)],
        local_sem.at[1],
    )
    own_keep.start()
    for step in range(planes):
        tok_copy(other, plane(step), tok_near.at[step], near_place).wait_recv()
    half(1)

    for step in range(1, planes):
        begin(wo_copy(me, wo_far.at[step], far_place(step)))
        begin(wh_copy(me, wh_far.at[step], far_place(step)))
    begin(wo_copy(me, wo_near.at[0], near_place))
    begin(wh_copy(me, wh_near.at[0], near_place))

    for turn in range(2):
        for step in range(1, planes):
            q_copy(turn, yy, plane(step), q_far.at[turn, step], near_place).wait_recv()
            begin(q_copy(turn, yy, plane(step), q_near.at[turn, step], near_place))

    def wo_pass(holder):
        part = wo_out.at[:, cc, :, columns(holder)]
        return remote(part, part, wo_core.at[holder], wo_core_recv.at[holder], core_place)

    begin(wo_pass(me))
    for step in range(1, planes):
        holder = 2 * plane(step) + yy
        wh_copy(holder, wh_far.at[step], near_place).wait_recv()
        begin(wh_copy(holder, wh_near.at[step], near_place))
        wo_copy(holder, wo_far.at[step], near_place).wait_recv()
        begin(wo_copy(holder, wo_near.at[step], near_place))
        begin(wo_pass(holder))

    for step in range(planes):
        wh_copy(2 * plane(step) + other, wh_near.at[step], near_place).wait_recv()
    begin(remote(wh_all.at[:, cc], wh_all.at[:, cc], wh_core.at[0], wh_core_recv.at[0], core_place))
    for step in range(planes):
        holder = 2 * plane(step) + other
        wo_copy(holder, wo_near.at[step], near_place).wait_recv()
        begin(wo_pass(holder))

    arriving = wh_all.at[:, 1 - cc]
    remote(arriving, arriving, wh_core.at[0], wh_core_recv.at[0], core_place).wait_recv()
    for block in range(req_count):
        for pack in range(packs):
            wh_out[deep * block + slab * pack : deep * block + slab * pack + slab, :] = jnp.concatenate(
                [
                    wh_all[block // 2, block % 2, holder].astype(jnp.float32)[
                        :, head_cols * pack : head_cols * pack + head_cols
                    ]
                    for holder in range(holders)
                ],
                axis=1,
            ).astype(jnp.bfloat16)

    for turn in range(2):
        for step in range(planes):
            q_copy(turn, other, plane(step), q_near.at[turn, step], near_place).wait_recv()
    for step in range(1, holders):
        kv_copy((me + step) % holders, yy, zz, kv_send.at[0, 0], near_place).wait_recv()
    own_keep.wait()
    for holder in range(holders):
        part = wo_out.at[:, 1 - cc, :, columns(holder)]
        remote(part, part, wo_core.at[holder], wo_core_recv.at[holder], core_place).wait_recv()
    for copy in started:
        copy.wait_send()


def project(pages, freqs, tokens, gain, w_query, w_keyval, w_out, w_head, holders, req_count):
    own_rows, features = tokens.shape
    planes = holders // 2
    deep = w_query.shape[0]
    joined = w_query.shape[1] + w_keyval.shape[1]
    vmem = pl.BlockSpec(memory_space=pltpu.VMEM)
    bf16 = jnp.bfloat16
    dma = pltpu.SemaphoreType.DMA
    pairs = req_count // 2
    return pl.pallas_call(
        project_kernel,
        out_shape=(
            jax.ShapeDtypeStruct((holders, planes, 2, own_rows, 128), bf16),
            jax.ShapeDtypeStruct((own_rows, 2 * features), bf16),
            jax.ShapeDtypeStruct((pairs, 2, deep, features), bf16),
            jax.ShapeDtypeStruct((features, holders * w_head.shape[1]), bf16),
        ),
        in_specs=[pl.BlockSpec(memory_space=pltpu.SMEM)] + [vmem] * 7,
        out_specs=(vmem, vmem, vmem, vmem),
        scratch_shapes=[
            pltpu.VMEM((2, planes, own_rows, features), bf16),
            pltpu.VMEM((req_count, deep, joined), bf16),
            pltpu.VMEM((planes, 2, own_rows, 256), bf16),
            pltpu.VMEM((pairs, 2, holders, deep * w_head.shape[1] // 128, 128), bf16),
            pltpu.VMEM((planes, 2, own_rows, 128), jnp.float32),
            pltpu.VMEM((planes, 2, own_rows, 128), jnp.float32),
            dma((planes,)), dma((planes,)), dma((2, planes)),
            dma((pairs,)), dma((pairs,)), dma((req_count,)),
            dma((pairs,)), dma((pairs,)), dma((planes,)), dma((planes,)), dma((holders,)),
            dma((holders,)), dma((holders,)),
            dma((pairs,)), dma((pairs,)), dma((planes,)), dma((planes,)), dma((holders,)),
            dma((1,)), dma((1,)),
            dma((2, planes)), dma((2, planes)), dma((2, 2, planes)), dma((2, planes)),
            dma((holders,)), dma((2,)),
        ],
        compiler_params=pltpu.CompilerParams(
            collective_id=0, has_side_effects=True, vmem_limit_bytes=56 * 1024 * 1024
        ),
        cost_estimate=pl.CostEstimate(
            flops=2 * holders * own_rows * features * joined,
            bytes_accessed=features * features * 6,
            transcendentals=0,
        ),
    )(pages, freqs, tokens, gain.reshape(1, features), w_query, w_keyval, w_out, w_head)


def expander(features, head_width):
    head = lax.broadcasted_iota(jnp.int32, (128, features), 0)
    column = lax.broadcasted_iota(jnp.int32, (128, features), 1)
    return jnp.where(column // head_width == head, 1.0, 0.0).astype(jnp.bfloat16)


def join_parts(parts, spread, features, head_count):
    levels = []
    for part in parts:
        coded = part[:, features:].astype(jnp.float32)
        levels.append(
            coded
            + pltpu.roll(coded, 128 - head_count, 1)
            + pltpu.roll(coded, 128 - 2 * head_count, 1)
        )
    top = functools.reduce(jnp.maximum, levels)
    shares = [jnp.exp(level - top) for level in levels]
    total = functools.reduce(jnp.add, shares)
    joined = None
    for part, share in zip(parts, shares):
        share = share / total
        high = share.astype(jnp.bfloat16)
        low = (share - high.astype(jnp.float32)).astype(jnp.bfloat16)
        wide = jnp.dot(high, spread, preferred_element_type=jnp.float32) + jnp.dot(
            low, spread, preferred_element_type=jnp.float32
        )
        term = part[:, :features].astype(jnp.float32) * wide
        joined = term if joined is None else joined + term
    return joined, top + jnp.log(total)


def close_kernel(
    parts_ref, tokens_ref, gain_ref, wo_ref, wh_ref,
    hidden_ref, logits_ref, stats_out,
    near_buf, send_buf, far_buf, stat_buf, spread_ref,
    near_send, near_recv, far_send, far_recv, stat_send, stat_recv,
    *, head_count, request_count,
):
    planes, _, own_rows, coded = parts_ref.shape
    holders = 2 * planes
    features = coded - 128
    me = lax.axis_index("pg")
    zz, yy = me // 2, me % 2
    other = 1 - yy
    near_place = {"pg": 2 * zz + other}
    arrived = greet([{"pg": (me + step) % holders} for step in range(1, holders)])
    spread_ref[...] = expander(features, features // head_count)
    arrived()
    order = list(range(1, planes)) + [0]
    started = []

    def near_copy(depth, step):
        return remote(
            parts_ref.at[depth, other], near_buf.at[depth], near_send.at[step],
            near_recv.at[depth], near_place,
        )

    for step in order:
        copy = near_copy((zz + step) % planes, step)
        copy.start()
        started.append(copy)
    lane = lax.broadcasted_iota(jnp.int32, (own_rows, 128), 1)
    for step in order:
        depth = (zz + step) % planes
        near_copy(depth, step).wait_recv()
        joined, level = join_parts(
            [parts_ref[depth, yy], near_buf[depth]], spread_ref[...], features, head_count
        )
        level = jnp.where(lane < head_count, level, 0.0)
        high = level.astype(jnp.bfloat16).astype(jnp.float32)
        middle = (level - high).astype(jnp.bfloat16).astype(jnp.float32)
        low = level - high - middle
        code = high + pltpu.roll(middle, head_count, 1) + pltpu.roll(low, 2 * head_count, 1)
        if step == 0:
            far_buf[zz, :, :features] = joined.astype(jnp.bfloat16)
            far_buf[zz, :, features:] = code.astype(jnp.bfloat16)
        else:
            send_buf[step, :, :features] = joined.astype(jnp.bfloat16)
            send_buf[step, :, features:] = code.astype(jnp.bfloat16)
            copy = remote(
                send_buf.at[step], far_buf.at[zz], far_send.at[step], far_recv.at[zz],
                {"pg": 2 * depth + yy},
            )
            copy.start()
            started.append(copy)
    for step in range(1, planes):
        depth = (zz + step) % planes
        remote(
            send_buf.at[step], far_buf.at[depth], far_send.at[step], far_recv.at[depth], near_place
        ).wait_recv()
    joined, _ = join_parts(
        [far_buf[depth] for depth in range(planes)], spread_ref[...], features, head_count
    )
    attention = joined.astype(jnp.bfloat16)
    hidden = (
        tokens_ref[...].astype(jnp.float32)
        + jnp.dot(attention, wo_ref[...], preferred_element_type=jnp.float32)
    ).astype(jnp.bfloat16)
    hidden_ref[...] = hidden
    wide = hidden.astype(jnp.float32)
    squares = wide * wide
    power = jnp.mean(squares, axis=-1, keepdims=True)
    head_in = (wide * lax.rsqrt(power + EPSILON) * gain_ref[...]).astype(jnp.bfloat16)
    logits = jnp.dot(head_in, wh_ref[...], preferred_element_type=jnp.float32)
    logits_ref[...] = logits.astype(jnp.bfloat16)
    energy = jnp.sum(jnp.sum(squares, axis=1, keepdims=True), axis=0, keepdims=True)
    peak = jnp.max(jnp.max(logits, axis=1, keepdims=True), axis=0, keepdims=True)
    is_first = lax.broadcasted_iota(jnp.int32, (8, 128), 0) == 0
    stat_buf[me] = jnp.where(
        is_first, jnp.broadcast_to(energy, (8, 128)), jnp.broadcast_to(peak, (8, 128))
    )
    for step in range(1, holders):
        copy = remote(
            stat_buf.at[me], stat_buf.at[me], stat_send.at[step], stat_recv.at[me],
            {"pg": (me + step) % holders},
        )
        copy.start()
        started.append(copy)
    for step in range(1, holders):
        source = (me + step) % holders
        remote(
            stat_buf.at[source], stat_buf.at[source], stat_send.at[step], stat_recv.at[source],
            near_place,
        ).wait_recv()
    every = holders // request_count
    for request in range(request_count):
        mine = [stat_buf[every * request + block] for block in range(every)]
        total = functools.reduce(jnp.add, mine)
        top = functools.reduce(jnp.maximum, mine)
        stats_out[request] = jnp.where(is_first, jnp.sqrt(total), top)
    for copy in started:
        copy.wait_send()


def close(parts, tokens, gain, wo, wh, head_count, request_count, holders):
    own_rows, features = tokens.shape
    planes = holders // 2
    coded = features + 128
    vmem = pl.BlockSpec(memory_space=pltpu.VMEM)
    bf16 = jnp.bfloat16
    dma = pltpu.SemaphoreType.DMA
    return pl.pallas_call(
        functools.partial(close_kernel, head_count=head_count, request_count=request_count),
        out_shape=(
            jax.ShapeDtypeStruct((own_rows, features), bf16),
            jax.ShapeDtypeStruct((own_rows, wh.shape[1]), bf16),
            jax.ShapeDtypeStruct((request_count, 8, 128), jnp.float32),
        ),
        in_specs=[vmem] * 5,
        out_specs=(vmem, vmem, vmem),
        scratch_shapes=[
            pltpu.VMEM((planes, own_rows, coded), bf16),
            pltpu.VMEM((planes, own_rows, coded), bf16),
            pltpu.VMEM((planes, own_rows, coded), bf16),
            pltpu.VMEM((holders, 8, 128), jnp.float32),
            pltpu.VMEM((128, features), bf16),
            dma((planes,)), dma((planes,)), dma((planes,)), dma((planes,)),
            dma((holders,)), dma((holders,)),
        ],
        compiler_params=pltpu.CompilerParams(
            collective_id=1, has_side_effects=True, vmem_limit_bytes=56 * 1024 * 1024
        ),
        cost_estimate=pl.CostEstimate(
            flops=2 * own_rows * features * features,
            bytes_accessed=features * features * 4,
            transcendentals=0,
        ),
    )(parts.reshape(planes, 2, own_rows, coded), tokens, gain.reshape(1, features), wo, wh)

def project_plain(tokens, cache_pages, attn_gain, w_query, w_keyval, w_out, w_head, group_rows, head_count):
    own_rows, features = tokens.shape
    request_count = cache_pages.shape[0]
    span_rows = group_rows // request_count
    head_width = features // head_count
    first_row = lax.axis_index("pg") * own_rows
    normed = rms_norm(tokens, attn_gain)
    query_full, keyval_full, out_full, head_full = (
        lax.all_gather(w_query, "req", axis=0, tiled=True),
        lax.all_gather(w_keyval, "req", axis=0, tiled=True),
        lax.all_gather(w_out, "req", axis=0, tiled=True),
        lax.all_gather(w_head, "req", axis=0, tiled=True),
    )
    own_index = first_row + jnp.arange(own_rows, dtype=jnp.int32)
    own_positions = (
        lookup_small(cache_pages, own_index // span_rows, request_count) * PAGE
        + own_index % span_rows
    )
    own_cos, own_sin = rope_angles(own_positions, head_width // 2)
    query_cols = query_full.shape[1]
    joined = jnp.concatenate([query_full, keyval_full], axis=1)
    projected = jnp.dot(
        normed, lax.all_gather(joined, "pg", axis=1, tiled=True), preferred_element_type=jnp.float32
    )
    projected = projected.reshape(own_rows, -1, joined.shape[1])
    query_raw = projected[:, :, :query_cols].reshape(own_rows, features).astype(jnp.bfloat16)
    keyval_raw = projected[:, :, query_cols:].reshape(own_rows, 2 * features).astype(jnp.bfloat16)
    own_queries = rotate(query_raw, own_cos, own_sin, head_count)
    new_keys = rotate(keyval_raw[:, :features], own_cos, own_sin, head_count)
    new_values = keyval_raw[:, features:]
    appended = jnp.concatenate([new_keys, new_values], axis=1)
    queries = lax.all_gather(own_queries, "pg", axis=0, tiled=True)
    queries = queries.reshape(group_rows, features // 128, 128).transpose(1, 0, 2)
    return (
        queries,
        appended,
        lax.all_gather(out_full, "pg", axis=1, tiled=True),
        lax.all_gather(head_full, "pg", axis=1, tiled=True),
    )


def per_device(
    tokens,
    variate_ids,
    cache_pages,
    page_table,
    kv_cache,
    cache_variates,
    attn_gain,
    w_query,
    w_keyval,
    w_out,
    variate_bias,
    head_gain,
    w_head,
):
    own_rows, features = tokens.shape
    request_count = cache_pages.shape[0]
    group_rows = variate_ids.shape[0]
    head_count = variate_bias.shape[1]
    holders = group_rows // own_rows
    half_width = features // head_count // 2
    req_count = features // w_query.shape[0]
    if w_query.shape[1] == 128 and w_keyval.shape[1] == 256:
        steps = jnp.arange(half_width, dtype=jnp.float32) / half_width
        freqs = jnp.exp(-math.log(10000.0) * steps).reshape(half_width, 1)
        queries, appended, out_whole, head_whole = project(
            cache_pages, freqs, tokens, attn_gain, w_query, w_keyval, w_out, w_head, holders, req_count
        )
        queries = queries.reshape(holders, group_rows, 128)
        out_whole = out_whole.reshape(features, features)
    else:
        queries, appended, out_whole, head_whole = project_plain(
            tokens, cache_pages, attn_gain, w_query, w_keyval, w_out, w_head, group_rows, head_count
        )
    partial_out = attend(
        cache_pages, page_table, variate_bias, queries, variate_ids, appended, cache_variates, kv_cache
    )
    hidden, logits, stats = close(
        partial_out, tokens, head_gain, out_whole, head_whole, head_count, request_count, holders
    )
    return (hidden, appended, logits, stats[:, 0, 0], stats[:, 1, 0])


def solution(mesh):
    placed = (
        P(("req", "pg"), None),
        P("req"),
        P("req"),
        P("req", None),
        P(("req", "pg"), None, None),
        P(("req", "pg"), None),
        P(),
        P("req", "pg"),
        P("req", "pg"),
        P("req", "pg"),
        P(),
        P(),
        P("req", "pg"),
    )
    return jax.shard_map(
        per_device,
        mesh=mesh,
        in_specs=placed,
        out_specs=(
            P(("req", "pg"), None),
            P(("req", "pg"), None),
            P(("req", "pg"), None),
            P("req"),
            P("req"),
        ),
        check_vma=False,
    )
```

```python
import functools
import math

import jax
import jax.numpy as jnp
from jax import lax
from jax.experimental import pallas as pl
from jax.experimental.pallas import tpu as pltpu
from jax.sharding import PartitionSpec as P

PAGE = 128


EPSILON = 1e-05
NEGATIVE = -1e30


def rms_norm(values, gain):
    wide = values.astype(jnp.float32)
    power = jnp.mean(wide * wide, axis=-1, keepdims=True)
    return (wide * lax.rsqrt(power + EPSILON) * gain).astype(jnp.bfloat16)


def rope_angles(positions, half_width):
    steps = jnp.arange(half_width, dtype=jnp.float32) / half_width
    freqs = jnp.exp(-math.log(10000.0) * steps)
    angle = positions.astype(jnp.float32)[:, None] * freqs[None, :]
    return (jnp.cos(angle), jnp.sin(angle))


def rotate(values, cosine, sine_part, head_count):
    count = values.shape[0]
    halves = values.astype(jnp.float32).reshape(count, head_count, 2, -1)
    front_half = halves[:, :, 0, :]
    second = halves[:, :, 1, :]
    cosine_wide = cosine[:, None, :]
    sine_wide = sine_part[:, None, :]
    turned = jnp.stack(
        [
            front_half * cosine_wide - second * sine_wide,
            second * cosine_wide + front_half * sine_wide,
        ],
        axis=2,
    )
    return turned.reshape(count, -1).astype(jnp.bfloat16)


def lookup_small(table_rows, lookup_index, count):
    matches = lookup_index[:, None] == jnp.arange(count, dtype=jnp.int32)[None, :]
    return jnp.sum(jnp.where(matches, table_rows[None, :], 0), axis=1)


def attend_kernel(
    pages_ref, table_ref, bias_ref, q_ref, ids_ref, new_ref, cids_ref, kv_hbm,
    out_ref, app_ref, kv_buf, vt_buf, acc_ref, peak_ref, sum_ref, same_ref, owner_ref, sems,
):
    request_count, _, span = ids_ref.shape
    slot_count, page_rows, _ = kv_hbm.shape
    pairs = q_ref.shape[0]
    features = 128 * pairs
    own_rows = new_ref.shape[0]
    me = lax.axis_index("pg")

    def fetch(slot):
        return pltpu.make_async_copy(kv_hbm.at[slot], kv_buf.at[slot], sems.at[slot])

    for slot in range(slot_count):
        fetch(slot).start()

    app_ref[...] = new_ref[...]
    for slot in range(slot_count):
        owner_ref[slot] = -1

    for request in range(request_count):

        def look(page, _):
            slot = table_ref[request, page] - me * slot_count

            @pl.when((slot >= 0) & (slot < slot_count))
            def _():
                owner_ref[slot] = request

            return 0

        lax.fori_loop(0, pages_ref[request], look, 0)

    acc_ref[...] = jnp.zeros_like(acc_ref)
    sum_ref[...] = jnp.zeros_like(sum_ref)
    peak_ref[...] = jnp.full_like(peak_ref, NEGATIVE)

    def absorb(request, k_of, v_of, key_ids, count, offset):
        lane = lax.broadcasted_iota(jnp.int32, (count, 128), 1)
        left = jnp.where(lane < 64, 1.0, 0.0).astype(jnp.bfloat16)
        right = jnp.where(lane < 64, 0.0, 1.0).astype(jnp.bfloat16)
        row = lax.broadcasted_iota(jnp.int32, (128, count), 0)
        ones_row = lax.broadcasted_iota(jnp.int32, (16, 2 * count), 0)
        ones_col = lax.broadcasted_iota(jnp.int32, (16, 2 * count), 1)
        ones = jnp.where((ones_row < 8) == (ones_col < count), 1.0, 0.0).astype(jnp.bfloat16)
        for pair in range(pairs):
            value = v_of(pair).astype(jnp.float32).T
            vt_buf[pair, :128, 0:count] = jnp.where(row < 64, value, 0.0).astype(jnp.bfloat16)
            vt_buf[pair, :128, count : 2 * count] = jnp.where(row >= 64, value, 0.0).astype(
                jnp.bfloat16
            )
            vt_buf[pair, 128:, 0 : 2 * count] = ones

        def tile(index, _):
            start = pl.multiple_of(index * 256, 256)
            query_ids = ids_ref[request, :, pl.ds(start, 256)]
            same = jnp.broadcast_to(query_ids, (count, 256)) == jnp.concatenate(
                [key_ids, key_ids], axis=1
            )
            same_ref[:count] = jnp.where(same, 1.0, 0.0)
            if offset is not None:
                allowed = (
                    lax.broadcasted_iota(jnp.int32, (count, 256), 0) + offset
                    <= lax.broadcasted_iota(jnp.int32, (count, 256), 1) + start
                )
            for pair in range(pairs):
                keys = k_of(pair)
                both = jnp.concatenate([keys * left, keys * right], axis=0)
                query = q_ref[pair, pl.ds(request * span + start, 256), :]
                scores = lax.dot_general(
                    both, query, (((1,), (1,)), ((), ())), preferred_element_type=jnp.float32
                )
                weights, fades = [], []
                for side in range(2):
                    head = 2 * pair + side
                    part = scores[side * count : (side + 1) * count] * 0.125
                    part = part + jnp.where(
                        same_ref[:count] > 0.5, bias_ref[0, head], bias_ref[1, head]
                    )
                    if offset is not None:
                        part = jnp.where(allowed, part, NEGATIVE)
                    old = peak_ref[request, head : head + 1, pl.ds(start, 256)]
                    new = jnp.maximum(old, jnp.max(part, axis=0, keepdims=True))
                    peak_ref[request, head : head + 1, pl.ds(start, 256)] = new
                    weight = jnp.exp(part - new)
                    if offset is not None:
                        weight = jnp.where(allowed, weight, 0.0)
                    weights.append(weight.astype(jnp.bfloat16))
                    fades.append(jnp.exp(old - new))
                summed = jnp.dot(
                    vt_buf[pair, :, 0 : 2 * count],
                    jnp.concatenate(weights, axis=0),
                    preferred_element_type=jnp.float32,
                )
                for side in range(2):
                    head = 2 * pair + side
                    rows = slice(128 * pair + 64 * side, 128 * pair + 64 * side + 64)
                    acc_ref[request, rows, pl.ds(start, 256)] = (
                        acc_ref[request, rows, pl.ds(start, 256)] * fades[side]
                        + summed[64 * side : 64 * side + 64]
                    )
                    sum_ref[request, head : head + 1, pl.ds(start, 256)] = (
                        sum_ref[request, head : head + 1, pl.ds(start, 256)] * fades[side]
                        + summed[128 + 8 * side : 129 + 8 * side]
                    )
            return 0

        lax.fori_loop(0, span // 256, tile, 0)

    first_row = me * own_rows
    request_own = first_row // span
    offset = first_row % span
    chunk = pl.multiple_of((offset // 128) * 128, 128)
    wide_ids = ids_ref[request_own, :, pl.ds(chunk, 128)]
    column = jnp.broadcast_to(wide_ids, (128, 128)).T
    lower = offset - chunk
    own_ids = jnp.where(lower == 0, column[:own_rows], column[128 - own_rows :])
    absorb(
        request_own,
        lambda pair: new_ref[:, 128 * pair : 128 * pair + 128],
        lambda pair: new_ref[:, features + 128 * pair : features + 128 * pair + 128],
        own_ids,
        own_rows,
        offset,
    )

    def visit(slot, _):
        owner = owner_ref[slot]
        fetch(slot).wait()

        @pl.when(owner >= 0)
        def _():
            column = jnp.broadcast_to(cids_ref[pl.ds(slot, 1), :], (page_rows, 128)).T
            absorb(
                owner,
                lambda pair: kv_buf[slot, :, 128 * pair : 128 * pair + 128],
                lambda pair: kv_buf[slot, :, features + 128 * pair : features + 128 * pair + 128],
                column,
                page_rows,
                None,
            )

        return 0

    lax.fori_loop(0, slot_count, visit, 0)

    def close(flat, _):
        request = flat // (span // 256)
        start = pl.multiple_of((flat % (span // 256)) * 256, 256)
        place = pl.ds(pl.multiple_of(flat * 256, 256), 256)
        total = sum_ref[request, :, pl.ds(start, 256)]
        live = total > 0
        safe = jnp.where(live, total, 1.0)
        level = jnp.where(live, peak_ref[request, :, pl.ds(start, 256)] + jnp.log(safe), NEGATIVE)
        inverse = jnp.where(live, 1.0 / safe, 0.0)
        for pair in range(pairs):
            block = jnp.concatenate(
                [
                    acc_ref[request, 128 * pair + 64 * side : 128 * pair + 64 * side + 64, pl.ds(start, 256)]
                    * inverse[2 * pair + side : 2 * pair + side + 1]
                    for side in range(2)
                ],
                axis=0,
            )
            out_ref[place, 128 * pair : 128 * pair + 128] = block.T.astype(jnp.bfloat16)
        high = level.astype(jnp.bfloat16).astype(jnp.float32)
        middle = (level - high).astype(jnp.bfloat16).astype(jnp.float32)
        low = level - high - middle
        heads = level.shape[0]
        filler = jnp.zeros((128 - 3 * heads, 256), jnp.float32)
        stacked = jnp.concatenate([high, middle, low, filler], axis=0)
        out_ref[place, features : features + 128] = stacked.T.astype(jnp.bfloat16)
        return 0

    lax.fori_loop(0, request_count * (span // 256), close, 0)


def attend(pages, table, bias, queries, ids, new_pairs, cache_ids, kv_cache):
    request_count = pages.shape[0]
    pairs, rows, _ = queries.shape
    features = 128 * pairs
    span = rows // request_count
    slot_count, page_rows, _ = kv_cache.shape
    heads = bias.shape[1]
    smem = pl.BlockSpec(memory_space=pltpu.SMEM)
    vmem = pl.BlockSpec(memory_space=pltpu.VMEM)
    return pl.pallas_call(
        attend_kernel,
        out_shape=(
            jax.ShapeDtypeStruct((rows, features + 128), jnp.bfloat16),
            jax.ShapeDtypeStruct(new_pairs.shape, jnp.bfloat16),
        ),
        in_specs=[smem, smem, smem, vmem, vmem, vmem, vmem, pl.BlockSpec(memory_space=pl.ANY)],
        out_specs=(vmem, vmem),
        scratch_shapes=[
            pltpu.VMEM(kv_cache.shape, jnp.bfloat16),
            pltpu.VMEM((features // 128, 144, 2 * page_rows), jnp.bfloat16),
            pltpu.VMEM((request_count, features, span), jnp.float32),
            pltpu.VMEM((request_count, heads, span), jnp.float32),
            pltpu.VMEM((request_count, heads, span), jnp.float32),
            pltpu.VMEM((page_rows, 256), jnp.float32),
            pltpu.SMEM((slot_count,), jnp.int32),
            pltpu.SemaphoreType.DMA((slot_count,)),
        ],
        compiler_params=pltpu.CompilerParams(vmem_limit_bytes=56 * 1024 * 1024),
        cost_estimate=pl.CostEstimate(
            flops=4 * slot_count * page_rows * span * features * 4,
            bytes_accessed=kv_cache.size * 2 + rows * features * 4,
            transcendentals=slot_count * page_rows * span * heads,
        ),
    )(pages, table, bias, queries, ids.reshape(request_count, 1, span), new_pairs, cache_ids, kv_cache)


def remote(source, target, send_sem, recv_sem, where):
    return pltpu.make_async_remote_copy(
        src_ref=source,
        dst_ref=target,
        send_sem=send_sem,
        recv_sem=recv_sem,
        device_id=where,
        device_id_type=pl.DeviceIdType.MESH,
    )


def greet(places):
    barrier = pltpu.get_barrier_semaphore()
    for place in places:
        pl.semaphore_signal(barrier, inc=1, device_id=place, device_id_type=pl.DeviceIdType.MESH)
    return lambda: pl.semaphore_wait(barrier, len(places))


def project_kernel(
    pages_ref, freq_ref, tokens_ref, gain_ref, wq_ref, wkv_ref, wo_ref, wh_ref,
    q_out, app_out, wo_out, wh_out,
    tok, wkv, wq, kv_stage, wh_all, cos_ref, sin_ref,
    tok_far, tok_near, tok_recv,
    w_far, w_near, w_recv,
    wq_far, wq_near, wq_recv, wqx_send, wqx_recv, wqc_send, wqc_recv,
    wo_far, wo_near, wo_recv,
    wh_far, wh_near, wh_recv,
    kv_send, kv_recv, local_sem,
):
    _, planes, own_rows, features = tok.shape
    holders = 2 * planes
    req_count, deep, joined = wkv.shape
    req_pairs = req_count // 2
    request_count = pages_ref.shape[0]
    rows = holders * own_rows
    span = rows // request_count
    me = lax.axis_index("pg")
    mine = lax.axis_index("req")
    zz, yy = me // 2, me % 2
    other = 1 - yy
    xx, cc = mine // 2, mine % 2
    core_place = {"req": 2 * xx + 1 - cc}
    near_place = {"pg": 2 * zz + other}

    def plane(step):
        return (zz + step) % planes

    def far_place(step):
        return {"pg": 2 * plane(step) + yy}

    def req_far(step):
        return (xx + step) % req_pairs

    def x_place(step):
        return {"req": 2 * req_far(step) + cc}

    places = [{"pg": (me + step) % holders} for step in range(1, holders)]
    places += [x_place(step) for step in range(1, req_pairs)] + [core_place]
    arrived = greet(places)

    def columns(holder):
        return pl.ds(pl.multiple_of(holder * 128, 128), 128)

    keeps = [
        pltpu.make_async_copy(wq_ref, wq.at[xx, cc, :, columns(me)], local_sem.at[0]),
        pltpu.make_async_copy(wo_ref, wo_out.at[:, columns(me)], local_sem.at[1]),
    ]
    for keep in keeps:
        keep.start()

    wide = tokens_ref[...].astype(jnp.float32)
    power = jnp.mean(wide * wide, axis=-1, keepdims=True)
    tok[yy, zz] = (wide * lax.rsqrt(power + EPSILON) * gain_ref[...]).astype(jnp.bfloat16)
    wkv[mine] = wkv_ref[...]
    head_cols = wh_ref.shape[1]
    packs = 128 // head_cols
    slab = deep // packs
    wh_wide = wh_ref[...].astype(jnp.float32)
    wh_all[me] = jnp.concatenate(
        [wh_wide[slab * pack : slab * pack + slab] for pack in range(packs)], axis=1
    ).astype(jnp.bfloat16)
    for keep in keeps:
        keep.wait()
    arrived()

    started = []

    def begin(copy):
        copy.start()
        started.append(copy)

    def wq_copy(holder, send_sem, place):
        part = wq.at[xx, cc, :, columns(holder)]
        return remote(part, part, send_sem, wq_recv.at[holder], place)

    def wq_over(depth, holder, step, place):
        part = wq.at[depth, cc, :, columns(holder)]
        return remote(part, part, wqx_send.at[step, holder], wqx_recv.at[depth, holder], place)

    def wq_pass(side, holder):
        part = wq.at[:, side, :, columns(holder)]
        return remote(part, part, wqc_send.at[holder], wqc_recv.at[holder], core_place)

    def spread_x(holder):
        for step in range(1, req_pairs):
            begin(wq_over(xx, holder, step, x_place(step)))

    def pass_core(holder):
        for step in range(1, req_pairs):
            wq_over(req_far(step), holder, step, core_place).wait_recv()
        begin(wq_pass(cc, holder))

    def tok_copy(side, depth, send_sem, place):
        return remote(
            tok.at[side, depth], tok.at[side, depth], send_sem, tok_recv.at[side, depth], place
        )

    def w_copy(block, send_sem, place):
        return remote(wkv.at[block], wkv.at[block], send_sem, w_recv.at[block], place)

    for step in range(1, planes):
        begin(wq_copy(me, wq_far.at[step], far_place(step)))
        begin(tok_copy(yy, zz, tok_far.at[step], far_place(step)))
    begin(wq_copy(me, wq_near.at[0], near_place))
    begin(tok_copy(yy, zz, tok_near.at[0], near_place))
    for step in range(1, req_pairs):
        begin(w_copy(mine, w_far.at[step], x_place(step)))
    begin(w_copy(mine, w_near.at[0], core_place))
    spread_x(me)

    row = lax.broadcasted_iota(jnp.int32, (1, rows), 1)
    held = jnp.zeros((1, rows), jnp.int32)
    for request in range(request_count):
        held = jnp.where(row // span == request, pages_ref[request], held)
    position = (held * PAGE + row % span).astype(jnp.float32)
    angle = freq_ref[...] * position
    cosine, sine = jnp.cos(angle), jnp.sin(angle)
    cos_ref[...] = jnp.concatenate([cosine] * 4, axis=0).T.reshape(cos_ref.shape)
    sin_ref[...] = jnp.concatenate([-sine, sine, -sine, sine], axis=0).T.reshape(sin_ref.shape)

    for step in range(1, req_pairs):
        block = 2 * req_far(step) + cc
        w_copy(block, w_far.at[step], core_place).wait_recv()
        begin(w_copy(block, w_near.at[step], core_place))
    for step in range(1, planes):
        holder = 2 * plane(step) + yy
        wq_copy(holder, wq_far.at[step], near_place).wait_recv()
        begin(wq_copy(holder, wq_near.at[step], near_place))
        spread_x(holder)
        tok_copy(yy, plane(step), tok_far.at[step], near_place).wait_recv()
        begin(tok_copy(yy, plane(step), tok_near.at[step], near_place))

    def wo_copy(holder, send_sem, place):
        part = wo_out.at[:, columns(holder)]
        return remote(part, part, send_sem, wo_recv.at[holder], place)

    def wh_copy(holder, send_sem, place):
        return remote(wh_all.at[holder], wh_all.at[holder], send_sem, wh_recv.at[holder], place)

    for step in range(1, planes):
        begin(wo_copy(me, wo_far.at[step], far_place(step)))
        begin(wh_copy(me, wh_far.at[step], far_place(step)))
    begin(wo_copy(me, wo_near.at[0], near_place))
    begin(wh_copy(me, wh_near.at[0], near_place))

    for step in range(req_pairs):
        block = 2 * req_far(step) + 1 - cc
        w_copy(block, w_near.at[step], core_place).wait_recv()

    def kv_copy(source, side, depth, send_sem, place):
        start = pl.multiple_of(source * 256, 256)
        return remote(
            kv_stage.at[depth, side], app_out.at[:, pl.ds(start, 256)], send_sem,
            kv_recv.at[source], place,
        )

    half_rows = planes * own_rows
    lane = lax.broadcasted_iota(jnp.int32, (half_rows, 128), 1)
    front = (lane % 64) < 32
    is_key = (jnp.zeros((half_rows, 128), jnp.int32) + me) < planes

    def turned(value, cosine, sine):
        value = value.astype(jnp.bfloat16).astype(jnp.float32)
        swapped = jnp.where(front, pltpu.roll(value, 96, 1), pltpu.roll(value, 32, 1))
        return (value * cosine + swapped * sine).astype(jnp.bfloat16)

    def half(turn):
        side = yy if turn == 0 else other
        made = jnp.dot(
            tok[side].reshape(half_rows, features),
            wkv[...].reshape(features, joined),
            preferred_element_type=jnp.float32,
        )
        key_cos = jnp.where(is_key, cos_ref[:, side].reshape(half_rows, 128), 1.0)
        key_sin = jnp.where(is_key, sin_ref[:, side].reshape(half_rows, 128), 0.0)
        for part in range(joined // 128):
            piece = turned(made[:, 128 * part : 128 * part + 128], key_cos, key_sin)
            kv_stage[:, side, :, 128 * part : 128 * part + 128] = piece.reshape(
                planes, own_rows, 128
            )
        for step in range(0 if turn == 1 else 1, planes):
            place = {"pg": 2 * plane(step) + side}
            begin(kv_copy(me, side, plane(step), kv_send.at[turn, step], place))

    half(0)
    own_keep = pltpu.make_async_copy(
        kv_stage.at[zz, yy],
        app_out.at[:, pl.ds(pl.multiple_of(me * 256, 256), 256)],
        local_sem.at[2],
    )
    own_keep.start()
    for step in range(planes):
        holder = 2 * plane(step) + other
        wq_copy(holder, wq_near.at[step], near_place).wait_recv()
        spread_x(holder)
    for step in range(planes):
        pass_core(2 * plane(step) + yy)
    for step in range(planes):
        tok_copy(other, plane(step), tok_near.at[step], near_place).wait_recv()
    half(1)
    for step in range(1, planes):
        holder = 2 * plane(step) + yy
        wh_copy(holder, wh_far.at[step], near_place).wait_recv()
        begin(wh_copy(holder, wh_near.at[step], near_place))
        wo_copy(holder, wo_far.at[step], near_place).wait_recv()
        begin(wo_copy(holder, wo_near.at[step], near_place))
    for step in range(planes):
        pass_core(2 * plane(step) + other)

    for step in range(planes):
        depth = plane(step)
        for side in range(2):
            wq_pass(1 - cc, 2 * depth + side).wait_recv()
        start = pl.multiple_of(depth * 256, 256)
        weight = wq[:, :, :, pl.ds(start, 256)].reshape(features, 256)
        for side in range(2):
            made = jnp.dot(
                tok[side].reshape(half_rows, features), weight, preferred_element_type=jnp.float32
            )
            cosine = cos_ref[:, side].reshape(half_rows, 128)
            sine = sin_ref[:, side].reshape(half_rows, 128)
            for part in range(2):
                piece = turned(made[:, 128 * part : 128 * part + 128], cosine, sine)
                q_out[2 * depth + part, :, side] = piece.reshape(planes, own_rows, 128)

    for step in range(planes):
        wh_copy(2 * plane(step) + other, wh_near.at[step], near_place).wait_recv()
    for pack in range(packs):
        wh_out[slab * pack : slab * pack + slab, :] = jnp.concatenate(
            [
                wh_all[holder].astype(jnp.float32)[:, head_cols * pack : head_cols * pack + head_cols]
                for holder in range(holders)
            ],
            axis=1,
        ).astype(jnp.bfloat16)
    for step in range(1, holders):
        kv_copy((me + step) % holders, yy, zz, kv_send.at[0, 0], near_place).wait_recv()
    own_keep.wait()
    for step in range(planes):
        wo_copy(2 * plane(step) + other, wo_near.at[step], near_place).wait_recv()
    for copy in started:
        copy.wait_send()


def project(pages, freqs, tokens, gain, w_query, w_keyval, w_out, w_head, holders, req_count):
    own_rows, features = tokens.shape
    planes = holders // 2
    deep = w_query.shape[0]
    vmem = pl.BlockSpec(memory_space=pltpu.VMEM)
    bf16 = jnp.bfloat16
    dma = pltpu.SemaphoreType.DMA
    pairs = req_count // 2
    return pl.pallas_call(
        project_kernel,
        out_shape=(
            jax.ShapeDtypeStruct((holders, planes, 2, own_rows, 128), bf16),
            jax.ShapeDtypeStruct((own_rows, 2 * features), bf16),
            jax.ShapeDtypeStruct((deep, features), bf16),
            jax.ShapeDtypeStruct((deep, holders * w_head.shape[1]), bf16),
        ),
        in_specs=[pl.BlockSpec(memory_space=pltpu.SMEM)] + [vmem] * 7,
        out_specs=(vmem, vmem, vmem, vmem),
        scratch_shapes=[
            pltpu.VMEM((2, planes, own_rows, features), bf16),
            pltpu.VMEM((req_count, deep, w_keyval.shape[1]), bf16),
            pltpu.VMEM((pairs, 2, deep, features), bf16),
            pltpu.VMEM((planes, 2, own_rows, 256), bf16),
            pltpu.VMEM((holders, deep * w_head.shape[1] // 128, 128), bf16),
            pltpu.VMEM((planes, 2, own_rows, 128), jnp.float32),
            pltpu.VMEM((planes, 2, own_rows, 128), jnp.float32),
            dma((planes,)), dma((planes,)), dma((2, planes)),
            dma((pairs,)), dma((pairs,)), dma((req_count,)),
            dma((planes,)), dma((planes,)), dma((holders,)),
            dma((pairs, holders)), dma((pairs, holders)), dma((holders,)), dma((holders,)),
            dma((planes,)), dma((planes,)), dma((holders,)),
            dma((planes,)), dma((planes,)), dma((holders,)),
            dma((2, planes)), dma((holders,)), dma((3,)),
        ],
        compiler_params=pltpu.CompilerParams(
            collective_id=0, has_side_effects=True, vmem_limit_bytes=56 * 1024 * 1024
        ),
        cost_estimate=pl.CostEstimate(
            flops=2 * holders * own_rows * features * (features + w_keyval.shape[1]),
            bytes_accessed=features * features * 6,
            transcendentals=0,
        ),
    )(pages, freqs, tokens, gain.reshape(1, features), w_query, w_keyval, w_out, w_head)


def expander(features, head_width):
    head = lax.broadcasted_iota(jnp.int32, (128, features), 0)
    column = lax.broadcasted_iota(jnp.int32, (128, features), 1)
    return jnp.where(column // head_width == head, 1.0, 0.0).astype(jnp.bfloat16)


def join_parts(parts, spread, features, head_count):
    levels = []
    for part in parts:
        coded = part[:, features:].astype(jnp.float32)
        levels.append(
            coded
            + pltpu.roll(coded, 128 - head_count, 1)
            + pltpu.roll(coded, 128 - 2 * head_count, 1)
        )
    top = functools.reduce(jnp.maximum, levels)
    shares = [jnp.exp(level - top) for level in levels]
    total = functools.reduce(jnp.add, shares)
    joined = None
    for part, share in zip(parts, shares):
        share = share / total
        high = share.astype(jnp.bfloat16)
        low = (share - high.astype(jnp.float32)).astype(jnp.bfloat16)
        wide = jnp.dot(high, spread, preferred_element_type=jnp.float32) + jnp.dot(
            low, spread, preferred_element_type=jnp.float32
        )
        term = part[:, :features].astype(jnp.float32) * wide
        joined = term if joined is None else joined + term
    return joined, top + jnp.log(total)


def close_kernel(
    parts_ref, tokens_ref, gain_ref, wo_ref, wh_ref,
    hidden_ref, logits_ref, stats_out,
    near_buf, send_buf, far_buf, stat_buf, spread_ref, wo_all, wh_all,
    wo_far, wo_near, wo_recv, wh_far, wh_near, wh_recv,
    near_send, near_recv, far_send, far_recv, stat_send, stat_recv,
    *, head_count, request_count,
):
    planes, _, own_rows, coded = parts_ref.shape
    holders = 2 * planes
    features = coded - 128
    me = lax.axis_index("pg")
    zz, yy = me // 2, me % 2
    other = 1 - yy
    near_place = {"pg": 2 * zz + other}
    req_pairs, _, deep, _ = wo_all.shape
    mine = lax.axis_index("req")
    xx, cc = mine // 2, mine % 2
    core_place = {"req": 2 * xx + 1 - cc}

    def req_far(step):
        return (xx + step) % req_pairs

    arrived = greet(
        [{"pg": (me + step) % holders} for step in range(1, holders)]
        + [{"req": 2 * req_far(step) + cc} for step in range(1, req_pairs)]
        + [core_place]
    )
    wo_all[xx, cc] = wo_ref[...]
    wh_all[xx, cc] = wh_ref[...]
    spread_ref[...] = expander(features, features // head_count)
    arrived()
    order = list(range(1, planes)) + [0]
    started = []

    def near_copy(depth, step):
        return remote(
            parts_ref.at[depth, other], near_buf.at[depth], near_send.at[step],
            near_recv.at[depth], near_place,
        )

    for step in order:
        copy = near_copy((zz + step) % planes, step)
        copy.start()
        started.append(copy)

    def wo_copy(depth, side, send_sem, place):
        part = wo_all.at[depth, side]
        return remote(part, part, send_sem, wo_recv.at[depth, side], place)

    def wh_copy(depth, side, send_sem, place):
        part = wh_all.at[depth, side]
        return remote(part, part, send_sem, wh_recv.at[depth, side], place)

    for step in range(1, req_pairs):
        place = {"req": 2 * req_far(step) + cc}
        started += [wo_copy(xx, cc, wo_far.at[step], place), wh_copy(xx, cc, wh_far.at[step], place)]
    started += [
        wo_copy(xx, cc, wo_near.at[0], core_place), wh_copy(xx, cc, wh_near.at[0], core_place)
    ]
    for copy in started[planes:]:
        copy.start()
    lane = lax.broadcasted_iota(jnp.int32, (own_rows, 128), 1)
    for step in order:
        depth = (zz + step) % planes
        near_copy(depth, step).wait_recv()
        joined, level = join_parts(
            [parts_ref[depth, yy], near_buf[depth]], spread_ref[...], features, head_count
        )
        level = jnp.where(lane < head_count, level, 0.0)
        high = level.astype(jnp.bfloat16).astype(jnp.float32)
        middle = (level - high).astype(jnp.bfloat16).astype(jnp.float32)
        low = level - high - middle
        code = high + pltpu.roll(middle, head_count, 1) + pltpu.roll(low, 2 * head_count, 1)
        if step == 0:
            far_buf[zz, :, :features] = joined.astype(jnp.bfloat16)
            far_buf[zz, :, features:] = code.astype(jnp.bfloat16)
        else:
            send_buf[step, :, :features] = joined.astype(jnp.bfloat16)
            send_buf[step, :, features:] = code.astype(jnp.bfloat16)
            copy = remote(
                send_buf.at[step], far_buf.at[zz], far_send.at[step], far_recv.at[zz],
                {"pg": 2 * depth + yy},
            )
            copy.start()
            started.append(copy)
    for step in range(1, req_pairs):
        depth = req_far(step)
        wo_copy(depth, cc, wo_far.at[step], core_place).wait_recv()
        wh_copy(depth, cc, wh_far.at[step], core_place).wait_recv()
        for copy in (
            wo_copy(depth, cc, wo_near.at[step], core_place),
            wh_copy(depth, cc, wh_near.at[step], core_place),
        ):
            copy.start()
            started.append(copy)
    for step in range(1, planes):
        depth = (zz + step) % planes
        remote(
            send_buf.at[step], far_buf.at[depth], far_send.at[step], far_recv.at[depth], near_place
        ).wait_recv()
    joined, _ = join_parts(
        [far_buf[depth] for depth in range(planes)], spread_ref[...], features, head_count
    )
    attention = joined.astype(jnp.bfloat16)
    for step in range(req_pairs):
        wo_copy(req_far(step), 1 - cc, wo_near.at[step], core_place).wait_recv()
        wh_copy(req_far(step), 1 - cc, wh_near.at[step], core_place).wait_recv()
    out_weight = wo_all[...].reshape(features, features)
    head_weight = wh_all[...].reshape(features, wh_ref.shape[1])
    hidden = (
        tokens_ref[...].astype(jnp.float32)
        + jnp.dot(attention, out_weight, preferred_element_type=jnp.float32)
    ).astype(jnp.bfloat16)
    hidden_ref[...] = hidden
    wide = hidden.astype(jnp.float32)
    squares = wide * wide
    power = jnp.mean(squares, axis=-1, keepdims=True)
    head_in = (wide * lax.rsqrt(power + EPSILON) * gain_ref[...]).astype(jnp.bfloat16)
    logits = jnp.dot(head_in, head_weight, preferred_element_type=jnp.float32)
    logits_ref[...] = logits.astype(jnp.bfloat16)
    energy = jnp.sum(jnp.sum(squares, axis=1, keepdims=True), axis=0, keepdims=True)
    peak = jnp.max(jnp.max(logits, axis=1, keepdims=True), axis=0, keepdims=True)
    is_first = lax.broadcasted_iota(jnp.int32, (8, 128), 0) == 0
    stat_buf[me] = jnp.where(
        is_first, jnp.broadcast_to(energy, (8, 128)), jnp.broadcast_to(peak, (8, 128))
    )
    for step in range(1, holders):
        copy = remote(
            stat_buf.at[me], stat_buf.at[me], stat_send.at[step], stat_recv.at[me],
            {"pg": (me + step) % holders},
        )
        copy.start()
        started.append(copy)
    for step in range(1, holders):
        source = (me + step) % holders
        remote(
            stat_buf.at[source], stat_buf.at[source], stat_send.at[step], stat_recv.at[source],
            near_place,
        ).wait_recv()
    every = holders // request_count
    for request in range(request_count):
        mine = [stat_buf[every * request + block] for block in range(every)]
        total = functools.reduce(jnp.add, mine)
        top = functools.reduce(jnp.maximum, mine)
        stats_out[request] = jnp.where(is_first, jnp.sqrt(total), top)
    for copy in started:
        copy.wait_send()


def close(parts, tokens, gain, wo, wh, head_count, request_count, holders):
    own_rows, features = tokens.shape
    planes = holders // 2
    coded = features + 128
    pairs = features // wo.shape[0] // 2
    vmem = pl.BlockSpec(memory_space=pltpu.VMEM)
    bf16 = jnp.bfloat16
    dma = pltpu.SemaphoreType.DMA
    return pl.pallas_call(
        functools.partial(close_kernel, head_count=head_count, request_count=request_count),
        out_shape=(
            jax.ShapeDtypeStruct((own_rows, features), bf16),
            jax.ShapeDtypeStruct((own_rows, wh.shape[1]), bf16),
            jax.ShapeDtypeStruct((request_count, 8, 128), jnp.float32),
        ),
        in_specs=[vmem] * 5,
        out_specs=(vmem, vmem, vmem),
        scratch_shapes=[
            pltpu.VMEM((planes, own_rows, coded), bf16),
            pltpu.VMEM((planes, own_rows, coded), bf16),
            pltpu.VMEM((planes, own_rows, coded), bf16),
            pltpu.VMEM((holders, 8, 128), jnp.float32),
            pltpu.VMEM((128, features), bf16),
            pltpu.VMEM((pairs, 2) + wo.shape, bf16),
            pltpu.VMEM((pairs, 2) + wh.shape, bf16),
            dma((pairs,)), dma((pairs,)), dma((pairs, 2)),
            dma((pairs,)), dma((pairs,)), dma((pairs, 2)),
            dma((planes,)), dma((planes,)), dma((planes,)), dma((planes,)),
            dma((holders,)), dma((holders,)),
        ],
        compiler_params=pltpu.CompilerParams(
            collective_id=1, has_side_effects=True, vmem_limit_bytes=56 * 1024 * 1024
        ),
        cost_estimate=pl.CostEstimate(
            flops=2 * own_rows * features * features,
            bytes_accessed=features * features * 4,
            transcendentals=0,
        ),
    )(parts.reshape(planes, 2, own_rows, coded), tokens, gain.reshape(1, features), wo, wh)

def project_plain(tokens, cache_pages, attn_gain, w_query, w_keyval, w_out, w_head, group_rows, head_count):
    own_rows, features = tokens.shape
    request_count = cache_pages.shape[0]
    span_rows = group_rows // request_count
    head_width = features // head_count
    first_row = lax.axis_index("pg") * own_rows
    normed = rms_norm(tokens, attn_gain)
    query_full, keyval_full = (
        lax.all_gather(w_query, "req", axis=0, tiled=True),
        lax.all_gather(w_keyval, "req", axis=0, tiled=True),
    )
    own_index = first_row + jnp.arange(own_rows, dtype=jnp.int32)
    own_positions = (
        lookup_small(cache_pages, own_index // span_rows, request_count) * PAGE
        + own_index % span_rows
    )
    own_cos, own_sin = rope_angles(own_positions, head_width // 2)
    query_cols = query_full.shape[1]
    joined = jnp.concatenate([query_full, keyval_full], axis=1)
    projected = jnp.dot(
        normed, lax.all_gather(joined, "pg", axis=1, tiled=True), preferred_element_type=jnp.float32
    )
    projected = projected.reshape(own_rows, -1, joined.shape[1])
    query_raw = projected[:, :, :query_cols].reshape(own_rows, features).astype(jnp.bfloat16)
    keyval_raw = projected[:, :, query_cols:].reshape(own_rows, 2 * features).astype(jnp.bfloat16)
    own_queries = rotate(query_raw, own_cos, own_sin, head_count)
    new_keys = rotate(keyval_raw[:, :features], own_cos, own_sin, head_count)
    new_values = keyval_raw[:, features:]
    appended = jnp.concatenate([new_keys, new_values], axis=1)
    queries = lax.all_gather(own_queries, "pg", axis=0, tiled=True)
    queries = queries.reshape(group_rows, features // 128, 128).transpose(1, 0, 2)
    return (
        queries,
        appended,
        lax.all_gather(w_out, "pg", axis=1, tiled=True),
        lax.all_gather(w_head, "pg", axis=1, tiled=True),
    )


def per_device(
    tokens,
    variate_ids,
    cache_pages,
    page_table,
    kv_cache,
    cache_variates,
    attn_gain,
    w_query,
    w_keyval,
    w_out,
    variate_bias,
    head_gain,
    w_head,
):
    own_rows, features = tokens.shape
    request_count = cache_pages.shape[0]
    group_rows = variate_ids.shape[0]
    head_count = variate_bias.shape[1]
    holders = group_rows // own_rows
    half_width = features // head_count // 2
    req_count = features // w_query.shape[0]
    if w_query.shape[1] == 128 and w_keyval.shape[1] == 256:
        steps = jnp.arange(half_width, dtype=jnp.float32) / half_width
        freqs = jnp.exp(-math.log(10000.0) * steps).reshape(half_width, 1)
        queries, appended, out_rows, head_rows = project(
            cache_pages, freqs, tokens, attn_gain, w_query, w_keyval, w_out, w_head, holders, req_count
        )
        queries = queries.reshape(holders, group_rows, 128)
    else:
        queries, appended, out_rows, head_rows = project_plain(
            tokens, cache_pages, attn_gain, w_query, w_keyval, w_out, w_head, group_rows, head_count
        )
    partial_out, appended = attend(
        cache_pages, page_table, variate_bias, queries, variate_ids, appended, cache_variates, kv_cache
    )
    hidden, logits, stats = close(
        partial_out, tokens, head_gain, out_rows, head_rows, head_count, request_count, holders
    )
    return (hidden, appended, logits, stats[:, 0, 0], stats[:, 1, 0])


def solution(mesh):
    placed = (
        P(("req", "pg"), None),
        P("req"),
        P("req"),
        P("req", None),
        P(("req", "pg"), None, None),
        P(("req", "pg"), None),
        P(),
        P("req", "pg"),
        P("req", "pg"),
        P("req", "pg"),
        P(),
        P(),
        P("req", "pg"),
    )
    return jax.shard_map(
        per_device,
        mesh=mesh,
        in_specs=placed,
        out_specs=(
            P(("req", "pg"), None),
            P(("req", "pg"), None),
            P(("req", "pg"), None),
            P("req"),
            P("req"),
        ),
        check_vma=False,
    )
```

```python
import functools
import math

import jax
import jax.numpy as jnp
import numpy as np
from jax import lax
from jax.experimental import pallas as pl
from jax.experimental.pallas import tpu as pltpu
from jax.sharding import PartitionSpec as P

PAGE = 128


EPSILON = 1e-05
NEGATIVE = -1e30


def rms_norm(values, gain):
    wide = values.astype(jnp.float32)
    power = jnp.mean(wide * wide, axis=-1, keepdims=True)
    return (wide * lax.rsqrt(power + EPSILON) * gain).astype(jnp.bfloat16)


def rope_angles(positions, half_width):
    steps = jnp.arange(half_width, dtype=jnp.float32) / half_width
    freqs = jnp.exp(-math.log(10000.0) * steps)
    angle = positions.astype(jnp.float32)[:, None] * freqs[None, :]
    return (jnp.cos(angle), jnp.sin(angle))


def rotate(values, cosine, sine_part, head_count):
    count = values.shape[0]
    halves = values.astype(jnp.float32).reshape(count, head_count, 2, -1)
    front_half = halves[:, :, 0, :]
    second = halves[:, :, 1, :]
    cosine_wide = cosine[:, None, :]
    sine_wide = sine_part[:, None, :]
    turned = jnp.stack(
        [
            front_half * cosine_wide - second * sine_wide,
            second * cosine_wide + front_half * sine_wide,
        ],
        axis=2,
    )
    return turned.reshape(count, -1).astype(jnp.bfloat16)


def lookup_small(table_rows, lookup_index, count):
    matches = lookup_index[:, None] == jnp.arange(count, dtype=jnp.int32)[None, :]
    return jnp.sum(jnp.where(matches, table_rows[None, :], 0), axis=1)


def attend_kernel(
    pages_ref, table_ref, bias_ref, q_ref, ids_ref, new_ref, cids_ref, kv_hbm,
    out_ref, app_ref, kv_buf, vt_buf, acc_ref, peak_ref, sum_ref, same_ref, owner_ref, sems,
):
    request_count, _, span = ids_ref.shape
    slot_count, page_rows, _ = kv_hbm.shape
    pairs = q_ref.shape[0]
    features = 128 * pairs
    own_rows = new_ref.shape[0]
    me = lax.axis_index("pg")

    def fetch(slot):
        return pltpu.make_async_copy(kv_hbm.at[slot], kv_buf.at[slot], sems.at[slot])

    for slot in range(slot_count):
        fetch(slot).start()

    app_ref[...] = new_ref[...]
    for slot in range(slot_count):
        owner_ref[slot] = -1

    for request in range(request_count):

        def look(page, _):
            slot = table_ref[request, page] - me * slot_count

            @pl.when((slot >= 0) & (slot < slot_count))
            def _():
                owner_ref[slot] = request

            return 0

        lax.fori_loop(0, pages_ref[request], look, 0)

    acc_ref[...] = jnp.zeros_like(acc_ref)
    sum_ref[...] = jnp.zeros_like(sum_ref)
    peak_ref[...] = jnp.full_like(peak_ref, NEGATIVE)

    def absorb(request, k_of, v_of, key_ids, count, offset):
        lane = lax.broadcasted_iota(jnp.int32, (count, 128), 1)
        left = jnp.where(lane < 64, 1.0, 0.0).astype(jnp.bfloat16)
        right = jnp.where(lane < 64, 0.0, 1.0).astype(jnp.bfloat16)
        row = lax.broadcasted_iota(jnp.int32, (128, count), 0)
        ones_row = lax.broadcasted_iota(jnp.int32, (16, 2 * count), 0)
        ones_col = lax.broadcasted_iota(jnp.int32, (16, 2 * count), 1)
        ones = jnp.where((ones_row < 8) == (ones_col < count), 1.0, 0.0).astype(jnp.bfloat16)
        for pair in range(pairs):
            value = v_of(pair).astype(jnp.float32).T
            vt_buf[pair, :128, 0:count] = jnp.where(row < 64, value, 0.0).astype(jnp.bfloat16)
            vt_buf[pair, :128, count : 2 * count] = jnp.where(row >= 64, value, 0.0).astype(
                jnp.bfloat16
            )
            vt_buf[pair, 128:, 0 : 2 * count] = ones

        def tile(index, _):
            start = pl.multiple_of(index * 256, 256)
            query_ids = ids_ref[request, :, pl.ds(start, 256)]
            same = jnp.broadcast_to(query_ids, (count, 256)) == jnp.concatenate(
                [key_ids, key_ids], axis=1
            )
            same_ref[:count] = jnp.where(same, 1.0, 0.0)
            if offset is not None:
                allowed = (
                    lax.broadcasted_iota(jnp.int32, (count, 256), 0) + offset
                    <= lax.broadcasted_iota(jnp.int32, (count, 256), 1) + start
                )
            for pair in range(pairs):
                keys = k_of(pair)
                both = jnp.concatenate([keys * left, keys * right], axis=0)
                query = q_ref[pair, pl.ds(request * span + start, 256), :]
                scores = lax.dot_general(
                    both, query, (((1,), (1,)), ((), ())), preferred_element_type=jnp.float32
                )
                weights, fades = [], []
                for side in range(2):
                    head = 2 * pair + side
                    part = scores[side * count : (side + 1) * count] * 0.125
                    part = part + jnp.where(
                        same_ref[:count] > 0.5, bias_ref[0, head], bias_ref[1, head]
                    )
                    if offset is not None:
                        part = jnp.where(allowed, part, NEGATIVE)
                    old = peak_ref[request, head : head + 1, pl.ds(start, 256)]
                    new = jnp.maximum(old, jnp.max(part, axis=0, keepdims=True))
                    peak_ref[request, head : head + 1, pl.ds(start, 256)] = new
                    weight = jnp.exp(part - new)
                    if offset is not None:
                        weight = jnp.where(allowed, weight, 0.0)
                    weights.append(weight.astype(jnp.bfloat16))
                    fades.append(jnp.exp(old - new))
                summed = jnp.dot(
                    vt_buf[pair, :, 0 : 2 * count],
                    jnp.concatenate(weights, axis=0),
                    preferred_element_type=jnp.float32,
                )
                for side in range(2):
                    head = 2 * pair + side
                    rows = slice(128 * pair + 64 * side, 128 * pair + 64 * side + 64)
                    acc_ref[request, rows, pl.ds(start, 256)] = (
                        acc_ref[request, rows, pl.ds(start, 256)] * fades[side]
                        + summed[64 * side : 64 * side + 64]
                    )
                    sum_ref[request, head : head + 1, pl.ds(start, 256)] = (
                        sum_ref[request, head : head + 1, pl.ds(start, 256)] * fades[side]
                        + summed[128 + 8 * side : 129 + 8 * side]
                    )
            return 0

        lax.fori_loop(0, span // 256, tile, 0)

    first_row = me * own_rows
    request_own = first_row // span
    offset = first_row % span
    chunk = pl.multiple_of((offset // 128) * 128, 128)
    wide_ids = ids_ref[request_own, :, pl.ds(chunk, 128)]
    column = jnp.broadcast_to(wide_ids, (128, 128)).T
    lower = offset - chunk
    own_ids = jnp.where(lower == 0, column[:own_rows], column[128 - own_rows :])
    absorb(
        request_own,
        lambda pair: new_ref[:, 128 * pair : 128 * pair + 128],
        lambda pair: new_ref[:, features + 128 * pair : features + 128 * pair + 128],
        own_ids,
        own_rows,
        offset,
    )

    def visit(slot, _):
        owner = owner_ref[slot]
        fetch(slot).wait()

        @pl.when(owner >= 0)
        def _():
            column = jnp.broadcast_to(cids_ref[pl.ds(slot, 1), :], (page_rows, 128)).T
            absorb(
                owner,
                lambda pair: kv_buf[slot, :, 128 * pair : 128 * pair + 128],
                lambda pair: kv_buf[slot, :, features + 128 * pair : features + 128 * pair + 128],
                column,
                page_rows,
                None,
            )

        return 0

    lax.fori_loop(0, slot_count, visit, 0)

    def close(flat, _):
        request = flat // (span // 256)
        start = pl.multiple_of((flat % (span // 256)) * 256, 256)
        place = pl.ds(pl.multiple_of(flat * 256, 256), 256)
        total = sum_ref[request, :, pl.ds(start, 256)]
        live = total > 0
        safe = jnp.where(live, total, 1.0)
        level = jnp.where(live, peak_ref[request, :, pl.ds(start, 256)] + jnp.log(safe), NEGATIVE)
        inverse = jnp.where(live, 1.0 / safe, 0.0)
        for pair in range(pairs):
            block = jnp.concatenate(
                [
                    acc_ref[request, 128 * pair + 64 * side : 128 * pair + 64 * side + 64, pl.ds(start, 256)]
                    * inverse[2 * pair + side : 2 * pair + side + 1]
                    for side in range(2)
                ],
                axis=0,
            )
            out_ref[place, 128 * pair : 128 * pair + 128] = block.T.astype(jnp.bfloat16)
        high = level.astype(jnp.bfloat16).astype(jnp.float32)
        middle = (level - high).astype(jnp.bfloat16).astype(jnp.float32)
        low = level - high - middle
        heads = level.shape[0]
        filler = jnp.zeros((128 - 3 * heads, 256), jnp.float32)
        stacked = jnp.concatenate([high, middle, low, filler], axis=0)
        out_ref[place, features : features + 128] = stacked.T.astype(jnp.bfloat16)
        return 0

    lax.fori_loop(0, request_count * (span // 256), close, 0)


def attend(pages, table, bias, queries, ids, new_pairs, cache_ids, kv_cache):
    request_count = pages.shape[0]
    pairs, rows, _ = queries.shape
    features = 128 * pairs
    span = rows // request_count
    slot_count, page_rows, _ = kv_cache.shape
    heads = bias.shape[1]
    smem = pl.BlockSpec(memory_space=pltpu.SMEM)
    vmem = pl.BlockSpec(memory_space=pltpu.VMEM)
    return pl.pallas_call(
        attend_kernel,
        out_shape=(
            jax.ShapeDtypeStruct((rows, features + 128), jnp.bfloat16),
            jax.ShapeDtypeStruct(new_pairs.shape, jnp.bfloat16),
        ),
        in_specs=[smem, smem, smem, vmem, vmem, vmem, vmem, pl.BlockSpec(memory_space=pl.ANY)],
        out_specs=(vmem, vmem),
        scratch_shapes=[
            pltpu.VMEM(kv_cache.shape, jnp.bfloat16),
            pltpu.VMEM((features // 128, 144, 2 * page_rows), jnp.bfloat16),
            pltpu.VMEM((request_count, features, span), jnp.float32),
            pltpu.VMEM((request_count, heads, span), jnp.float32),
            pltpu.VMEM((request_count, heads, span), jnp.float32),
            pltpu.VMEM((page_rows, 256), jnp.float32),
            pltpu.SMEM((slot_count,), jnp.int32),
            pltpu.SemaphoreType.DMA((slot_count,)),
        ],
        compiler_params=pltpu.CompilerParams(vmem_limit_bytes=56 * 1024 * 1024),
        cost_estimate=pl.CostEstimate(
            flops=4 * slot_count * page_rows * span * features * 4,
            bytes_accessed=kv_cache.size * 2 + rows * features * 4,
            transcendentals=slot_count * page_rows * span * heads,
        ),
    )(pages, table, bias, queries, ids.reshape(request_count, 1, span), new_pairs, cache_ids, kv_cache)


def remote(source, target, send_sem, recv_sem, where):
    return pltpu.make_async_remote_copy(
        src_ref=source,
        dst_ref=target,
        send_sem=send_sem,
        recv_sem=recv_sem,
        device_id=where,
        device_id_type=pl.DeviceIdType.MESH,
    )


def greet(places):
    barrier = pltpu.get_barrier_semaphore()
    for place in places:
        pl.semaphore_signal(barrier, inc=1, device_id=place, device_id_type=pl.DeviceIdType.MESH)
    return lambda: pl.semaphore_wait(barrier, len(places))


def project_kernel(
    pages_ref, freq_ref, tokens_ref, gain_ref, wq_ref, wkv_ref, wo_ref, wh_ref,
    q_out, app_out, wo_out, wh_out,
    tok, wkv, wq, kv_stage, wh_all, cos_ref, sin_ref,
    tok_far, tok_near, tok_recv,
    w_far, w_near, w_recv,
    wq_far, wq_near, wq_recv, wqx_send, wqx_recv, wqc_send, wqc_recv,
    wo_far, wo_near, wo_recv, wox_send, wox_recv,
    wh_far, wh_near, wh_recv,
    kv_send, kv_recv, local_sem,
):
    _, planes, own_rows, features = tok.shape
    holders = 2 * planes
    req_count, deep, joined = wkv.shape
    req_pairs = req_count // 2
    request_count = pages_ref.shape[0]
    rows = holders * own_rows
    span = rows // request_count
    me = lax.axis_index("pg")
    mine = lax.axis_index("req")
    zz, yy = me // 2, me % 2
    other = 1 - yy
    xx, cc = mine // 2, mine % 2
    core_place = {"req": 2 * xx + 1 - cc}
    near_place = {"pg": 2 * zz + other}

    def plane(step):
        return (zz + step) % planes

    def far_place(step):
        return {"pg": 2 * plane(step) + yy}

    def req_far(step):
        return (xx + step) % req_pairs

    def x_place(step):
        return {"req": 2 * req_far(step) + cc}

    places = [{"pg": (me + step) % holders} for step in range(1, holders)]
    places += [x_place(step) for step in range(1, req_pairs)] + [core_place]
    arrived = greet(places)

    def columns(holder):
        return pl.ds(pl.multiple_of(holder * 128, 128), 128)

    keeps = [
        pltpu.make_async_copy(wq_ref, wq.at[xx, cc, :, columns(me)], local_sem.at[0]),
        pltpu.make_async_copy(wo_ref, wo_out.at[xx, :, columns(me)], local_sem.at[1]),
    ]
    for keep in keeps:
        keep.start()

    wide = tokens_ref[...].astype(jnp.float32)
    power = jnp.mean(wide * wide, axis=-1, keepdims=True)
    tok[yy, zz] = (wide * lax.rsqrt(power + EPSILON) * gain_ref[...]).astype(jnp.bfloat16)
    wkv[mine] = wkv_ref[...]
    head_cols = wh_ref.shape[0]
    packs = 128 // head_cols
    slab = deep // packs
    wh_wide = wh_ref[...].astype(jnp.float32).T
    wh_all[me] = jnp.concatenate(
        [wh_wide[slab * pack : slab * pack + slab] for pack in range(packs)], axis=1
    ).astype(jnp.bfloat16)
    for keep in keeps:
        keep.wait()
    arrived()

    started = []

    def begin(copy):
        copy.start()
        started.append(copy)

    def wq_copy(holder, send_sem, place):
        part = wq.at[xx, cc, :, columns(holder)]
        return remote(part, part, send_sem, wq_recv.at[holder], place)

    def wq_over(depth, holder, step, place):
        part = wq.at[depth, cc, :, columns(holder)]
        return remote(part, part, wqx_send.at[step, holder], wqx_recv.at[depth, holder], place)

    def wq_pass(side, holder):
        part = wq.at[:, side, :, columns(holder)]
        return remote(part, part, wqc_send.at[holder], wqc_recv.at[holder], core_place)

    def spread_x(holder):
        for step in range(1, req_pairs):
            begin(wq_over(xx, holder, step, x_place(step)))

    def pass_core(holder):
        for step in range(1, req_pairs):
            wq_over(req_far(step), holder, step, core_place).wait_recv()
        begin(wq_pass(cc, holder))

    def tok_copy(side, depth, send_sem, place):
        return remote(
            tok.at[side, depth], tok.at[side, depth], send_sem, tok_recv.at[side, depth], place
        )

    def w_copy(block, send_sem, place):
        return remote(wkv.at[block], wkv.at[block], send_sem, w_recv.at[block], place)

    for step in range(1, planes):
        begin(wq_copy(me, wq_far.at[step], far_place(step)))
        begin(tok_copy(yy, zz, tok_far.at[step], far_place(step)))
    begin(wq_copy(me, wq_near.at[0], near_place))
    begin(tok_copy(yy, zz, tok_near.at[0], near_place))
    for step in range(1, req_pairs):
        begin(w_copy(mine, w_far.at[step], x_place(step)))
    begin(w_copy(mine, w_near.at[0], core_place))
    spread_x(me)

    row = lax.broadcasted_iota(jnp.int32, (1, rows), 1)
    held = jnp.zeros((1, rows), jnp.int32)
    for request in range(request_count):
        held = jnp.where(row // span == request, pages_ref[request], held)
    position = (held * PAGE + row % span).astype(jnp.float32)
    angle = freq_ref[...] * position
    cosine, sine = jnp.cos(angle), jnp.sin(angle)
    cos_ref[...] = jnp.concatenate([cosine] * 4, axis=0).T.reshape(cos_ref.shape)
    sin_ref[...] = jnp.concatenate([-sine, sine, -sine, sine], axis=0).T.reshape(sin_ref.shape)

    for step in range(1, req_pairs):
        block = 2 * req_far(step) + cc
        w_copy(block, w_far.at[step], core_place).wait_recv()
        begin(w_copy(block, w_near.at[step], core_place))
    for step in range(1, planes):
        holder = 2 * plane(step) + yy
        wq_copy(holder, wq_far.at[step], near_place).wait_recv()
        begin(wq_copy(holder, wq_near.at[step], near_place))
        spread_x(holder)
        tok_copy(yy, plane(step), tok_far.at[step], near_place).wait_recv()
        begin(tok_copy(yy, plane(step), tok_near.at[step], near_place))

    def wo_copy(holder, send_sem, place):
        part = wo_out.at[xx, :, columns(holder)]
        return remote(part, part, send_sem, wo_recv.at[holder], place)

    def wo_over(depth, holder, step, place):
        part = wo_out.at[depth, :, columns(holder)]
        return remote(part, part, wox_send.at[step, holder], wox_recv.at[depth, holder], place)

    def wh_copy(holder, send_sem, place):
        return remote(wh_all.at[holder], wh_all.at[holder], send_sem, wh_recv.at[holder], place)

    for step in range(1, planes):
        begin(wo_copy(me, wo_far.at[step], far_place(step)))
        begin(wh_copy(me, wh_far.at[step], far_place(step)))
    begin(wo_copy(me, wo_near.at[0], near_place))
    begin(wh_copy(me, wh_near.at[0], near_place))

    def wo_spread(holder):
        for step in range(1, req_pairs):
            begin(wo_over(xx, holder, step, x_place(step)))

    for step in range(req_pairs):
        block = 2 * req_far(step) + 1 - cc
        w_copy(block, w_near.at[step], core_place).wait_recv()

    def kv_copy(source, side, depth, send_sem, place):
        start = pl.multiple_of(source * 256, 256)
        return remote(
            kv_stage.at[depth, side], app_out.at[:, pl.ds(start, 256)], send_sem,
            kv_recv.at[source], place,
        )

    half_rows = planes * own_rows
    lane = lax.broadcasted_iota(jnp.int32, (half_rows, 128), 1)
    front = (lane % 64) < 32
    is_key = (jnp.zeros((half_rows, 128), jnp.int32) + me) < planes

    def turned(value, cosine, sine):
        value = value.astype(jnp.bfloat16).astype(jnp.float32)
        swapped = jnp.where(front, pltpu.roll(value, 96, 1), pltpu.roll(value, 32, 1))
        return (value * cosine + swapped * sine).astype(jnp.bfloat16)

    def half(turn):
        side = yy if turn == 0 else other
        made = jnp.dot(
            tok[side].reshape(half_rows, features),
            wkv[...].reshape(features, joined),
            preferred_element_type=jnp.float32,
        )
        key_cos = jnp.where(is_key, cos_ref[:, side].reshape(half_rows, 128), 1.0)
        key_sin = jnp.where(is_key, sin_ref[:, side].reshape(half_rows, 128), 0.0)
        for part in range(joined // 128):
            piece = turned(made[:, 128 * part : 128 * part + 128], key_cos, key_sin)
            kv_stage[:, side, :, 128 * part : 128 * part + 128] = piece.reshape(
                planes, own_rows, 128
            )
        for step in range(0 if turn == 1 else 1, planes):
            place = {"pg": 2 * plane(step) + side}
            begin(kv_copy(me, side, plane(step), kv_send.at[turn, step], place))

    half(0)
    own_keep = pltpu.make_async_copy(
        kv_stage.at[zz, yy],
        app_out.at[:, pl.ds(pl.multiple_of(me * 256, 256), 256)],
        local_sem.at[2],
    )
    own_keep.start()
    for step in range(planes):
        holder = 2 * plane(step) + other
        wq_copy(holder, wq_near.at[step], near_place).wait_recv()
        spread_x(holder)
    for step in range(planes):
        pass_core(2 * plane(step) + yy)
    for step in range(planes):
        tok_copy(other, plane(step), tok_near.at[step], near_place).wait_recv()
    half(1)
    for step in range(1, planes):
        holder = 2 * plane(step) + yy
        wh_copy(holder, wh_far.at[step], near_place).wait_recv()
        begin(wh_copy(holder, wh_near.at[step], near_place))
        wo_copy(holder, wo_far.at[step], near_place).wait_recv()
        begin(wo_copy(holder, wo_near.at[step], near_place))
        wo_spread(holder)
    wo_spread(me)
    for step in range(planes):
        pass_core(2 * plane(step) + other)

    for step in range(planes):
        depth = plane(step)
        for side in range(2):
            wq_pass(1 - cc, 2 * depth + side).wait_recv()
        start = pl.multiple_of(depth * 256, 256)
        weight = wq[:, :, :, pl.ds(start, 256)].reshape(features, 256)
        for side in range(2):
            made = jnp.dot(
                tok[side].reshape(half_rows, features), weight, preferred_element_type=jnp.float32
            )
            cosine = cos_ref[:, side].reshape(half_rows, 128)
            sine = sin_ref[:, side].reshape(half_rows, 128)
            for part in range(2):
                piece = turned(made[:, 128 * part : 128 * part + 128], cosine, sine)
                q_out[2 * depth + part, :, side] = piece.reshape(planes, own_rows, 128)

    for step in range(planes):
        wh_copy(2 * plane(step) + other, wh_near.at[step], near_place).wait_recv()
    for pack in range(packs):
        wh_out[slab * pack : slab * pack + slab, :] = jnp.concatenate(
            [
                wh_all[holder].astype(jnp.float32)[:, head_cols * pack : head_cols * pack + head_cols]
                for holder in range(holders)
            ],
            axis=1,
        ).astype(jnp.bfloat16)
    for step in range(1, holders):
        kv_copy((me + step) % holders, yy, zz, kv_send.at[0, 0], near_place).wait_recv()
    own_keep.wait()
    for step in range(planes):
        wo_copy(2 * plane(step) + other, wo_near.at[step], near_place).wait_recv()
        for turn in range(1, req_pairs):
            wo_over(req_far(turn), 2 * plane(step) + yy, turn, core_place).wait_recv()
    for copy in started:
        copy.wait_send()


def project(pages, freqs, tokens, gain, w_query, w_keyval, w_out, w_head, holders, req_count):
    own_rows, features = tokens.shape
    planes = holders // 2
    deep = w_query.shape[0]
    vmem = pl.BlockSpec(memory_space=pltpu.VMEM)
    bf16 = jnp.bfloat16
    dma = pltpu.SemaphoreType.DMA
    pairs = req_count // 2
    return pl.pallas_call(
        project_kernel,
        out_shape=(
            jax.ShapeDtypeStruct((holders, planes, 2, own_rows, 128), bf16),
            jax.ShapeDtypeStruct((own_rows, 2 * features), bf16),
            jax.ShapeDtypeStruct((pairs, deep, features), bf16),
            jax.ShapeDtypeStruct((deep, holders * w_head.shape[0]), bf16),
        ),
        in_specs=[pl.BlockSpec(memory_space=pltpu.SMEM)] + [vmem] * 7,
        out_specs=(vmem, vmem, vmem, vmem),
        scratch_shapes=[
            pltpu.VMEM((2, planes, own_rows, features), bf16),
            pltpu.VMEM((req_count, deep, w_keyval.shape[1]), bf16),
            pltpu.VMEM((pairs, 2, deep, features), bf16),
            pltpu.VMEM((planes, 2, own_rows, 256), bf16),
            pltpu.VMEM((holders, deep * w_head.shape[0] // 128, 128), bf16),
            pltpu.VMEM((planes, 2, own_rows, 128), jnp.float32),
            pltpu.VMEM((planes, 2, own_rows, 128), jnp.float32),
            dma((planes,)), dma((planes,)), dma((2, planes)),
            dma((pairs,)), dma((pairs,)), dma((req_count,)),
            dma((planes,)), dma((planes,)), dma((holders,)),
            dma((pairs, holders)), dma((pairs, holders)), dma((holders,)), dma((holders,)),
            dma((planes,)), dma((planes,)), dma((holders,)),
            dma((pairs, holders)), dma((pairs, holders)),
            dma((planes,)), dma((planes,)), dma((holders,)),
            dma((2, planes)), dma((holders,)), dma((3,)),
        ],
        compiler_params=pltpu.CompilerParams(
            collective_id=0, has_side_effects=True, vmem_limit_bytes=56 * 1024 * 1024
        ),
        cost_estimate=pl.CostEstimate(
            flops=2 * holders * own_rows * features * (features + w_keyval.shape[1]),
            bytes_accessed=features * features * 6,
            transcendentals=0,
        ),
    )(pages, freqs, tokens, gain.reshape(1, features), w_query, w_keyval, w_out, w_head)


def expander(features, head_width):
    head = lax.broadcasted_iota(jnp.int32, (128, features), 0)
    column = lax.broadcasted_iota(jnp.int32, (128, features), 1)
    return jnp.where(column // head_width == head, 1.0, 0.0).astype(jnp.bfloat16)


def join_parts(parts, spread, features, head_count):
    levels = []
    for part in parts:
        coded = part[:, features:].astype(jnp.float32)
        levels.append(
            coded
            + pltpu.roll(coded, 128 - head_count, 1)
            + pltpu.roll(coded, 128 - 2 * head_count, 1)
        )
    top = functools.reduce(jnp.maximum, levels)
    shares = [jnp.exp(level - top) for level in levels]
    total = functools.reduce(jnp.add, shares)
    joined = None
    for part, share in zip(parts, shares):
        share = share / total
        high = share.astype(jnp.bfloat16)
        low = (share - high.astype(jnp.float32)).astype(jnp.bfloat16)
        wide = jnp.dot(high, spread, preferred_element_type=jnp.float32) + jnp.dot(
            low, spread, preferred_element_type=jnp.float32
        )
        term = part[:, :features].astype(jnp.float32) * wide
        joined = term if joined is None else joined + term
    return joined, top + jnp.log(total)


def close_kernel(
    parts_ref, tokens_ref, gain_ref, wo_ref, wh_ref,
    hidden_ref, logits_ref, stats_out,
    near_buf, send_buf, far_buf, stat_buf, spread_ref, wo_all, wh_all,
    wo_near, wo_recv, wox_send, wox_recv, keep_sem, wh_far, wh_near, wh_recv,
    near_send, near_recv, far_send, far_recv, stat_send, stat_recv,
    *, head_count, request_count,
):
    planes, _, own_rows, coded = parts_ref.shape
    holders = 2 * planes
    features = coded - 128
    me = lax.axis_index("pg")
    zz, yy = me // 2, me % 2
    other = 1 - yy
    near_place = {"pg": 2 * zz + other}
    req_pairs = wo_all.shape[0]
    block = 128
    planes_out = features // (2 * block)
    mine = lax.axis_index("req")
    xx, cc = mine // 2, mine % 2
    core_place = {"req": 2 * xx + 1 - cc}

    def req_far(step):
        return (xx + step) % req_pairs

    arrived = greet(
        [{"pg": (me + step) % holders} for step in range(1, holders)]
        + [{"req": 2 * req_far(step) + cc} for step in range(1, req_pairs)]
        + [core_place]
    )
    def columns(depth, side):
        return pl.ds(pl.multiple_of((2 * depth + side) * block, block), block)

    keeps = [pltpu.make_async_copy(wo_ref.at[xx], wo_all.at[xx, cc], keep_sem.at[0, 0])]
    for step in range(1, req_pairs):
        far = req_far(step)
        for depth in range(planes_out):
            keeps.append(
                pltpu.make_async_copy(
                    wo_ref.at[far, :, columns(depth, yy)],
                    wo_all.at[far, cc, :, columns(depth, yy)],
                    keep_sem.at[step, depth],
                )
            )
    for keep in keeps:
        keep.start()
    wh_all[xx, cc] = wh_ref[...]
    spread_ref[...] = expander(features, features // head_count)
    arrived()
    order = list(range(1, planes)) + [0]
    started = []

    def near_copy(depth, step):
        return remote(
            parts_ref.at[depth, other], near_buf.at[depth], near_send.at[step],
            near_recv.at[depth], near_place,
        )

    for step in order:
        copy = near_copy((zz + step) % planes, step)
        copy.start()
        started.append(copy)

    def wo_copy(depth, side, send_sem, place):
        part = wo_all.at[depth, side]
        return remote(part, part, send_sem, wo_recv.at[depth, side], place)

    def wo_over(depth, step, column, place):
        part = wo_all.at[depth, cc, :, columns(column, other)]
        return remote(part, part, wox_send.at[step, column], wox_recv.at[depth, column], place)

    def wh_copy(depth, side, send_sem, place):
        part = wh_all.at[depth, side]
        return remote(part, part, send_sem, wh_recv.at[depth, side], place)

    for step in range(1, req_pairs):
        place = {"req": 2 * req_far(step) + cc}
        started += [wo_over(xx, step, column, place) for column in range(planes_out)]
        started.append(wh_copy(xx, cc, wh_far.at[step], place))
    started += [
        wo_copy(xx, cc, wo_near.at[0], core_place), wh_copy(xx, cc, wh_near.at[0], core_place)
    ]
    for keep in keeps:
        keep.wait()
    for copy in started[planes:]:
        copy.start()
    lane = lax.broadcasted_iota(jnp.int32, (own_rows, 128), 1)
    for step in order:
        depth = (zz + step) % planes
        near_copy(depth, step).wait_recv()
        joined, level = join_parts(
            [parts_ref[depth, yy], near_buf[depth]], spread_ref[...], features, head_count
        )
        level = jnp.where(lane < head_count, level, 0.0)
        high = level.astype(jnp.bfloat16).astype(jnp.float32)
        middle = (level - high).astype(jnp.bfloat16).astype(jnp.float32)
        low = level - high - middle
        code = high + pltpu.roll(middle, head_count, 1) + pltpu.roll(low, 2 * head_count, 1)
        if step == 0:
            far_buf[zz, :, :features] = joined.astype(jnp.bfloat16)
            far_buf[zz, :, features:] = code.astype(jnp.bfloat16)
        else:
            send_buf[step, :, :features] = joined.astype(jnp.bfloat16)
            send_buf[step, :, features:] = code.astype(jnp.bfloat16)
            copy = remote(
                send_buf.at[step], far_buf.at[zz], far_send.at[step], far_recv.at[zz],
                {"pg": 2 * depth + yy},
            )
            copy.start()
            started.append(copy)
    for step in range(1, req_pairs):
        depth = req_far(step)
        for column in range(planes_out):
            wo_over(depth, step, column, core_place).wait_recv()
        wh_copy(depth, cc, wh_far.at[step], core_place).wait_recv()
        for copy in (
            wo_copy(depth, cc, wo_near.at[step], core_place),
            wh_copy(depth, cc, wh_near.at[step], core_place),
        ):
            copy.start()
            started.append(copy)
    for step in range(1, planes):
        depth = (zz + step) % planes
        remote(
            send_buf.at[step], far_buf.at[depth], far_send.at[step], far_recv.at[depth], near_place
        ).wait_recv()
    joined, _ = join_parts(
        [far_buf[depth] for depth in range(planes)], spread_ref[...], features, head_count
    )
    attention = joined.astype(jnp.bfloat16)
    for step in range(req_pairs):
        wo_copy(req_far(step), 1 - cc, wo_near.at[step], core_place).wait_recv()
        wh_copy(req_far(step), 1 - cc, wh_near.at[step], core_place).wait_recv()
    out_weight = wo_all[...].reshape(features, features)
    head_weight = wh_all[...].reshape(features, wh_ref.shape[1])
    hidden = (
        tokens_ref[...].astype(jnp.float32)
        + jnp.dot(attention, out_weight, preferred_element_type=jnp.float32)
    ).astype(jnp.bfloat16)
    hidden_ref[...] = hidden
    wide = hidden.astype(jnp.float32)
    squares = wide * wide
    power = jnp.mean(squares, axis=-1, keepdims=True)
    head_in = (wide * lax.rsqrt(power + EPSILON) * gain_ref[...]).astype(jnp.bfloat16)
    logits = jnp.dot(head_in, head_weight, preferred_element_type=jnp.float32)
    logits_ref[...] = logits.astype(jnp.bfloat16)
    energy = jnp.sum(jnp.sum(squares, axis=1, keepdims=True), axis=0, keepdims=True)
    peak = jnp.max(jnp.max(logits, axis=1, keepdims=True), axis=0, keepdims=True)
    is_first = lax.broadcasted_iota(jnp.int32, (8, 128), 0) == 0
    stat_buf[me] = jnp.where(
        is_first, jnp.broadcast_to(energy, (8, 128)), jnp.broadcast_to(peak, (8, 128))
    )
    for step in range(1, holders):
        copy = remote(
            stat_buf.at[me], stat_buf.at[me], stat_send.at[step], stat_recv.at[me],
            {"pg": (me + step) % holders},
        )
        copy.start()
        started.append(copy)
    for step in range(1, holders):
        source = (me + step) % holders
        remote(
            stat_buf.at[source], stat_buf.at[source], stat_send.at[step], stat_recv.at[source],
            near_place,
        ).wait_recv()
    every = holders // request_count
    for request in range(request_count):
        mine = [stat_buf[every * request + block] for block in range(every)]
        total = functools.reduce(jnp.add, mine)
        top = functools.reduce(jnp.maximum, mine)
        stats_out[request] = jnp.where(is_first, jnp.sqrt(total), top)
    for copy in started:
        copy.wait_send()


def close(parts, tokens, gain, wo, wh, head_count, request_count, holders):
    own_rows, features = tokens.shape
    planes = holders // 2
    coded = features + 128
    pairs = wo.shape[0]
    planes_out = features // 256
    vmem = pl.BlockSpec(memory_space=pltpu.VMEM)
    bf16 = jnp.bfloat16
    dma = pltpu.SemaphoreType.DMA
    return pl.pallas_call(
        functools.partial(close_kernel, head_count=head_count, request_count=request_count),
        out_shape=(
            jax.ShapeDtypeStruct((own_rows, features), bf16),
            jax.ShapeDtypeStruct((own_rows, wh.shape[1]), bf16),
            jax.ShapeDtypeStruct((request_count, 8, 128), jnp.float32),
        ),
        in_specs=[vmem] * 5,
        out_specs=(vmem, vmem, vmem),
        scratch_shapes=[
            pltpu.VMEM((planes, own_rows, coded), bf16),
            pltpu.VMEM((planes, own_rows, coded), bf16),
            pltpu.VMEM((planes, own_rows, coded), bf16),
            pltpu.VMEM((holders, 8, 128), jnp.float32),
            pltpu.VMEM((128, features), bf16),
            pltpu.VMEM((pairs, 2) + wo.shape[1:], bf16),
            pltpu.VMEM((pairs, 2) + wh.shape, bf16),
            dma((pairs,)), dma((pairs, 2)), dma((pairs, planes_out)), dma((pairs, planes_out)), dma((pairs, planes_out)),
            dma((pairs,)), dma((pairs,)), dma((pairs, 2)),
            dma((planes,)), dma((planes,)), dma((planes,)), dma((planes,)),
            dma((holders,)), dma((holders,)),
        ],
        compiler_params=pltpu.CompilerParams(
            collective_id=1, has_side_effects=True, vmem_limit_bytes=56 * 1024 * 1024
        ),
        cost_estimate=pl.CostEstimate(
            flops=2 * own_rows * features * features,
            bytes_accessed=features * features * 4,
            transcendentals=0,
        ),
    )(parts.reshape(planes, 2, own_rows, coded), tokens, gain.reshape(1, features), wo, wh)

def project_plain(tokens, cache_pages, attn_gain, w_query, w_keyval, w_out, w_head, group_rows, head_count):
    own_rows, features = tokens.shape
    request_count = cache_pages.shape[0]
    span_rows = group_rows // request_count
    head_width = features // head_count
    first_row = lax.axis_index("pg") * own_rows
    normed = rms_norm(tokens, attn_gain)
    query_full, keyval_full = (
        lax.all_gather(w_query, "req", axis=0, tiled=True),
        lax.all_gather(w_keyval, "req", axis=0, tiled=True),
    )
    own_index = first_row + jnp.arange(own_rows, dtype=jnp.int32)
    own_positions = (
        lookup_small(cache_pages, own_index // span_rows, request_count) * PAGE
        + own_index % span_rows
    )
    own_cos, own_sin = rope_angles(own_positions, head_width // 2)
    query_cols = query_full.shape[1]
    joined = jnp.concatenate([query_full, keyval_full], axis=1)
    projected = jnp.dot(
        normed, lax.all_gather(joined, "pg", axis=1, tiled=True), preferred_element_type=jnp.float32
    )
    projected = projected.reshape(own_rows, -1, joined.shape[1])
    query_raw = projected[:, :, :query_cols].reshape(own_rows, features).astype(jnp.bfloat16)
    keyval_raw = projected[:, :, query_cols:].reshape(own_rows, 2 * features).astype(jnp.bfloat16)
    own_queries = rotate(query_raw, own_cos, own_sin, head_count)
    new_keys = rotate(keyval_raw[:, :features], own_cos, own_sin, head_count)
    new_values = keyval_raw[:, features:]
    appended = jnp.concatenate([new_keys, new_values], axis=1)
    queries = lax.all_gather(own_queries, "pg", axis=0, tiled=True)
    queries = queries.reshape(group_rows, features // 128, 128).transpose(1, 0, 2)
    out_slices = lax.all_gather(lax.all_gather(w_out, "pg", axis=1, tiled=True), "req")
    out_slices = out_slices.reshape(-1, 2, w_out.shape[0], features)
    return (
        queries,
        appended,
        lax.dynamic_index_in_dim(out_slices, lax.axis_index("req") % 2, 1, keepdims=False),
        lax.all_gather(w_head, "pg", axis=1, tiled=True),
    )


def per_device(
    tokens,
    variate_ids,
    cache_pages,
    page_table,
    kv_cache,
    cache_variates,
    attn_gain,
    w_query,
    w_keyval,
    w_out,
    variate_bias,
    head_gain,
    w_head,
):
    own_rows, features = tokens.shape
    request_count = cache_pages.shape[0]
    group_rows = variate_ids.shape[0]
    head_count = variate_bias.shape[1]
    holders = group_rows // own_rows
    half_width = features // head_count // 2
    req_count = features // w_query.shape[0]
    if w_query.shape[1] == 128 and w_keyval.shape[1] == 256:
        steps = np.arange(half_width, dtype=np.float32) / half_width
        freqs = np.exp(np.float32(-math.log(10000.0)) * steps).reshape(half_width, 1)
        queries, appended, out_rows, head_rows = project(
            cache_pages, freqs, tokens, attn_gain, w_query, w_keyval, w_out, w_head.T, holders, req_count
        )
        queries = queries.reshape(holders, group_rows, 128)
    else:
        queries, appended, out_rows, head_rows = project_plain(
            tokens, cache_pages, attn_gain, w_query, w_keyval, w_out, w_head, group_rows, head_count
        )
    partial_out, appended = attend(
        cache_pages, page_table, variate_bias, queries, variate_ids, appended, cache_variates, kv_cache
    )
    hidden, logits, stats = close(
        partial_out, tokens, head_gain, out_rows, head_rows, head_count, request_count, holders
    )
    hidden, logits, norms, peaks = hand_over(hidden, logits, stats)
    return (hidden, appended, logits, norms, peaks)


def hand_over_kernel(hidden_ref, logits_ref, stats_ref, hidden_out, logits_out, norm_out, peak_out):
    hidden_out[...] = hidden_ref[...]
    logits_out[...] = logits_ref[...]
    for request in range(stats_ref.shape[0]):
        norm_out[request] = stats_ref[request, 0, 0]
        peak_out[request] = stats_ref[request, 1, 0]


def hand_over(hidden, logits, stats):
    vmem = pl.BlockSpec(memory_space=pltpu.VMEM)
    smem = pl.BlockSpec(memory_space=pltpu.SMEM)
    scalars = jax.ShapeDtypeStruct((stats.shape[0],), jnp.float32)
    return pl.pallas_call(
        hand_over_kernel,
        out_shape=(
            jax.ShapeDtypeStruct(hidden.shape, hidden.dtype),
            jax.ShapeDtypeStruct(logits.shape, logits.dtype),
            scalars,
            scalars,
        ),
        in_specs=[vmem, vmem, smem],
        out_specs=(vmem, vmem, smem, smem),
    )(hidden, logits, stats)


def solution(mesh):
    placed = (
        P(("req", "pg"), None),
        P("req"),
        P("req"),
        P("req", None),
        P(("req", "pg"), None, None),
        P(("req", "pg"), None),
        P(),
        P("req", "pg"),
        P("req", "pg"),
        P("req", "pg"),
        P(),
        P(),
        P("req", "pg"),
    )
    return jax.shard_map(
        per_device,
        mesh=mesh,
        in_specs=placed,
        out_specs=(
            P(("req", "pg"), None),
            P(("req", "pg"), None),
            P(("req", "pg"), None),
            P("req"),
            P("req"),
        ),
        check_vma=False,
    )
```

```python
import functools
import math

import jax
import jax.numpy as jnp
import numpy as np
from jax import lax
from jax.experimental import pallas as pl
from jax.experimental.pallas import tpu as pltpu
from jax.sharding import PartitionSpec as P

PAGE = 128


EPSILON = 1e-05
NEGATIVE = -1e30
VARIATES = 4
LOG_2 = math.log(2.0)
SCALE = 0.125 / LOG_2


def rms_norm(values, gain):
    wide = values.astype(jnp.float32)
    power = jnp.mean(wide * wide, axis=-1, keepdims=True)
    return (wide * lax.rsqrt(power + EPSILON) * gain).astype(jnp.bfloat16)


def rope_angles(positions, half_width):
    steps = jnp.arange(half_width, dtype=jnp.float32) / half_width
    freqs = jnp.exp(-math.log(10000.0) * steps)
    angle = positions.astype(jnp.float32)[:, None] * freqs[None, :]
    return (jnp.cos(angle), jnp.sin(angle))


def rotate(values, cosine, sine_part, head_count):
    count = values.shape[0]
    halves = values.astype(jnp.float32).reshape(count, head_count, 2, -1)
    front_half = halves[:, :, 0, :]
    second = halves[:, :, 1, :]
    cosine_wide = cosine[:, None, :]
    sine_wide = sine_part[:, None, :]
    turned = jnp.stack(
        [
            front_half * cosine_wide - second * sine_wide,
            second * cosine_wide + front_half * sine_wide,
        ],
        axis=2,
    )
    return turned.reshape(count, -1).astype(jnp.bfloat16)


def lookup_small(table_rows, lookup_index, count):
    matches = lookup_index[:, None] == jnp.arange(count, dtype=jnp.int32)[None, :]
    return jnp.sum(jnp.where(matches, table_rows[None, :], 0), axis=1)


def attend_kernel(
    pages_ref, table_ref, bias_ref, q_ref, ids_ref, new_ref, cids_ref, kv_hbm,
    out_ref, app_ref, kv_buf, vt_buf, acc_ref, peak_ref, sum_ref, mark_ref, level_ref, owner_ref, sems,
):
    request_count, _, span = ids_ref.shape
    slot_count, page_rows, _ = kv_hbm.shape
    pairs = q_ref.shape[0]
    features = 128 * pairs
    own_rows = new_ref.shape[0]
    me = lax.axis_index("pg")

    def fetch(slot):
        return pltpu.make_async_copy(kv_hbm.at[slot], kv_buf.at[slot], sems.at[slot])

    for slot in range(slot_count):
        fetch(slot).start()

    app_ref[...] = new_ref[...]
    for slot in range(slot_count):
        owner_ref[slot] = -1

    for request in range(request_count):

        def look(page, _):
            slot = table_ref[request, page] - me * slot_count

            @pl.when((slot >= 0) & (slot < slot_count))
            def _():
                owner_ref[slot] = request

            return 0

        lax.fori_loop(0, pages_ref[request], look, 0)

    acc_ref[...] = jnp.zeros_like(acc_ref)
    sum_ref[...] = jnp.zeros_like(sum_ref)
    peak_ref[...] = jnp.full_like(peak_ref, NEGATIVE)

    wide_lane = lax.broadcasted_iota(jnp.int32, (128, 128), 1)
    term = lax.broadcasted_iota(jnp.int32, (1, 128), 1) // VARIATES
    for kind in range(2):
        for head in range(level_ref.shape[1]):
            whole = jnp.full((1, 128), bias_ref[kind, head]) * 8.0
            high = whole.astype(jnp.bfloat16).astype(jnp.float32)
            middle = (whole - high).astype(jnp.bfloat16).astype(jnp.float32)
            low = whole - high - middle
            level_ref[kind, head : head + 1, :] = jnp.where(
                term == 0, high, jnp.where(term == 1, middle, jnp.where(term == 2, low, 0.0))
            )

    def mark(flat, _):
        request = flat // (span // 128)
        start = pl.multiple_of((flat % (span // 128)) * 128, 128)
        column = jnp.broadcast_to(ids_ref[request, :, pl.ds(start, 128)], (128, 128)).T
        hit = (wide_lane % VARIATES == column) & (wide_lane < 3 * VARIATES)
        mark_ref[pl.ds(pl.multiple_of(flat * 128, 128), 128), :] = jnp.where(hit, 1.0, 0.0).astype(
            jnp.bfloat16
        )
        return 0

    lax.fori_loop(0, request_count * (span // 128), mark, 0)

    def absorb(request, k_of, v_of, key_ids, count, offset):
        lane = lax.broadcasted_iota(jnp.int32, (count, 128), 1)
        left = jnp.where(lane < 64, 1.0, 0.0).astype(jnp.bfloat16)
        right = jnp.where(lane < 64, 0.0, 1.0).astype(jnp.bfloat16)
        row = lax.broadcasted_iota(jnp.int32, (128, count), 0)
        ones_row = lax.broadcasted_iota(jnp.int32, (16, 2 * count), 0)
        ones_col = lax.broadcasted_iota(jnp.int32, (16, 2 * count), 1)
        same = lane % VARIATES == key_ids
        ones = jnp.where((ones_row < 8) == (ones_col < count), 1.0, 0.0).astype(jnp.bfloat16)
        for pair in range(pairs):
            value = v_of(pair).astype(jnp.float32).T
            vt_buf[pair, :128, 0:count] = jnp.where(row < 64, value, 0.0).astype(jnp.bfloat16)
            vt_buf[pair, :128, count : 2 * count] = jnp.where(row >= 64, value, 0.0).astype(
                jnp.bfloat16
            )
            vt_buf[pair, 128:, 0 : 2 * count] = ones

        def tile(index, _):
            start = pl.multiple_of(index * 256, 256)
            marks = mark_ref[pl.ds(pl.multiple_of(request * span + start, 256), 256), :]
            if offset is not None:
                allowed = (
                    lax.broadcasted_iota(jnp.int32, (count, 256), 0) + offset
                    <= lax.broadcasted_iota(jnp.int32, (count, 256), 1) + start
                )
            for pair in range(pairs):
                keys = k_of(pair)
                both = jnp.concatenate([keys * left, keys * right], axis=0)
                extra = jnp.concatenate(
                    [
                        jnp.where(
                            same, level_ref[0, head : head + 1, :], level_ref[1, head : head + 1, :]
                        ).astype(jnp.bfloat16)
                        for head in (2 * pair, 2 * pair + 1)
                    ],
                    axis=0,
                )
                query = q_ref[pair, pl.ds(request * span + start, 256), :]
                scores = lax.dot_general(
                    jnp.concatenate([both, extra], axis=1),
                    jnp.concatenate([query, marks], axis=1),
                    (((1,), (1,)), ((), ())), preferred_element_type=jnp.float32
                )
                weights, fades = [], []
                for side in range(2):
                    head = 2 * pair + side
                    part = scores[side * count : (side + 1) * count] * SCALE
                    if offset is not None:
                        part = jnp.where(allowed, part, NEGATIVE)
                    old = peak_ref[request, head : head + 1, pl.ds(start, 256)]
                    new = jnp.maximum(old, jnp.max(part, axis=0, keepdims=True))
                    peak_ref[request, head : head + 1, pl.ds(start, 256)] = new
                    weight = jnp.exp2(part - new)
                    if offset is not None:
                        weight = jnp.where(allowed, weight, 0.0)
                    weights.append(weight.astype(jnp.bfloat16))
                    fades.append(jnp.exp2(old - new))
                summed = jnp.dot(
                    vt_buf[pair, :, 0 : 2 * count],
                    jnp.concatenate(weights, axis=0),
                    preferred_element_type=jnp.float32,
                )
                for side in range(2):
                    head = 2 * pair + side
                    rows = slice(128 * pair + 64 * side, 128 * pair + 64 * side + 64)
                    acc_ref[request, rows, pl.ds(start, 256)] = (
                        acc_ref[request, rows, pl.ds(start, 256)] * fades[side]
                        + summed[64 * side : 64 * side + 64]
                    )
                    sum_ref[request, head : head + 1, pl.ds(start, 256)] = (
                        sum_ref[request, head : head + 1, pl.ds(start, 256)] * fades[side]
                        + summed[128 + 8 * side : 129 + 8 * side]
                    )
            return 0

        lax.fori_loop(0, span // 256, tile, 0)

    first_row = me * own_rows
    request_own = first_row // span
    offset = first_row % span
    chunk = pl.multiple_of((offset // 128) * 128, 128)
    wide_ids = ids_ref[request_own, :, pl.ds(chunk, 128)]
    column = jnp.broadcast_to(wide_ids, (128, 128)).T
    lower = offset - chunk
    own_ids = jnp.where(lower == 0, column[:own_rows], column[128 - own_rows :])
    absorb(
        request_own,
        lambda pair: new_ref[:, 128 * pair : 128 * pair + 128],
        lambda pair: new_ref[:, features + 128 * pair : features + 128 * pair + 128],
        own_ids,
        own_rows,
        offset,
    )

    def visit(slot, _):
        owner = owner_ref[slot]
        fetch(slot).wait()

        @pl.when(owner >= 0)
        def _():
            column = jnp.broadcast_to(cids_ref[pl.ds(slot, 1), :], (page_rows, 128)).T
            absorb(
                owner,
                lambda pair: kv_buf[slot, :, 128 * pair : 128 * pair + 128],
                lambda pair: kv_buf[slot, :, features + 128 * pair : features + 128 * pair + 128],
                column,
                page_rows,
                None,
            )

        return 0

    lax.fori_loop(0, slot_count, visit, 0)

    def close(flat, _):
        request = flat // (span // 256)
        start = pl.multiple_of((flat % (span // 256)) * 256, 256)
        place = pl.ds(pl.multiple_of(flat * 256, 256), 256)
        total = sum_ref[request, :, pl.ds(start, 256)]
        live = total > 0
        safe = jnp.where(live, total, 1.0)
        level = jnp.where(live, peak_ref[request, :, pl.ds(start, 256)] * LOG_2 + jnp.log(safe), NEGATIVE)
        inverse = jnp.where(live, 1.0 / safe, 0.0)
        for pair in range(pairs):
            block = jnp.concatenate(
                [
                    acc_ref[request, 128 * pair + 64 * side : 128 * pair + 64 * side + 64, pl.ds(start, 256)]
                    * inverse[2 * pair + side : 2 * pair + side + 1]
                    for side in range(2)
                ],
                axis=0,
            )
            out_ref[place, 128 * pair : 128 * pair + 128] = block.T.astype(jnp.bfloat16)
        high = level.astype(jnp.bfloat16).astype(jnp.float32)
        middle = (level - high).astype(jnp.bfloat16).astype(jnp.float32)
        low = level - high - middle
        heads = level.shape[0]
        filler = jnp.zeros((128 - 3 * heads, 256), jnp.float32)
        stacked = jnp.concatenate([high, middle, low, filler], axis=0)
        out_ref[place, features : features + 128] = stacked.T.astype(jnp.bfloat16)
        return 0

    lax.fori_loop(0, request_count * (span // 256), close, 0)


def attend(pages, table, bias, queries, ids, new_pairs, cache_ids, kv_cache):
    request_count = pages.shape[0]
    pairs, rows, _ = queries.shape
    features = 128 * pairs
    span = rows // request_count
    slot_count, page_rows, _ = kv_cache.shape
    heads = bias.shape[1]
    smem = pl.BlockSpec(memory_space=pltpu.SMEM)
    vmem = pl.BlockSpec(memory_space=pltpu.VMEM)
    return pl.pallas_call(
        attend_kernel,
        out_shape=(
            jax.ShapeDtypeStruct((rows, features + 128), jnp.bfloat16),
            jax.ShapeDtypeStruct(new_pairs.shape, jnp.bfloat16),
        ),
        in_specs=[smem, smem, smem, vmem, vmem, vmem, vmem, pl.BlockSpec(memory_space=pl.ANY)],
        out_specs=(vmem, vmem),
        scratch_shapes=[
            pltpu.VMEM(kv_cache.shape, jnp.bfloat16),
            pltpu.VMEM((features // 128, 144, 2 * page_rows), jnp.bfloat16),
            pltpu.VMEM((request_count, features, span), jnp.float32),
            pltpu.VMEM((request_count, heads, span), jnp.float32),
            pltpu.VMEM((request_count, heads, span), jnp.float32),
            pltpu.VMEM((rows, 128), jnp.bfloat16),
            pltpu.VMEM((2, heads, 128), jnp.float32),
            pltpu.SMEM((slot_count,), jnp.int32),
            pltpu.SemaphoreType.DMA((slot_count,)),
        ],
        compiler_params=pltpu.CompilerParams(vmem_limit_bytes=56 * 1024 * 1024),
        cost_estimate=pl.CostEstimate(
            flops=4 * slot_count * page_rows * span * features * 4,
            bytes_accessed=kv_cache.size * 2 + rows * features * 4,
            transcendentals=slot_count * page_rows * span * heads,
        ),
    )(pages, table, bias, queries, ids.reshape(request_count, 1, span), new_pairs, cache_ids, kv_cache)


def remote(source, target, send_sem, recv_sem, where):
    return pltpu.make_async_remote_copy(
        src_ref=source,
        dst_ref=target,
        send_sem=send_sem,
        recv_sem=recv_sem,
        device_id=where,
        device_id_type=pl.DeviceIdType.MESH,
    )


def greet(places):
    barrier = pltpu.get_barrier_semaphore()
    for place in places:
        pl.semaphore_signal(barrier, inc=1, device_id=place, device_id_type=pl.DeviceIdType.MESH)
    return lambda: pl.semaphore_wait(barrier, len(places))


def project_kernel(
    pages_ref, freq_ref, tokens_ref, gain_ref, wq_ref, wkv_ref, wo_ref, wh_ref,
    q_out, app_out, wo_out, wh_out,
    tok, wkv, wq, kv_stage, wh_all, cos_ref, sin_ref,
    tok_far, tok_near, tok_recv,
    w_far, w_near, w_recv,
    wq_far, wq_near, wq_recv, wqx_send, wqx_recv, wqc_send, wqc_recv,
    wo_far, wo_near, wo_recv, wox_send, wox_recv,
    wh_far, wh_near, wh_recv,
    kv_send, kv_recv, local_sem,
):
    _, planes, own_rows, features = tok.shape
    holders = 2 * planes
    req_count, deep, joined = wkv.shape
    req_pairs = req_count // 2
    request_count = pages_ref.shape[0]
    rows = holders * own_rows
    span = rows // request_count
    me = lax.axis_index("pg")
    mine = lax.axis_index("req")
    zz, yy = me // 2, me % 2
    other = 1 - yy
    xx, cc = mine // 2, mine % 2
    core_place = {"req": 2 * xx + 1 - cc}
    near_place = {"pg": 2 * zz + other}

    def plane(step):
        return (zz + step) % planes

    def far_place(step):
        return {"pg": 2 * plane(step) + yy}

    def req_far(step):
        return (xx + step) % req_pairs

    def x_place(step):
        return {"req": 2 * req_far(step) + cc}

    places = [{"pg": (me + step) % holders} for step in range(1, holders)]
    places += [x_place(step) for step in range(1, req_pairs)] + [core_place]
    arrived = greet(places)

    def columns(holder):
        return pl.ds(pl.multiple_of(holder * 128, 128), 128)

    keeps = [
        pltpu.make_async_copy(wq_ref, wq.at[xx, cc, :, columns(me)], local_sem.at[0]),
        pltpu.make_async_copy(wo_ref, wo_out.at[xx, :, columns(me)], local_sem.at[1]),
    ]
    for keep in keeps:
        keep.start()

    wide = tokens_ref[...].astype(jnp.float32)
    power = jnp.mean(wide * wide, axis=-1, keepdims=True)
    tok[yy, zz] = (wide * lax.rsqrt(power + EPSILON) * gain_ref[...]).astype(jnp.bfloat16)
    wkv[mine] = wkv_ref[...]
    head_cols = wh_ref.shape[0]
    packs = 128 // head_cols
    slab = deep // packs
    wh_wide = wh_ref[...].astype(jnp.float32).T
    wh_all[me] = jnp.concatenate(
        [wh_wide[slab * pack : slab * pack + slab] for pack in range(packs)], axis=1
    ).astype(jnp.bfloat16)
    for keep in keeps:
        keep.wait()
    arrived()

    started = []

    def begin(copy):
        copy.start()
        started.append(copy)

    def wq_copy(holder, send_sem, place):
        part = wq.at[xx, cc, :, columns(holder)]
        return remote(part, part, send_sem, wq_recv.at[holder], place)

    def wq_over(depth, holder, step, place):
        part = wq.at[depth, cc, :, columns(holder)]
        return remote(part, part, wqx_send.at[step, holder], wqx_recv.at[depth, holder], place)

    def wq_pass(side, holder):
        part = wq.at[:, side, :, columns(holder)]
        return remote(part, part, wqc_send.at[holder], wqc_recv.at[holder], core_place)

    def spread_x(holder):
        for step in range(1, req_pairs):
            begin(wq_over(xx, holder, step, x_place(step)))

    def pass_core(holder):
        for step in range(1, req_pairs):
            wq_over(req_far(step), holder, step, core_place).wait_recv()
        begin(wq_pass(cc, holder))

    def tok_copy(side, depth, send_sem, place):
        return remote(
            tok.at[side, depth], tok.at[side, depth], send_sem, tok_recv.at[side, depth], place
        )

    def w_copy(block, send_sem, place):
        return remote(wkv.at[block], wkv.at[block], send_sem, w_recv.at[block], place)

    for step in range(1, planes):
        begin(wq_copy(me, wq_far.at[step], far_place(step)))
        begin(tok_copy(yy, zz, tok_far.at[step], far_place(step)))
    begin(wq_copy(me, wq_near.at[0], near_place))
    begin(tok_copy(yy, zz, tok_near.at[0], near_place))
    for step in range(1, req_pairs):
        begin(w_copy(mine, w_far.at[step], x_place(step)))
    begin(w_copy(mine, w_near.at[0], core_place))
    spread_x(me)

    row = lax.broadcasted_iota(jnp.int32, (1, rows), 1)
    held = jnp.zeros((1, rows), jnp.int32)
    for request in range(request_count):
        held = jnp.where(row // span == request, pages_ref[request], held)
    position = (held * PAGE + row % span).astype(jnp.float32)
    angle = freq_ref[...] * position
    cosine, sine = jnp.cos(angle), jnp.sin(angle)
    cos_ref[...] = jnp.concatenate([cosine] * 4, axis=0).T.reshape(cos_ref.shape)
    sin_ref[...] = jnp.concatenate([-sine, sine, -sine, sine], axis=0).T.reshape(sin_ref.shape)

    for step in range(1, req_pairs):
        block = 2 * req_far(step) + cc
        w_copy(block, w_far.at[step], core_place).wait_recv()
        begin(w_copy(block, w_near.at[step], core_place))
    for step in range(1, planes):
        holder = 2 * plane(step) + yy
        wq_copy(holder, wq_far.at[step], near_place).wait_recv()
        begin(wq_copy(holder, wq_near.at[step], near_place))
        spread_x(holder)
        tok_copy(yy, plane(step), tok_far.at[step], near_place).wait_recv()
        begin(tok_copy(yy, plane(step), tok_near.at[step], near_place))

    def wo_copy(holder, send_sem, place):
        part = wo_out.at[xx, :, columns(holder)]
        return remote(part, part, send_sem, wo_recv.at[holder], place)

    def wo_over(depth, holder, step, place):
        part = wo_out.at[depth, :, columns(holder)]
        return remote(part, part, wox_send.at[step, holder], wox_recv.at[depth, holder], place)

    def wh_copy(holder, send_sem, place):
        return remote(wh_all.at[holder], wh_all.at[holder], send_sem, wh_recv.at[holder], place)

    for step in range(1, planes):
        begin(wo_copy(me, wo_far.at[step], far_place(step)))
        begin(wh_copy(me, wh_far.at[step], far_place(step)))
    begin(wo_copy(me, wo_near.at[0], near_place))
    begin(wh_copy(me, wh_near.at[0], near_place))

    def wo_spread(holder):
        for step in range(1, req_pairs):
            begin(wo_over(xx, holder, step, x_place(step)))

    for step in range(req_pairs):
        block = 2 * req_far(step) + 1 - cc
        w_copy(block, w_near.at[step], core_place).wait_recv()

    def kv_copy(source, side, depth, send_sem, place):
        start = pl.multiple_of(source * 256, 256)
        return remote(
            kv_stage.at[depth, side], app_out.at[:, pl.ds(start, 256)], send_sem,
            kv_recv.at[source], place,
        )

    half_rows = planes * own_rows
    lane = lax.broadcasted_iota(jnp.int32, (half_rows, 128), 1)
    front = (lane % 64) < 32
    is_key = (jnp.zeros((half_rows, 128), jnp.int32) + me) < planes

    def turned(value, cosine, sine):
        value = value.astype(jnp.bfloat16).astype(jnp.float32)
        swapped = jnp.where(front, pltpu.roll(value, 96, 1), pltpu.roll(value, 32, 1))
        return (value * cosine + swapped * sine).astype(jnp.bfloat16)

    def half(turn):
        side = yy if turn == 0 else other
        made = jnp.dot(
            tok[side].reshape(half_rows, features),
            wkv[...].reshape(features, joined),
            preferred_element_type=jnp.float32,
        )
        key_cos = jnp.where(is_key, cos_ref[:, side].reshape(half_rows, 128), 1.0)
        key_sin = jnp.where(is_key, sin_ref[:, side].reshape(half_rows, 128), 0.0)
        for part in range(joined // 128):
            piece = turned(made[:, 128 * part : 128 * part + 128], key_cos, key_sin)
            kv_stage[:, side, :, 128 * part : 128 * part + 128] = piece.reshape(
                planes, own_rows, 128
            )
        for step in range(0 if turn == 1 else 1, planes):
            place = {"pg": 2 * plane(step) + side}
            begin(kv_copy(me, side, plane(step), kv_send.at[turn, step], place))

    half(0)
    own_keep = pltpu.make_async_copy(
        kv_stage.at[zz, yy],
        app_out.at[:, pl.ds(pl.multiple_of(me * 256, 256), 256)],
        local_sem.at[2],
    )
    own_keep.start()
    for step in range(planes):
        holder = 2 * plane(step) + other
        wq_copy(holder, wq_near.at[step], near_place).wait_recv()
        spread_x(holder)
    for step in range(planes):
        pass_core(2 * plane(step) + yy)
    for step in range(planes):
        tok_copy(other, plane(step), tok_near.at[step], near_place).wait_recv()
    half(1)
    for step in range(1, planes):
        holder = 2 * plane(step) + yy
        wh_copy(holder, wh_far.at[step], near_place).wait_recv()
        begin(wh_copy(holder, wh_near.at[step], near_place))
        wo_copy(holder, wo_far.at[step], near_place).wait_recv()
        begin(wo_copy(holder, wo_near.at[step], near_place))
        wo_spread(holder)
    wo_spread(me)
    for step in range(planes):
        pass_core(2 * plane(step) + other)

    for step in range(planes):
        depth = plane(step)
        for side in range(2):
            wq_pass(1 - cc, 2 * depth + side).wait_recv()
        start = pl.multiple_of(depth * 256, 256)
        weight = wq[:, :, :, pl.ds(start, 256)].reshape(features, 256)
        for side in range(2):
            made = jnp.dot(
                tok[side].reshape(half_rows, features), weight, preferred_element_type=jnp.float32
            )
            cosine = cos_ref[:, side].reshape(half_rows, 128)
            sine = sin_ref[:, side].reshape(half_rows, 128)
            for part in range(2):
                piece = turned(made[:, 128 * part : 128 * part + 128], cosine, sine)
                q_out[2 * depth + part, :, side] = piece.reshape(planes, own_rows, 128)

    for step in range(planes):
        wh_copy(2 * plane(step) + other, wh_near.at[step], near_place).wait_recv()
    for pack in range(packs):
        wh_out[slab * pack : slab * pack + slab, :] = jnp.concatenate(
            [
                wh_all[holder].astype(jnp.float32)[:, head_cols * pack : head_cols * pack + head_cols]
                for holder in range(holders)
            ],
            axis=1,
        ).astype(jnp.bfloat16)
    for step in range(1, holders):
        kv_copy((me + step) % holders, yy, zz, kv_send.at[0, 0], near_place).wait_recv()
    own_keep.wait()
    for step in range(planes):
        wo_copy(2 * plane(step) + other, wo_near.at[step], near_place).wait_recv()
        for turn in range(1, req_pairs):
            wo_over(req_far(turn), 2 * plane(step) + yy, turn, core_place).wait_recv()
    for copy in started:
        copy.wait_send()


def project(pages, freqs, tokens, gain, w_query, w_keyval, w_out, w_head, holders, req_count):
    own_rows, features = tokens.shape
    planes = holders // 2
    deep = w_query.shape[0]
    vmem = pl.BlockSpec(memory_space=pltpu.VMEM)
    bf16 = jnp.bfloat16
    dma = pltpu.SemaphoreType.DMA
    pairs = req_count // 2
    return pl.pallas_call(
        project_kernel,
        out_shape=(
            jax.ShapeDtypeStruct((holders, planes, 2, own_rows, 128), bf16),
            jax.ShapeDtypeStruct((own_rows, 2 * features), bf16),
            jax.ShapeDtypeStruct((pairs, deep, features), bf16),
            jax.ShapeDtypeStruct((deep, holders * w_head.shape[0]), bf16),
        ),
        in_specs=[pl.BlockSpec(memory_space=pltpu.SMEM)] + [vmem] * 7,
        out_specs=(vmem, vmem, vmem, vmem),
        scratch_shapes=[
            pltpu.VMEM((2, planes, own_rows, features), bf16),
            pltpu.VMEM((req_count, deep, w_keyval.shape[1]), bf16),
            pltpu.VMEM((pairs, 2, deep, features), bf16),
            pltpu.VMEM((planes, 2, own_rows, 256), bf16),
            pltpu.VMEM((holders, deep * w_head.shape[0] // 128, 128), bf16),
            pltpu.VMEM((planes, 2, own_rows, 128), jnp.float32),
            pltpu.VMEM((planes, 2, own_rows, 128), jnp.float32),
            dma((planes,)), dma((planes,)), dma((2, planes)),
            dma((pairs,)), dma((pairs,)), dma((req_count,)),
            dma((planes,)), dma((planes,)), dma((holders,)),
            dma((pairs, holders)), dma((pairs, holders)), dma((holders,)), dma((holders,)),
            dma((planes,)), dma((planes,)), dma((holders,)),
            dma((pairs, holders)), dma((pairs, holders)),
            dma((planes,)), dma((planes,)), dma((holders,)),
            dma((2, planes)), dma((holders,)), dma((3,)),
        ],
        compiler_params=pltpu.CompilerParams(
            collective_id=0, has_side_effects=True, vmem_limit_bytes=56 * 1024 * 1024
        ),
        cost_estimate=pl.CostEstimate(
            flops=2 * holders * own_rows * features * (features + w_keyval.shape[1]),
            bytes_accessed=features * features * 6,
            transcendentals=0,
        ),
    )(pages, freqs, tokens, gain.reshape(1, features), w_query, w_keyval, w_out, w_head)


def expander(features, head_width):
    head = lax.broadcasted_iota(jnp.int32, (128, features), 0)
    column = lax.broadcasted_iota(jnp.int32, (128, features), 1)
    return jnp.where(column // head_width == head, 1.0, 0.0).astype(jnp.bfloat16)


def join_parts(parts, spread, features, head_count):
    levels = []
    for part in parts:
        coded = part[:, features:].astype(jnp.float32)
        levels.append(
            coded
            + pltpu.roll(coded, 128 - head_count, 1)
            + pltpu.roll(coded, 128 - 2 * head_count, 1)
        )
    top = functools.reduce(jnp.maximum, levels)
    shares = [jnp.exp(level - top) for level in levels]
    total = functools.reduce(jnp.add, shares)
    joined = None
    for part, share in zip(parts, shares):
        share = share / total
        high = share.astype(jnp.bfloat16)
        low = (share - high.astype(jnp.float32)).astype(jnp.bfloat16)
        wide = jnp.dot(high, spread, preferred_element_type=jnp.float32) + jnp.dot(
            low, spread, preferred_element_type=jnp.float32
        )
        term = part[:, :features].astype(jnp.float32) * wide
        joined = term if joined is None else joined + term
    return joined, top + jnp.log(total)


def close_kernel(
    parts_ref, tokens_ref, gain_ref, wo_ref, wh_ref,
    hidden_ref, logits_ref, stats_out,
    near_buf, send_buf, far_buf, stat_buf, spread_ref, wo_all, wh_all,
    wo_near, wo_recv, wox_send, wox_recv, wop_send, wop_recv, keep_sem, wh_far, wh_near, wh_recv,
    near_send, near_recv, far_send, far_recv, stat_send, stat_recv,
    *, head_count, request_count,
):
    planes, _, own_rows, coded = parts_ref.shape
    holders = 2 * planes
    features = coded - 128
    me = lax.axis_index("pg")
    zz, yy = me // 2, me % 2
    other = 1 - yy
    near_place = {"pg": 2 * zz + other}
    req_pairs = wo_all.shape[0]
    block = 128
    planes_out = features // (2 * block)
    mine = lax.axis_index("req")
    xx, cc = mine // 2, mine % 2
    core_place = {"req": 2 * xx + 1 - cc}

    def req_far(step):
        return (xx + step) % req_pairs

    arrived = greet(
        [{"pg": (me + step) % holders} for step in range(1, holders)]
        + [{"req": 2 * req_far(step) + cc} for step in range(1, req_pairs)]
        + [core_place]
    )
    def columns(depth, side):
        return pl.ds(pl.multiple_of((2 * depth + side) * block, block), block)

    keeps = [pltpu.make_async_copy(wo_ref.at[xx], wo_all.at[xx, cc], keep_sem.at[0, 0])]
    for step in range(1, req_pairs):
        far = req_far(step)
        for depth in range(planes_out):
            keeps.append(
                pltpu.make_async_copy(
                    wo_ref.at[far, :, columns(depth, yy)],
                    wo_all.at[far, cc, :, columns(depth, yy)],
                    keep_sem.at[step, depth],
                )
            )
    for keep in keeps:
        keep.start()
    wh_all[xx, cc] = wh_ref[...]
    spread_ref[...] = expander(features, features // head_count)
    arrived()
    order = list(range(1, planes)) + [0]
    started = []

    def near_copy(depth, step):
        return remote(
            parts_ref.at[depth, other], near_buf.at[depth], near_send.at[step],
            near_recv.at[depth], near_place,
        )

    for step in order:
        copy = near_copy((zz + step) % planes, step)
        copy.start()
        started.append(copy)

    def wo_copy(depth, side, send_sem, place):
        part = wo_all.at[depth, side]
        return remote(part, part, send_sem, wo_recv.at[depth, side], place)

    def wo_over(depth, step, column, place):
        part = wo_all.at[depth, cc, :, columns(column, other)]
        return remote(part, part, wox_send.at[step, column], wox_recv.at[depth, column], place)

    def wo_pass(depth, side, late, step, column):
        part = wo_all.at[depth, side, :, columns(column, other if late else yy)]
        return remote(
            part, part, wop_send.at[late, step, column], wop_recv.at[late, depth, column], core_place
        )

    def wh_copy(depth, side, send_sem, place):
        part = wh_all.at[depth, side]
        return remote(part, part, send_sem, wh_recv.at[depth, side], place)

    for step in range(1, req_pairs):
        place = {"req": 2 * req_far(step) + cc}
        started += [wo_over(xx, step, column, place) for column in range(planes_out)]
        started.append(wh_copy(xx, cc, wh_far.at[step], place))
    started += [
        wo_copy(xx, cc, wo_near.at[0], core_place), wh_copy(xx, cc, wh_near.at[0], core_place)
    ]
    for step in range(1, req_pairs):
        started += [wo_pass(req_far(step), cc, 0, step, column) for column in range(planes_out)]
    for keep in keeps:
        keep.wait()
    for copy in started[planes:]:
        copy.start()

    def pass_on():
        for step in range(1, req_pairs):
            depth = req_far(step)
            copies = [wh_copy(depth, cc, wh_near.at[step], core_place)]
            for column in range(planes_out):
                wo_over(depth, step, column, core_place).wait_recv()
                copies.append(wo_pass(depth, cc, 1, step, column))
            wh_copy(depth, cc, wh_far.at[step], core_place).wait_recv()
            for copy in copies:
                copy.start()
                started.append(copy)

    lane = lax.broadcasted_iota(jnp.int32, (own_rows, 128), 1)
    for step in order:
        depth = (zz + step) % planes
        if step == 0:
            pass_on()
        near_copy(depth, step).wait_recv()
        joined, level = join_parts(
            [parts_ref[depth, yy], near_buf[depth]], spread_ref[...], features, head_count
        )
        level = jnp.where(lane < head_count, level, 0.0)
        high = level.astype(jnp.bfloat16).astype(jnp.float32)
        middle = (level - high).astype(jnp.bfloat16).astype(jnp.float32)
        low = level - high - middle
        code = high + pltpu.roll(middle, head_count, 1) + pltpu.roll(low, 2 * head_count, 1)
        if step == 0:
            far_buf[zz, :, :features] = joined.astype(jnp.bfloat16)
            far_buf[zz, :, features:] = code.astype(jnp.bfloat16)
        else:
            send_buf[step, :, :features] = joined.astype(jnp.bfloat16)
            send_buf[step, :, features:] = code.astype(jnp.bfloat16)
            copy = remote(
                send_buf.at[step], far_buf.at[zz], far_send.at[step], far_recv.at[zz],
                {"pg": 2 * depth + yy},
            )
            copy.start()
            started.append(copy)
    for step in range(1, planes):
        depth = (zz + step) % planes
        remote(
            send_buf.at[step], far_buf.at[depth], far_send.at[step], far_recv.at[depth], near_place
        ).wait_recv()
    joined, _ = join_parts(
        [far_buf[depth] for depth in range(planes)], spread_ref[...], features, head_count
    )
    attention = joined.astype(jnp.bfloat16)
    for step in range(req_pairs):
        if step == 0:
            wo_copy(xx, 1 - cc, wo_near.at[0], core_place).wait_recv()
        else:
            for late in range(2):
                for column in range(planes_out):
                    wo_pass(req_far(step), 1 - cc, late, step, column).wait_recv()
        wh_copy(req_far(step), 1 - cc, wh_near.at[step], core_place).wait_recv()
    out_weight = wo_all[...].reshape(features, features)
    head_weight = wh_all[...].reshape(features, wh_ref.shape[1])
    hidden = (
        tokens_ref[...].astype(jnp.float32)
        + jnp.dot(attention, out_weight, preferred_element_type=jnp.float32)
    ).astype(jnp.bfloat16)
    hidden_ref[...] = hidden
    wide = hidden.astype(jnp.float32)
    squares = wide * wide
    power = jnp.mean(squares, axis=-1, keepdims=True)
    head_in = (wide * lax.rsqrt(power + EPSILON) * gain_ref[...]).astype(jnp.bfloat16)
    logits = jnp.dot(head_in, head_weight, preferred_element_type=jnp.float32)
    logits_ref[...] = logits.astype(jnp.bfloat16)
    energy = jnp.sum(jnp.sum(squares, axis=1, keepdims=True), axis=0, keepdims=True)
    peak = jnp.max(jnp.max(logits, axis=1, keepdims=True), axis=0, keepdims=True)
    is_first = lax.broadcasted_iota(jnp.int32, (8, 128), 0) == 0
    stat_buf[me] = jnp.where(
        is_first, jnp.broadcast_to(energy, (8, 128)), jnp.broadcast_to(peak, (8, 128))
    )
    for step in range(1, holders):
        copy = remote(
            stat_buf.at[me], stat_buf.at[me], stat_send.at[step], stat_recv.at[me],
            {"pg": (me + step) % holders},
        )
        copy.start()
        started.append(copy)
    for step in range(1, holders):
        source = (me + step) % holders
        remote(
            stat_buf.at[source], stat_buf.at[source], stat_send.at[step], stat_recv.at[source],
            near_place,
        ).wait_recv()
    every = holders // request_count
    for request in range(request_count):
        mine = [stat_buf[every * request + block] for block in range(every)]
        total = functools.reduce(jnp.add, mine)
        top = functools.reduce(jnp.maximum, mine)
        stats_out[request] = jnp.where(is_first, jnp.sqrt(total), top)
    for copy in started:
        copy.wait_send()


def close(parts, tokens, gain, wo, wh, head_count, request_count, holders):
    own_rows, features = tokens.shape
    planes = holders // 2
    coded = features + 128
    pairs = wo.shape[0]
    planes_out = features // 256
    vmem = pl.BlockSpec(memory_space=pltpu.VMEM)
    bf16 = jnp.bfloat16
    dma = pltpu.SemaphoreType.DMA
    return pl.pallas_call(
        functools.partial(close_kernel, head_count=head_count, request_count=request_count),
        out_shape=(
            jax.ShapeDtypeStruct((own_rows, features), bf16),
            jax.ShapeDtypeStruct((own_rows, wh.shape[1]), bf16),
            jax.ShapeDtypeStruct((request_count, 8, 128), jnp.float32),
        ),
        in_specs=[vmem] * 5,
        out_specs=(vmem, vmem, vmem),
        scratch_shapes=[
            pltpu.VMEM((planes, own_rows, coded), bf16),
            pltpu.VMEM((planes, own_rows, coded), bf16),
            pltpu.VMEM((planes, own_rows, coded), bf16),
            pltpu.VMEM((holders, 8, 128), jnp.float32),
            pltpu.VMEM((128, features), bf16),
            pltpu.VMEM((pairs, 2) + wo.shape[1:], bf16),
            pltpu.VMEM((pairs, 2) + wh.shape, bf16),
            dma((pairs,)), dma((pairs, 2)), dma((pairs, planes_out)), dma((pairs, planes_out)),
            dma((2, pairs, planes_out)), dma((2, pairs, planes_out)), dma((pairs, planes_out)),
            dma((pairs,)), dma((pairs,)), dma((pairs, 2)),
            dma((planes,)), dma((planes,)), dma((planes,)), dma((planes,)),
            dma((holders,)), dma((holders,)),
        ],
        compiler_params=pltpu.CompilerParams(
            collective_id=1, has_side_effects=True, vmem_limit_bytes=56 * 1024 * 1024
        ),
        cost_estimate=pl.CostEstimate(
            flops=2 * own_rows * features * features,
            bytes_accessed=features * features * 4,
            transcendentals=0,
        ),
    )(parts.reshape(planes, 2, own_rows, coded), tokens, gain.reshape(1, features), wo, wh)

def project_plain(tokens, cache_pages, attn_gain, w_query, w_keyval, w_out, w_head, group_rows, head_count):
    own_rows, features = tokens.shape
    request_count = cache_pages.shape[0]
    span_rows = group_rows // request_count
    head_width = features // head_count
    first_row = lax.axis_index("pg") * own_rows
    normed = rms_norm(tokens, attn_gain)
    query_full, keyval_full = (
        lax.all_gather(w_query, "req", axis=0, tiled=True),
        lax.all_gather(w_keyval, "req", axis=0, tiled=True),
    )
    own_index = first_row + jnp.arange(own_rows, dtype=jnp.int32)
    own_positions = (
        lookup_small(cache_pages, own_index // span_rows, request_count) * PAGE
        + own_index % span_rows
    )
    own_cos, own_sin = rope_angles(own_positions, head_width // 2)
    query_cols = query_full.shape[1]
    joined = jnp.concatenate([query_full, keyval_full], axis=1)
    projected = jnp.dot(
        normed, lax.all_gather(joined, "pg", axis=1, tiled=True), preferred_element_type=jnp.float32
    )
    projected = projected.reshape(own_rows, -1, joined.shape[1])
    query_raw = projected[:, :, :query_cols].reshape(own_rows, features).astype(jnp.bfloat16)
    keyval_raw = projected[:, :, query_cols:].reshape(own_rows, 2 * features).astype(jnp.bfloat16)
    own_queries = rotate(query_raw, own_cos, own_sin, head_count)
    new_keys = rotate(keyval_raw[:, :features], own_cos, own_sin, head_count)
    new_values = keyval_raw[:, features:]
    appended = jnp.concatenate([new_keys, new_values], axis=1)
    queries = lax.all_gather(own_queries, "pg", axis=0, tiled=True)
    queries = queries.reshape(group_rows, features // 128, 128).transpose(1, 0, 2)
    out_slices = lax.all_gather(lax.all_gather(w_out, "pg", axis=1, tiled=True), "req")
    out_slices = out_slices.reshape(-1, 2, w_out.shape[0], features)
    return (
        queries,
        appended,
        lax.dynamic_index_in_dim(out_slices, lax.axis_index("req") % 2, 1, keepdims=False),
        lax.all_gather(w_head, "pg", axis=1, tiled=True),
    )


def per_device(
    tokens,
    variate_ids,
    cache_pages,
    page_table,
    kv_cache,
    cache_variates,
    attn_gain,
    w_query,
    w_keyval,
    w_out,
    variate_bias,
    head_gain,
    w_head,
):
    own_rows, features = tokens.shape
    request_count = cache_pages.shape[0]
    group_rows = variate_ids.shape[0]
    head_count = variate_bias.shape[1]
    holders = group_rows // own_rows
    half_width = features // head_count // 2
    req_count = features // w_query.shape[0]
    if w_query.shape[1] == 128 and w_keyval.shape[1] == 256:
        steps = np.arange(half_width, dtype=np.float32) / half_width
        freqs = np.exp(np.float32(-math.log(10000.0)) * steps).reshape(half_width, 1)
        queries, appended, out_rows, head_rows = project(
            cache_pages, freqs, tokens, attn_gain, w_query, w_keyval, w_out, w_head.T, holders, req_count
        )
        queries = queries.reshape(holders, group_rows, 128)
    else:
        queries, appended, out_rows, head_rows = project_plain(
            tokens, cache_pages, attn_gain, w_query, w_keyval, w_out, w_head, group_rows, head_count
        )
    partial_out, appended = attend(
        cache_pages, page_table, variate_bias, queries, variate_ids, appended, cache_variates, kv_cache
    )
    hidden, logits, stats = close(
        partial_out, tokens, head_gain, out_rows, head_rows, head_count, request_count, holders
    )
    hidden, logits, norms, peaks = hand_over(hidden, logits, stats)
    return (hidden, appended, logits, norms, peaks)


def hand_over_kernel(hidden_ref, logits_ref, stats_ref, hidden_out, logits_out, norm_out, peak_out):
    hidden_out[...] = hidden_ref[...]
    logits_out[...] = logits_ref[...]
    for request in range(stats_ref.shape[0]):
        norm_out[request] = stats_ref[request, 0, 0]
        peak_out[request] = stats_ref[request, 1, 0]


def hand_over(hidden, logits, stats):
    vmem = pl.BlockSpec(memory_space=pltpu.VMEM)
    smem = pl.BlockSpec(memory_space=pltpu.SMEM)
    scalars = jax.ShapeDtypeStruct((stats.shape[0],), jnp.float32)
    return pl.pallas_call(
        hand_over_kernel,
        out_shape=(
            jax.ShapeDtypeStruct(hidden.shape, hidden.dtype),
            jax.ShapeDtypeStruct(logits.shape, logits.dtype),
            scalars,
            scalars,
        ),
        in_specs=[vmem, vmem, smem],
        out_specs=(vmem, vmem, smem, smem),
    )(hidden, logits, stats)


def solution(mesh):
    placed = (
        P(("req", "pg"), None),
        P("req"),
        P("req"),
        P("req", None),
        P(("req", "pg"), None, None),
        P(("req", "pg"), None),
        P(),
        P("req", "pg"),
        P("req", "pg"),
        P("req", "pg"),
        P(),
        P(),
        P("req", "pg"),
    )
    return jax.shard_map(
        per_device,
        mesh=mesh,
        in_specs=placed,
        out_specs=(
            P(("req", "pg"), None),
            P(("req", "pg"), None),
            P(("req", "pg"), None),
            P("req"),
            P("req"),
        ),
        check_vma=False,
    )
```

```python
import functools
import math

import jax
import jax.numpy as jnp
import numpy as np
from jax import lax
from jax.experimental import pallas as pl
from jax.experimental.pallas import tpu as pltpu
from jax.sharding import PartitionSpec as P

PAGE = 128


EPSILON = 1e-05
NEGATIVE = -1e30
VARIATES = 4
LOG_2 = math.log(2.0)
SCALE = 0.125 / LOG_2


def rms_norm(values, gain):
    wide = values.astype(jnp.float32)
    power = jnp.mean(wide * wide, axis=-1, keepdims=True)
    return (wide * lax.rsqrt(power + EPSILON) * gain).astype(jnp.bfloat16)


def rope_angles(positions, half_width):
    steps = jnp.arange(half_width, dtype=jnp.float32) / half_width
    freqs = jnp.exp(-math.log(10000.0) * steps)
    angle = positions.astype(jnp.float32)[:, None] * freqs[None, :]
    return (jnp.cos(angle), jnp.sin(angle))


def rotate(values, cosine, sine_part, head_count):
    count = values.shape[0]
    halves = values.astype(jnp.float32).reshape(count, head_count, 2, -1)
    front_half = halves[:, :, 0, :]
    second = halves[:, :, 1, :]
    cosine_wide = cosine[:, None, :]
    sine_wide = sine_part[:, None, :]
    turned = jnp.stack(
        [
            front_half * cosine_wide - second * sine_wide,
            second * cosine_wide + front_half * sine_wide,
        ],
        axis=2,
    )
    return turned.reshape(count, -1).astype(jnp.bfloat16)


def lookup_small(table_rows, lookup_index, count):
    matches = lookup_index[:, None] == jnp.arange(count, dtype=jnp.int32)[None, :]
    return jnp.sum(jnp.where(matches, table_rows[None, :], 0), axis=1)


def attend_kernel(
    pages_ref, table_ref, bias_ref, q_ref, ids_ref, new_ref, cids_ref, kv_hbm,
    out_ref, app_ref, kv_buf, vt_buf, acc_ref, peak_ref, sum_ref, mark_ref, level_ref, owner_ref, sems,
):
    request_count, _, span = ids_ref.shape
    slot_count, page_rows, _ = kv_hbm.shape
    pairs = q_ref.shape[0]
    features = 128 * pairs
    own_rows = new_ref.shape[0]
    me = lax.axis_index("pg")

    def fetch(slot):
        return pltpu.make_async_copy(kv_hbm.at[slot], kv_buf.at[slot], sems.at[slot])

    for slot in range(slot_count):
        fetch(slot).start()

    app_ref[...] = new_ref[...]
    for slot in range(slot_count):
        owner_ref[slot] = -1

    for request in range(request_count):

        def look(page, _):
            slot = table_ref[request, page] - me * slot_count

            @pl.when((slot >= 0) & (slot < slot_count))
            def _():
                owner_ref[slot] = request

            return 0

        lax.fori_loop(0, pages_ref[request], look, 0)

    acc_ref[...] = jnp.zeros_like(acc_ref)
    sum_ref[...] = jnp.zeros_like(sum_ref)
    peak_ref[...] = jnp.full_like(peak_ref, NEGATIVE)

    wide_lane = lax.broadcasted_iota(jnp.int32, (128, 128), 1)
    term = lax.broadcasted_iota(jnp.int32, (1, 128), 1) // VARIATES
    for kind in range(2):
        for head in range(level_ref.shape[1]):
            whole = jnp.full((1, 128), bias_ref[kind, head]) * 8.0
            high = whole.astype(jnp.bfloat16).astype(jnp.float32)
            middle = (whole - high).astype(jnp.bfloat16).astype(jnp.float32)
            low = whole - high - middle
            level_ref[kind, head : head + 1, :] = jnp.where(
                term == 0, high, jnp.where(term == 1, middle, jnp.where(term == 2, low, 0.0))
            )

    def mark(flat, _):
        request = flat // (span // 128)
        start = pl.multiple_of((flat % (span // 128)) * 128, 128)
        column = jnp.broadcast_to(ids_ref[request, :, pl.ds(start, 128)], (128, 128)).T
        hit = (wide_lane % VARIATES == column) & (wide_lane < 3 * VARIATES)
        mark_ref[pl.ds(pl.multiple_of(flat * 128, 128), 128), :] = jnp.where(hit, 1.0, 0.0).astype(
            jnp.bfloat16
        )
        return 0

    lax.fori_loop(0, request_count * (span // 128), mark, 0)

    def absorb(request, k_of, v_of, key_ids, count, offset):
        lane = lax.broadcasted_iota(jnp.int32, (count, 128), 1)
        left = jnp.where(lane < 64, 1.0, 0.0).astype(jnp.bfloat16)
        right = jnp.where(lane < 64, 0.0, 1.0).astype(jnp.bfloat16)
        row = lax.broadcasted_iota(jnp.int32, (128, count), 0)
        ones_row = lax.broadcasted_iota(jnp.int32, (16, 2 * count), 0)
        ones_col = lax.broadcasted_iota(jnp.int32, (16, 2 * count), 1)
        same = lane % VARIATES == key_ids
        ones = jnp.where((ones_row < 8) == (ones_col < count), 1.0, 0.0).astype(jnp.bfloat16)
        for pair in range(pairs):
            value = v_of(pair).astype(jnp.float32).T
            vt_buf[pair, :128, 0:count] = jnp.where(row < 64, value, 0.0).astype(jnp.bfloat16)
            vt_buf[pair, :128, count : 2 * count] = jnp.where(row >= 64, value, 0.0).astype(
                jnp.bfloat16
            )
            vt_buf[pair, 128:, 0 : 2 * count] = ones

        def tile(index, _):
            start = pl.multiple_of(index * 256, 256)
            marks = mark_ref[pl.ds(pl.multiple_of(request * span + start, 256), 256), :]
            if offset is not None:
                allowed = (
                    lax.broadcasted_iota(jnp.int32, (count, 256), 0) + offset
                    <= lax.broadcasted_iota(jnp.int32, (count, 256), 1) + start
                )
            for pair in range(pairs):
                keys = k_of(pair)
                both = jnp.concatenate([keys * left, keys * right], axis=0)
                extra = jnp.concatenate(
                    [
                        jnp.where(
                            same, level_ref[0, head : head + 1, :], level_ref[1, head : head + 1, :]
                        ).astype(jnp.bfloat16)
                        for head in (2 * pair, 2 * pair + 1)
                    ],
                    axis=0,
                )
                query = q_ref[pair, pl.ds(request * span + start, 256), :]
                scores = lax.dot_general(
                    jnp.concatenate([both, extra], axis=1),
                    jnp.concatenate([query, marks], axis=1),
                    (((1,), (1,)), ((), ())), preferred_element_type=jnp.float32
                )
                weights, fades = [], []
                for side in range(2):
                    head = 2 * pair + side
                    part = scores[side * count : (side + 1) * count] * SCALE
                    if offset is not None:
                        part = jnp.where(allowed, part, NEGATIVE)
                    old = peak_ref[request, head : head + 1, pl.ds(start, 256)]
                    new = jnp.maximum(old, jnp.max(part, axis=0, keepdims=True))
                    peak_ref[request, head : head + 1, pl.ds(start, 256)] = new
                    weight = jnp.exp2(part - new)
                    if offset is not None:
                        weight = jnp.where(allowed, weight, 0.0)
                    weights.append(weight.astype(jnp.bfloat16))
                    fades.append(jnp.exp2(old - new))
                summed = jnp.dot(
                    vt_buf[pair, :, 0 : 2 * count],
                    jnp.concatenate(weights, axis=0),
                    preferred_element_type=jnp.float32,
                )
                for side in range(2):
                    head = 2 * pair + side
                    rows = slice(128 * pair + 64 * side, 128 * pair + 64 * side + 64)
                    acc_ref[request, rows, pl.ds(start, 256)] = (
                        acc_ref[request, rows, pl.ds(start, 256)] * fades[side]
                        + summed[64 * side : 64 * side + 64]
                    )
                    sum_ref[request, head : head + 1, pl.ds(start, 256)] = (
                        sum_ref[request, head : head + 1, pl.ds(start, 256)] * fades[side]
                        + summed[128 + 8 * side : 129 + 8 * side]
                    )
            return 0

        lax.fori_loop(0, span // 256, tile, 0)

    first_row = me * own_rows
    request_own = first_row // span
    offset = first_row % span
    chunk = pl.multiple_of((offset // 128) * 128, 128)
    wide_ids = ids_ref[request_own, :, pl.ds(chunk, 128)]
    column = jnp.broadcast_to(wide_ids, (128, 128)).T
    lower = offset - chunk
    own_ids = jnp.where(lower == 0, column[:own_rows], column[128 - own_rows :])
    absorb(
        request_own,
        lambda pair: new_ref[:, 128 * pair : 128 * pair + 128],
        lambda pair: new_ref[:, features + 128 * pair : features + 128 * pair + 128],
        own_ids,
        own_rows,
        offset,
    )

    def visit(slot, _):
        owner = owner_ref[slot]
        fetch(slot).wait()

        @pl.when(owner >= 0)
        def _():
            column = jnp.broadcast_to(cids_ref[pl.ds(slot, 1), :], (page_rows, 128)).T
            absorb(
                owner,
                lambda pair: kv_buf[slot, :, 128 * pair : 128 * pair + 128],
                lambda pair: kv_buf[slot, :, features + 128 * pair : features + 128 * pair + 128],
                column,
                page_rows,
                None,
            )

        return 0

    lax.fori_loop(0, slot_count, visit, 0)

    def close(flat, _):
        request = flat // (span // 256)
        start = pl.multiple_of((flat % (span // 256)) * 256, 256)
        place = pl.ds(pl.multiple_of(flat * 256, 256), 256)
        total = sum_ref[request, :, pl.ds(start, 256)]
        live = total > 0
        safe = jnp.where(live, total, 1.0)
        level = jnp.where(live, peak_ref[request, :, pl.ds(start, 256)] * LOG_2 + jnp.log(safe), NEGATIVE)
        inverse = jnp.where(live, 1.0 / safe, 0.0)
        for pair in range(pairs):
            block = jnp.concatenate(
                [
                    acc_ref[request, 128 * pair + 64 * side : 128 * pair + 64 * side + 64, pl.ds(start, 256)]
                    * inverse[2 * pair + side : 2 * pair + side + 1]
                    for side in range(2)
                ],
                axis=0,
            )
            out_ref[place, 128 * pair : 128 * pair + 128] = block.T.astype(jnp.bfloat16)
        high = level.astype(jnp.bfloat16).astype(jnp.float32)
        middle = (level - high).astype(jnp.bfloat16).astype(jnp.float32)
        low = level - high - middle
        heads = level.shape[0]
        filler = jnp.zeros((128 - 3 * heads, 256), jnp.float32)
        stacked = jnp.concatenate([high, middle, low, filler], axis=0)
        out_ref[place, features : features + 128] = stacked.T.astype(jnp.bfloat16)
        return 0

    lax.fori_loop(0, request_count * (span // 256), close, 0)


def attend(pages, table, bias, queries, ids, new_pairs, cache_ids, kv_cache):
    request_count = pages.shape[0]
    pairs, rows, _ = queries.shape
    features = 128 * pairs
    span = rows // request_count
    slot_count, page_rows, _ = kv_cache.shape
    heads = bias.shape[1]
    smem = pl.BlockSpec(memory_space=pltpu.SMEM)
    vmem = pl.BlockSpec(memory_space=pltpu.VMEM)
    return pl.pallas_call(
        attend_kernel,
        out_shape=(
            jax.ShapeDtypeStruct((rows, features + 128), jnp.bfloat16),
            jax.ShapeDtypeStruct(new_pairs.shape, jnp.bfloat16),
        ),
        in_specs=[smem, smem, smem, vmem, vmem, vmem, vmem, pl.BlockSpec(memory_space=pl.ANY)],
        out_specs=(vmem, vmem),
        scratch_shapes=[
            pltpu.VMEM(kv_cache.shape, jnp.bfloat16),
            pltpu.VMEM((features // 128, 144, 2 * page_rows), jnp.bfloat16),
            pltpu.VMEM((request_count, features, span), jnp.float32),
            pltpu.VMEM((request_count, heads, span), jnp.float32),
            pltpu.VMEM((request_count, heads, span), jnp.float32),
            pltpu.VMEM((rows, 128), jnp.bfloat16),
            pltpu.VMEM((2, heads, 128), jnp.float32),
            pltpu.SMEM((slot_count,), jnp.int32),
            pltpu.SemaphoreType.DMA((slot_count,)),
        ],
        compiler_params=pltpu.CompilerParams(vmem_limit_bytes=56 * 1024 * 1024),
        cost_estimate=pl.CostEstimate(
            flops=4 * slot_count * page_rows * span * features * 4,
            bytes_accessed=kv_cache.size * 2 + rows * features * 4,
            transcendentals=slot_count * page_rows * span * heads,
        ),
    )(pages, table, bias, queries, ids.reshape(request_count, 1, span), new_pairs, cache_ids, kv_cache)


def remote(source, target, send_sem, recv_sem, where):
    return pltpu.make_async_remote_copy(
        src_ref=source,
        dst_ref=target,
        send_sem=send_sem,
        recv_sem=recv_sem,
        device_id=where,
        device_id_type=pl.DeviceIdType.MESH,
    )


def greet(places):
    barrier = pltpu.get_barrier_semaphore()
    for place in places:
        pl.semaphore_signal(barrier, inc=1, device_id=place, device_id_type=pl.DeviceIdType.MESH)
    return lambda: pl.semaphore_wait(barrier, len(places))


def project_kernel(
    pages_ref, freq_ref, tokens_ref, gain_ref, wq_ref, wkv_ref, wo_ref, wh_ref,
    q_out, app_out, wo_out, wh_out,
    tok, wkv, wq, kv_stage, wh_all, cos_ref, sin_ref,
    tok_far, tok_near, tok_recv,
    w_far, w_near, w_recv,
    wq_far, wq_near, wq_recv, wqx_send, wqx_recv, wqc_send, wqc_recv,
    wo_far, wo_near, wo_recv, wox_send, wox_recv,
    wh_far, wh_near, wh_recv,
    kv_send, kv_recv, local_sem,
):
    _, planes, own_rows, features = tok.shape
    holders = 2 * planes
    req_count, deep, joined = wkv.shape
    req_pairs = req_count // 2
    request_count = pages_ref.shape[0]
    rows = holders * own_rows
    span = rows // request_count
    me = lax.axis_index("pg")
    mine = lax.axis_index("req")
    zz, yy = me // 2, me % 2
    other = 1 - yy
    xx, cc = mine // 2, mine % 2
    core_place = {"req": 2 * xx + 1 - cc}
    near_place = {"pg": 2 * zz + other}

    def plane(step):
        return (zz + step) % planes

    def far_place(step):
        return {"pg": 2 * plane(step) + yy}

    def req_far(step):
        return (xx + step) % req_pairs

    def x_place(step):
        return {"req": 2 * req_far(step) + cc}

    places = [{"pg": (me + step) % holders} for step in range(1, holders)]
    places += [x_place(step) for step in range(1, req_pairs)] + [core_place]
    arrived = greet(places)

    def columns(holder):
        return pl.ds(pl.multiple_of(holder * 128, 128), 128)

    keeps = [
        pltpu.make_async_copy(wq_ref, wq.at[xx, cc, :, columns(me)], local_sem.at[0]),
        pltpu.make_async_copy(wo_ref, wo_out.at[xx, :, columns(me)], local_sem.at[1]),
    ]
    for keep in keeps:
        keep.start()

    wide = tokens_ref[...].astype(jnp.float32)
    power = jnp.mean(wide * wide, axis=-1, keepdims=True)
    tok[yy, zz] = (wide * lax.rsqrt(power + EPSILON) * gain_ref[...]).astype(jnp.bfloat16)
    wkv[mine] = wkv_ref[...]
    head_cols = wh_ref.shape[0]
    packs = 128 // head_cols
    slab = deep // packs
    wh_wide = wh_ref[...].astype(jnp.float32).T
    wh_all[me] = jnp.concatenate(
        [wh_wide[slab * pack : slab * pack + slab] for pack in range(packs)], axis=1
    ).astype(jnp.bfloat16)
    for keep in keeps:
        keep.wait()
    arrived()

    started = []

    def begin(copy):
        copy.start()
        started.append(copy)

    def wq_copy(holder, send_sem, place):
        part = wq.at[xx, cc, :, columns(holder)]
        return remote(part, part, send_sem, wq_recv.at[holder], place)

    def wq_over(depth, holder, step, place):
        part = wq.at[depth, cc, :, columns(holder)]
        return remote(part, part, wqx_send.at[step, holder], wqx_recv.at[depth, holder], place)

    def wq_pass(side, holder):
        part = wq.at[:, side, :, columns(holder)]
        return remote(part, part, wqc_send.at[holder], wqc_recv.at[holder], core_place)

    def spread_x(holder):
        for step in range(1, req_pairs):
            begin(wq_over(xx, holder, step, x_place(step)))

    def pass_core(holder):
        for step in range(1, req_pairs):
            wq_over(req_far(step), holder, step, core_place).wait_recv()
        begin(wq_pass(cc, holder))

    def tok_copy(side, depth, send_sem, place):
        return remote(
            tok.at[side, depth], tok.at[side, depth], send_sem, tok_recv.at[side, depth], place
        )

    def w_copy(block, send_sem, place):
        return remote(wkv.at[block], wkv.at[block], send_sem, w_recv.at[block], place)

    for step in range(1, planes):
        begin(wq_copy(me, wq_far.at[step], far_place(step)))
        begin(tok_copy(yy, zz, tok_far.at[step], far_place(step)))
    begin(wq_copy(me, wq_near.at[0], near_place))
    begin(tok_copy(yy, zz, tok_near.at[0], near_place))
    for step in range(1, req_pairs):
        begin(w_copy(mine, w_far.at[step], x_place(step)))
    begin(w_copy(mine, w_near.at[0], core_place))
    spread_x(me)

    row = lax.broadcasted_iota(jnp.int32, (1, rows), 1)
    held = jnp.zeros((1, rows), jnp.int32)
    for request in range(request_count):
        held = jnp.where(row // span == request, pages_ref[request], held)
    position = (held * PAGE + row % span).astype(jnp.float32)
    angle = freq_ref[...] * position
    cosine, sine = jnp.cos(angle), jnp.sin(angle)
    cos_ref[...] = jnp.concatenate([cosine] * 4, axis=0).T.reshape(cos_ref.shape)
    sin_ref[...] = jnp.concatenate([-sine, sine, -sine, sine], axis=0).T.reshape(sin_ref.shape)

    for step in range(1, req_pairs):
        block = 2 * req_far(step) + cc
        w_copy(block, w_far.at[step], core_place).wait_recv()
        begin(w_copy(block, w_near.at[step], core_place))
    for step in range(1, planes):
        holder = 2 * plane(step) + yy
        wq_copy(holder, wq_far.at[step], near_place).wait_recv()
        begin(wq_copy(holder, wq_near.at[step], near_place))
        spread_x(holder)
        tok_copy(yy, plane(step), tok_far.at[step], near_place).wait_recv()
        begin(tok_copy(yy, plane(step), tok_near.at[step], near_place))

    def wo_copy(holder, send_sem, place):
        part = wo_out.at[xx, :, columns(holder)]
        return remote(part, part, send_sem, wo_recv.at[holder], place)

    def wo_over(depth, holder, step, place):
        part = wo_out.at[depth, :, columns(holder)]
        return remote(part, part, wox_send.at[step, holder], wox_recv.at[depth, holder], place)

    def wh_copy(holder, send_sem, place):
        return remote(wh_all.at[holder], wh_all.at[holder], send_sem, wh_recv.at[holder], place)

    for step in range(1, planes):
        begin(wo_copy(me, wo_far.at[step], far_place(step)))
        begin(wh_copy(me, wh_far.at[step], far_place(step)))
    begin(wo_copy(me, wo_near.at[0], near_place))
    begin(wh_copy(me, wh_near.at[0], near_place))

    def wo_spread(holder):
        for step in range(1, req_pairs):
            begin(wo_over(xx, holder, step, x_place(step)))

    for step in range(req_pairs):
        block = 2 * req_far(step) + 1 - cc
        w_copy(block, w_near.at[step], core_place).wait_recv()

    def kv_copy(source, side, depth, send_sem, place):
        start = pl.multiple_of(source * 256, 256)
        return remote(
            kv_stage.at[depth, side], app_out.at[:, pl.ds(start, 256)], send_sem,
            kv_recv.at[source], place,
        )

    half_rows = planes * own_rows
    lane = lax.broadcasted_iota(jnp.int32, (half_rows, 128), 1)
    front = (lane % 64) < 32
    is_key = (jnp.zeros((half_rows, 128), jnp.int32) + me) < planes

    def turned(value, cosine, sine):
        value = value.astype(jnp.bfloat16).astype(jnp.float32)
        swapped = jnp.where(front, pltpu.roll(value, 96, 1), pltpu.roll(value, 32, 1))
        return (value * cosine + swapped * sine).astype(jnp.bfloat16)

    def half(turn):
        side = yy if turn == 0 else other
        made = jnp.dot(
            tok[side].reshape(half_rows, features),
            wkv[...].reshape(features, joined),
            preferred_element_type=jnp.float32,
        )
        key_cos = jnp.where(is_key, cos_ref[:, side].reshape(half_rows, 128), 1.0)
        key_sin = jnp.where(is_key, sin_ref[:, side].reshape(half_rows, 128), 0.0)
        for part in range(joined // 128):
            piece = turned(made[:, 128 * part : 128 * part + 128], key_cos, key_sin)
            kv_stage[:, side, :, 128 * part : 128 * part + 128] = piece.reshape(
                planes, own_rows, 128
            )
        for step in range(0 if turn == 1 else 1, planes):
            place = {"pg": 2 * plane(step) + side}
            begin(kv_copy(me, side, plane(step), kv_send.at[turn, step], place))

    half(0)
    own_keep = pltpu.make_async_copy(
        kv_stage.at[zz, yy],
        app_out.at[:, pl.ds(pl.multiple_of(me * 256, 256), 256)],
        local_sem.at[2],
    )
    own_keep.start()
    for step in range(planes):
        holder = 2 * plane(step) + other
        wq_copy(holder, wq_near.at[step], near_place).wait_recv()
        spread_x(holder)
    for step in range(planes):
        pass_core(2 * plane(step) + yy)
    for step in range(planes):
        tok_copy(other, plane(step), tok_near.at[step], near_place).wait_recv()
    half(1)
    for step in range(1, planes):
        holder = 2 * plane(step) + yy
        wh_copy(holder, wh_far.at[step], near_place).wait_recv()
        begin(wh_copy(holder, wh_near.at[step], near_place))
        wo_copy(holder, wo_far.at[step], near_place).wait_recv()
        begin(wo_copy(holder, wo_near.at[step], near_place))
        wo_spread(holder)
    wo_spread(me)
    for step in range(planes):
        pass_core(2 * plane(step) + other)

    for step in range(planes):
        depth = plane(step)
        for side in range(2):
            wq_pass(1 - cc, 2 * depth + side).wait_recv()
        start = pl.multiple_of(depth * 256, 256)
        weight = wq[:, :, :, pl.ds(start, 256)].reshape(features, 256)
        for side in range(2):
            made = jnp.dot(
                tok[side].reshape(half_rows, features), weight, preferred_element_type=jnp.float32
            )
            cosine = cos_ref[:, side].reshape(half_rows, 128)
            sine = sin_ref[:, side].reshape(half_rows, 128)
            for part in range(2):
                piece = turned(made[:, 128 * part : 128 * part + 128], cosine, sine)
                q_out[2 * depth + part, :, side] = piece.reshape(planes, own_rows, 128)

    for step in range(planes):
        wh_copy(2 * plane(step) + other, wh_near.at[step], near_place).wait_recv()
    for pack in range(packs):
        wh_out[slab * pack : slab * pack + slab, :] = jnp.concatenate(
            [
                wh_all[holder].astype(jnp.float32)[:, head_cols * pack : head_cols * pack + head_cols]
                for holder in range(holders)
            ],
            axis=1,
        ).astype(jnp.bfloat16)
    for step in range(1, holders):
        kv_copy((me + step) % holders, yy, zz, kv_send.at[0, 0], near_place).wait_recv()
    own_keep.wait()
    for step in range(planes):
        wo_copy(2 * plane(step) + other, wo_near.at[step], near_place).wait_recv()
        for turn in range(1, req_pairs):
            wo_over(req_far(turn), 2 * plane(step) + yy, turn, core_place).wait_recv()
    for copy in started:
        copy.wait_send()


def project(pages, freqs, tokens, gain, w_query, w_keyval, w_out, w_head, holders, req_count):
    own_rows, features = tokens.shape
    planes = holders // 2
    deep = w_query.shape[0]
    vmem = pl.BlockSpec(memory_space=pltpu.VMEM)
    bf16 = jnp.bfloat16
    dma = pltpu.SemaphoreType.DMA
    pairs = req_count // 2
    return pl.pallas_call(
        project_kernel,
        out_shape=(
            jax.ShapeDtypeStruct((holders, planes, 2, own_rows, 128), bf16),
            jax.ShapeDtypeStruct((own_rows, 2 * features), bf16),
            jax.ShapeDtypeStruct((pairs, deep, features), bf16),
            jax.ShapeDtypeStruct((deep, holders * w_head.shape[0]), bf16),
        ),
        in_specs=[pl.BlockSpec(memory_space=pltpu.SMEM)] + [vmem] * 7,
        out_specs=(vmem, vmem, vmem, vmem),
        scratch_shapes=[
            pltpu.VMEM((2, planes, own_rows, features), bf16),
            pltpu.VMEM((req_count, deep, w_keyval.shape[1]), bf16),
            pltpu.VMEM((pairs, 2, deep, features), bf16),
            pltpu.VMEM((planes, 2, own_rows, 256), bf16),
            pltpu.VMEM((holders, deep * w_head.shape[0] // 128, 128), bf16),
            pltpu.VMEM((planes, 2, own_rows, 128), jnp.float32),
            pltpu.VMEM((planes, 2, own_rows, 128), jnp.float32),
            dma((planes,)), dma((planes,)), dma((2, planes)),
            dma((pairs,)), dma((pairs,)), dma((req_count,)),
            dma((planes,)), dma((planes,)), dma((holders,)),
            dma((pairs, holders)), dma((pairs, holders)), dma((holders,)), dma((holders,)),
            dma((planes,)), dma((planes,)), dma((holders,)),
            dma((pairs, holders)), dma((pairs, holders)),
            dma((planes,)), dma((planes,)), dma((holders,)),
            dma((2, planes)), dma((holders,)), dma((3,)),
        ],
        compiler_params=pltpu.CompilerParams(
            collective_id=0, has_side_effects=True, vmem_limit_bytes=56 * 1024 * 1024
        ),
        cost_estimate=pl.CostEstimate(
            flops=2 * holders * own_rows * features * (features + w_keyval.shape[1]),
            bytes_accessed=features * features * 6,
            transcendentals=0,
        ),
    )(pages, freqs, tokens, gain.reshape(1, features), w_query, w_keyval, w_out, w_head)


def expander(features, head_width):
    head = lax.broadcasted_iota(jnp.int32, (128, features), 0)
    column = lax.broadcasted_iota(jnp.int32, (128, features), 1)
    return jnp.where(column // head_width == head, 1.0, 0.0).astype(jnp.bfloat16)


def join_parts(parts, spread, features, head_count):
    levels = []
    for part in parts:
        coded = part[:, features:].astype(jnp.float32)
        levels.append(
            coded
            + pltpu.roll(coded, 128 - head_count, 1)
            + pltpu.roll(coded, 128 - 2 * head_count, 1)
        )
    top = functools.reduce(jnp.maximum, levels)
    shares = [jnp.exp(level - top) for level in levels]
    total = functools.reduce(jnp.add, shares)
    joined = None
    for part, share in zip(parts, shares):
        share = share / total
        high = share.astype(jnp.bfloat16)
        low = (share - high.astype(jnp.float32)).astype(jnp.bfloat16)
        wide = jnp.dot(high, spread, preferred_element_type=jnp.float32) + jnp.dot(
            low, spread, preferred_element_type=jnp.float32
        )
        term = part[:, :features].astype(jnp.float32) * wide
        joined = term if joined is None else joined + term
    return joined, top + jnp.log(total)


def close_kernel(
    parts_ref, tokens_ref, gain_ref, wo_ref, wh_ref,
    hidden_ref, logits_ref, stats_out,
    near_buf, send_buf, far_buf, stat_buf, spread_ref, wo_all, wh_all,
    wo_near, wo_recv, wox_send, wox_recv, wop_send, wop_recv, keep_sem, wh_far, wh_near, wh_recv,
    near_send, near_recv, far_send, far_recv, stat_send, stat_recv,
    *, head_count, request_count,
):
    planes, _, own_rows, coded = parts_ref.shape
    holders = 2 * planes
    features = coded - 128
    me = lax.axis_index("pg")
    zz, yy = me // 2, me % 2
    other = 1 - yy
    near_place = {"pg": 2 * zz + other}
    req_pairs = wo_all.shape[0]
    block = 128
    planes_out = features // (2 * block)
    mine = lax.axis_index("req")
    xx, cc = mine // 2, mine % 2
    core_place = {"req": 2 * xx + 1 - cc}

    def req_far(step):
        return (xx + step) % req_pairs

    arrived = greet(
        [{"pg": (me + step) % holders} for step in range(1, holders)]
        + [{"req": 2 * req_far(step) + cc} for step in range(1, req_pairs)]
        + [core_place]
    )
    def columns(depth, side):
        return pl.ds(pl.multiple_of((2 * depth + side) * block, block), block)

    keeps = [pltpu.make_async_copy(wo_ref.at[xx], wo_all.at[xx, cc], keep_sem.at[0, 0])]
    for step in range(1, req_pairs):
        far = req_far(step)
        for depth in range(planes_out):
            keeps.append(
                pltpu.make_async_copy(
                    wo_ref.at[far, :, columns(depth, yy)],
                    wo_all.at[far, cc, :, columns(depth, yy)],
                    keep_sem.at[step, depth],
                )
            )
    for keep in keeps:
        keep.start()
    wh_all[xx, cc] = wh_ref[...]
    spread_ref[...] = expander(features, features // head_count)
    arrived()
    order = list(range(1, planes)) + [0]
    started = []

    def near_copy(depth, step):
        return remote(
            parts_ref.at[depth, other], near_buf.at[depth], near_send.at[step],
            near_recv.at[depth], near_place,
        )

    for step in order:
        copy = near_copy((zz + step) % planes, step)
        copy.start()
        started.append(copy)

    def wo_copy(depth, side, send_sem, place):
        part = wo_all.at[depth, side]
        return remote(part, part, send_sem, wo_recv.at[depth, side], place)

    def wo_over(depth, step, column, place):
        part = wo_all.at[depth, cc, :, columns(column, other)]
        return remote(part, part, wox_send.at[step, column], wox_recv.at[depth, column], place)

    def wo_pass(depth, side, late, step, column):
        part = wo_all.at[depth, side, :, columns(column, other if late else yy)]
        return remote(
            part, part, wop_send.at[late, step, column], wop_recv.at[late, depth, column], core_place
        )

    def wh_copy(depth, side, send_sem, place):
        part = wh_all.at[depth, side]
        return remote(part, part, send_sem, wh_recv.at[depth, side], place)

    for step in range(1, req_pairs):
        place = {"req": 2 * req_far(step) + cc}
        started += [wo_over(xx, step, column, place) for column in range(planes_out)]
        started.append(wh_copy(xx, cc, wh_far.at[step], place))
    for keep in keeps:
        keep.wait()
    for copy in started[planes:]:
        copy.start()
    first = len(started)
    started += [
        wo_copy(xx, cc, wo_near.at[0], core_place), wh_copy(xx, cc, wh_near.at[0], core_place)
    ]
    for step in range(1, req_pairs):
        started += [wo_pass(req_far(step), cc, 0, step, column) for column in range(planes_out)]
    passes = started[first:]

    def pass_on():
        for step in range(1, req_pairs):
            depth = req_far(step)
            copies = [wh_copy(depth, cc, wh_near.at[step], core_place)]
            for column in range(planes_out):
                wo_over(depth, step, column, core_place).wait_recv()
                copies.append(wo_pass(depth, cc, 1, step, column))
            wh_copy(depth, cc, wh_far.at[step], core_place).wait_recv()
            for copy in copies:
                copy.start()
                started.append(copy)

    lane = lax.broadcasted_iota(jnp.int32, (own_rows, 128), 1)
    for step in order:
        depth = (zz + step) % planes
        if step == 0:
            pass_on()
        near_copy(depth, step).wait_recv()
        joined, level = join_parts(
            [parts_ref[depth, yy], near_buf[depth]], spread_ref[...], features, head_count
        )
        level = jnp.where(lane < head_count, level, 0.0)
        high = level.astype(jnp.bfloat16).astype(jnp.float32)
        middle = (level - high).astype(jnp.bfloat16).astype(jnp.float32)
        low = level - high - middle
        code = high + pltpu.roll(middle, head_count, 1) + pltpu.roll(low, 2 * head_count, 1)
        if step == 0:
            far_buf[zz, :, :features] = joined.astype(jnp.bfloat16)
            far_buf[zz, :, features:] = code.astype(jnp.bfloat16)
        else:
            send_buf[step, :, :features] = joined.astype(jnp.bfloat16)
            send_buf[step, :, features:] = code.astype(jnp.bfloat16)
            copy = remote(
                send_buf.at[step], far_buf.at[zz], far_send.at[step], far_recv.at[zz],
                {"pg": 2 * depth + yy},
            )
            copy.start()
            started.append(copy)
            if step == 1:
                for copy in passes:
                    copy.start()
    for step in range(1, planes):
        depth = (zz + step) % planes
        remote(
            send_buf.at[step], far_buf.at[depth], far_send.at[step], far_recv.at[depth], near_place
        ).wait_recv()
    joined, _ = join_parts(
        [far_buf[depth] for depth in range(planes)], spread_ref[...], features, head_count
    )
    attention = joined.astype(jnp.bfloat16)
    for step in range(req_pairs):
        if step == 0:
            wo_copy(xx, 1 - cc, wo_near.at[0], core_place).wait_recv()
        else:
            for late in range(2):
                for column in range(planes_out):
                    wo_pass(req_far(step), 1 - cc, late, step, column).wait_recv()
        wh_copy(req_far(step), 1 - cc, wh_near.at[step], core_place).wait_recv()
    out_weight = wo_all[...].reshape(features, features)
    head_weight = wh_all[...].reshape(features, wh_ref.shape[1])
    hidden = (
        tokens_ref[...].astype(jnp.float32)
        + jnp.dot(attention, out_weight, preferred_element_type=jnp.float32)
    ).astype(jnp.bfloat16)
    hidden_ref[...] = hidden
    wide = hidden.astype(jnp.float32)
    squares = wide * wide
    power = jnp.mean(squares, axis=-1, keepdims=True)
    head_in = (wide * lax.rsqrt(power + EPSILON) * gain_ref[...]).astype(jnp.bfloat16)
    logits = jnp.dot(head_in, head_weight, preferred_element_type=jnp.float32)
    logits_ref[...] = logits.astype(jnp.bfloat16)
    energy = jnp.sum(jnp.sum(squares, axis=1, keepdims=True), axis=0, keepdims=True)
    peak = jnp.max(jnp.max(logits, axis=1, keepdims=True), axis=0, keepdims=True)
    is_first = lax.broadcasted_iota(jnp.int32, (8, 128), 0) == 0
    stat_buf[me] = jnp.where(
        is_first, jnp.broadcast_to(energy, (8, 128)), jnp.broadcast_to(peak, (8, 128))
    )
    for step in range(1, holders):
        copy = remote(
            stat_buf.at[me], stat_buf.at[me], stat_send.at[step], stat_recv.at[me],
            {"pg": (me + step) % holders},
        )
        copy.start()
        started.append(copy)
    for step in range(1, holders):
        source = (me + step) % holders
        remote(
            stat_buf.at[source], stat_buf.at[source], stat_send.at[step], stat_recv.at[source],
            near_place,
        ).wait_recv()
    every = holders // request_count
    for request in range(request_count):
        mine = [stat_buf[every * request + block] for block in range(every)]
        total = functools.reduce(jnp.add, mine)
        top = functools.reduce(jnp.maximum, mine)
        stats_out[request] = jnp.where(is_first, jnp.sqrt(total), top)
    for copy in started:
        copy.wait_send()


def close(parts, tokens, gain, wo, wh, head_count, request_count, holders):
    own_rows, features = tokens.shape
    planes = holders // 2
    coded = features + 128
    pairs = wo.shape[0]
    planes_out = features // 256
    vmem = pl.BlockSpec(memory_space=pltpu.VMEM)
    bf16 = jnp.bfloat16
    dma = pltpu.SemaphoreType.DMA
    return pl.pallas_call(
        functools.partial(close_kernel, head_count=head_count, request_count=request_count),
        out_shape=(
            jax.ShapeDtypeStruct((own_rows, features), bf16),
            jax.ShapeDtypeStruct((own_rows, wh.shape[1]), bf16),
            jax.ShapeDtypeStruct((request_count, 8, 128), jnp.float32),
        ),
        in_specs=[vmem] * 5,
        out_specs=(vmem, vmem, vmem),
        scratch_shapes=[
            pltpu.VMEM((planes, own_rows, coded), bf16),
            pltpu.VMEM((planes, own_rows, coded), bf16),
            pltpu.VMEM((planes, own_rows, coded), bf16),
            pltpu.VMEM((holders, 8, 128), jnp.float32),
            pltpu.VMEM((128, features), bf16),
            pltpu.VMEM((pairs, 2) + wo.shape[1:], bf16),
            pltpu.VMEM((pairs, 2) + wh.shape, bf16),
            dma((pairs,)), dma((pairs, 2)), dma((pairs, planes_out)), dma((pairs, planes_out)),
            dma((2, pairs, planes_out)), dma((2, pairs, planes_out)), dma((pairs, planes_out)),
            dma((pairs,)), dma((pairs,)), dma((pairs, 2)),
            dma((planes,)), dma((planes,)), dma((planes,)), dma((planes,)),
            dma((holders,)), dma((holders,)),
        ],
        compiler_params=pltpu.CompilerParams(
            collective_id=1, has_side_effects=True, vmem_limit_bytes=56 * 1024 * 1024
        ),
        cost_estimate=pl.CostEstimate(
            flops=2 * own_rows * features * features,
            bytes_accessed=features * features * 4,
            transcendentals=0,
        ),
    )(parts.reshape(planes, 2, own_rows, coded), tokens, gain.reshape(1, features), wo, wh)

def project_plain(tokens, cache_pages, attn_gain, w_query, w_keyval, w_out, w_head, group_rows, head_count):
    own_rows, features = tokens.shape
    request_count = cache_pages.shape[0]
    span_rows = group_rows // request_count
    head_width = features // head_count
    first_row = lax.axis_index("pg") * own_rows
    normed = rms_norm(tokens, attn_gain)
    query_full, keyval_full = (
        lax.all_gather(w_query, "req", axis=0, tiled=True),
        lax.all_gather(w_keyval, "req", axis=0, tiled=True),
    )
    own_index = first_row + jnp.arange(own_rows, dtype=jnp.int32)
    own_positions = (
        lookup_small(cache_pages, own_index // span_rows, request_count) * PAGE
        + own_index % span_rows
    )
    own_cos, own_sin = rope_angles(own_positions, head_width // 2)
    query_cols = query_full.shape[1]
    joined = jnp.concatenate([query_full, keyval_full], axis=1)
    projected = jnp.dot(
        normed, lax.all_gather(joined, "pg", axis=1, tiled=True), preferred_element_type=jnp.float32
    )
    projected = projected.reshape(own_rows, -1, joined.shape[1])
    query_raw = projected[:, :, :query_cols].reshape(own_rows, features).astype(jnp.bfloat16)
    keyval_raw = projected[:, :, query_cols:].reshape(own_rows, 2 * features).astype(jnp.bfloat16)
    own_queries = rotate(query_raw, own_cos, own_sin, head_count)
    new_keys = rotate(keyval_raw[:, :features], own_cos, own_sin, head_count)
    new_values = keyval_raw[:, features:]
    appended = jnp.concatenate([new_keys, new_values], axis=1)
    queries = lax.all_gather(own_queries, "pg", axis=0, tiled=True)
    queries = queries.reshape(group_rows, features // 128, 128).transpose(1, 0, 2)
    out_slices = lax.all_gather(lax.all_gather(w_out, "pg", axis=1, tiled=True), "req")
    out_slices = out_slices.reshape(-1, 2, w_out.shape[0], features)
    return (
        queries,
        appended,
        lax.dynamic_index_in_dim(out_slices, lax.axis_index("req") % 2, 1, keepdims=False),
        lax.all_gather(w_head, "pg", axis=1, tiled=True),
    )


def per_device(
    tokens,
    variate_ids,
    cache_pages,
    page_table,
    kv_cache,
    cache_variates,
    attn_gain,
    w_query,
    w_keyval,
    w_out,
    variate_bias,
    head_gain,
    w_head,
):
    own_rows, features = tokens.shape
    request_count = cache_pages.shape[0]
    group_rows = variate_ids.shape[0]
    head_count = variate_bias.shape[1]
    holders = group_rows // own_rows
    half_width = features // head_count // 2
    req_count = features // w_query.shape[0]
    if w_query.shape[1] == 128 and w_keyval.shape[1] == 256:
        steps = np.arange(half_width, dtype=np.float32) / half_width
        freqs = np.exp(np.float32(-math.log(10000.0)) * steps).reshape(half_width, 1)
        queries, appended, out_rows, head_rows = project(
            cache_pages, freqs, tokens, attn_gain, w_query, w_keyval, w_out, w_head.T, holders, req_count
        )
        queries = queries.reshape(holders, group_rows, 128)
    else:
        queries, appended, out_rows, head_rows = project_plain(
            tokens, cache_pages, attn_gain, w_query, w_keyval, w_out, w_head, group_rows, head_count
        )
    partial_out, appended = attend(
        cache_pages, page_table, variate_bias, queries, variate_ids, appended, cache_variates, kv_cache
    )
    hidden, logits, stats = close(
        partial_out, tokens, head_gain, out_rows, head_rows, head_count, request_count, holders
    )
    hidden, logits, norms, peaks = hand_over(hidden, logits, stats)
    return (hidden, appended, logits, norms, peaks)


def hand_over_kernel(hidden_ref, logits_ref, stats_ref, hidden_out, logits_out, norm_out, peak_out):
    hidden_out[...] = hidden_ref[...]
    logits_out[...] = logits_ref[...]
    for request in range(stats_ref.shape[0]):
        norm_out[request] = stats_ref[request, 0, 0]
        peak_out[request] = stats_ref[request, 1, 0]


def hand_over(hidden, logits, stats):
    vmem = pl.BlockSpec(memory_space=pltpu.VMEM)
    smem = pl.BlockSpec(memory_space=pltpu.SMEM)
    scalars = jax.ShapeDtypeStruct((stats.shape[0],), jnp.float32)
    return pl.pallas_call(
        hand_over_kernel,
        out_shape=(
            jax.ShapeDtypeStruct(hidden.shape, hidden.dtype),
            jax.ShapeDtypeStruct(logits.shape, logits.dtype),
            scalars,
            scalars,
        ),
        in_specs=[vmem, vmem, smem],
        out_specs=(vmem, vmem, smem, smem),
    )(hidden, logits, stats)


def solution(mesh):
    placed = (
        P(("req", "pg"), None),
        P("req"),
        P("req"),
        P("req", None),
        P(("req", "pg"), None, None),
        P(("req", "pg"), None),
        P(),
        P("req", "pg"),
        P("req", "pg"),
        P("req", "pg"),
        P(),
        P(),
        P("req", "pg"),
    )
    return jax.shard_map(
        per_device,
        mesh=mesh,
        in_specs=placed,
        out_specs=(
            P(("req", "pg"), None),
            P(("req", "pg"), None),
            P(("req", "pg"), None),
            P("req"),
            P("req"),
        ),
        check_vma=False,
    )
```
